32 devices in a mesh: ctx: 8 (over z, y), tp: 2 (over x), dp: 2 (over core).
Axes of the slice: x: 2, y: 2, z: 4, core: 2. Of those that a mesh axis runs over, the one named last changes fastest.
Arguments:
- vis_qkv: bfloat16 [8192, 3, 1280], P(('dp', 'ctx'), None, 'tp'), parts along dimension 0, may hold values from -60 to 60
- vis_resid: bfloat16 [8192, 1280], P(('dp', 'ctx'), 'tp'), parts along dimension 0, may hold values from -1.796875 to 1.796875
- vis_out_w: bfloat16 [1280, 1280], P(None, 'tp'), may hold values from -0.15625 to 0.15625
- merge_gain: float32 [1280], P('tp'), may hold values from 0.5 to 1.5
- merge_bias: float32 [1280], P('tp'), may hold values from -3 to 3
- vis_kv_w: bfloat16 [4, 1280, 2048], P(None, 'tp'), may hold values from -0.078125 to 0.078125
- frame_host: int32 [16], P('dp'), parts along dimension 0, may hold values from 0 to 7, as said below
- vis_pos: int32 [16], P('dp'), parts along dimension 0, may hold values from 0 to 1920, as said below
- doc_ids: int32 [4096], P('dp'), parts along dimension 0, may hold values from 0 to 3, as said below
- text_kv: bfloat16 [4096, 8, 2, 128], P(('dp', 'ctx'), 'tp'), parts along dimension 0, may hold values from -4 to 4
- queries: bfloat16 [4096, 4096], P(('dp', 'ctx'), 'tp'), parts along dimension 0, may hold values from -50 to 50
Outputs:
- attended: bfloat16 [4096, 4096], P(('dp', 'ctx'), 'tp'), parts along dimension 0
The draws below stay inside these ranges and needn't reach their ends.
There are 2 independent parts, one for each index of `dp`. The reference program is written for one: setup_inputs(seed, part) draws one part's arguments, and reference() takes and returns one part's arrays. A program takes and returns all parts, laid end to end along the dimension named above; an argument that names none is the same for every part. Nothing has to cross between parts.
Inputs may be any that keep to these rules, and one draw needn't show every extreme that they name: `vis_pos`: frame starts are multiples of 128 and increase with the frame; some block of 256 positions holds only frames. `frame_host`: each frame is encoded on the ctx device that holds its positions or on the device 8 / 2 indices away along ctx; every device encodes exactly 1 frame. `doc_ids`: never falls along the sequence.
All inputs are finite; a program needn't handle non-finite values.
Results may differ from the reference program's by a relative error of at most 0.0085.
Values may be sent and summed in bfloat16 or wider, within the bound.
No kernel may reach another device: no remote copies, remote signals or barrier semaphores. Data moves between devices by JAX's collectives and lax.ppermute only.
A program may use at most 64 MiB of HBM per device.

```python
import math
import jax
import jax.numpy as jnp
from jax import lax

VD = 1280
VH = 16
HD = 128
H = 32
KVH = 8
FT = 128
T_DEV = 256
FP = 512
FRAMES_DEV = 1
SEQ = 2048
FRAMES = 8
PATCHES = 4096
VTOK = 1024


def layout_tables(key):
    peers = SEQ // T_DEV
    half_count = peers // 2
    slot_count = T_DEV // FT
    swing = FRAMES_DEV - jax.random.randint(jax.random.fold_in(key, 11), (half_count,), 0, (FRAMES_DEV + 1) // 2 + 1)
    chosen_pair = jax.random.randint(jax.random.fold_in(key, 12), (), 0, half_count)
    swing = jnp.where(jnp.arange(half_count) == chosen_pair, FRAMES_DEV, swing)
    sign = 2 * jax.random.randint(jax.random.fold_in(key, 14), (half_count,), 0, 2) - 1
    lower_count = FRAMES_DEV + sign * swing
    counts = jnp.concatenate([lower_count, 2 * FRAMES_DEV - lower_count])
    noise = jax.random.randint(jax.random.fold_in(key, 13), (peers, slot_count), 0, 1 << 30)
    slot_rank = jnp.argsort(jnp.argsort(noise, axis=1, stable=True), axis=1, stable=True)
    chosen = slot_rank < counts[:, None]
    within = jnp.cumsum(chosen.astype(jnp.int32), axis=1) - 1
    device_ids = jnp.arange(peers)
    pair_of = device_ids % half_count
    pair_index = jnp.where(device_ids[:, None] < half_count, within, lower_count[pair_of][:, None] + within)
    pair_noise = jax.random.randint(jax.random.fold_in(key, 15), (half_count, 2 * FRAMES_DEV), 0, 1 << 30)
    pair_rank = jnp.argsort(jnp.argsort(pair_noise, axis=1, stable=True), axis=1, stable=True)
    safe_index = jnp.clip(pair_index, 0, 2 * FRAMES_DEV - 1)
    rank_here = jnp.take_along_axis(pair_rank[pair_of], safe_index, axis=1)
    host = jnp.where(rank_here < FRAMES_DEV, pair_of[:, None], pair_of[:, None] + half_count)
    candidates = (device_ids[:, None] * T_DEV + jnp.arange(slot_count)[None, :] * FT).reshape(peers * slot_count)
    flat_chosen = chosen.reshape(peers * slot_count)
    picked = jnp.argsort(jnp.where(flat_chosen, 0, 1), stable=True)[:FRAMES]
    return (candidates[picked].astype(jnp.int32), host.reshape(peers * slot_count)[picked].astype(jnp.int32))


def draw_vis_pos(key, part):
    return layout_tables(key)[0]


def draw_frame_host(key, part):
    return layout_tables(key)[1]


def doc_table(key):
    bounds = jax.random.randint(jax.random.fold_in(key, 31), (3,), 1, SEQ)
    position = jnp.arange(SEQ, dtype=jnp.int32)
    return jnp.sum(jnp.where(position[:, None] >= bounds[None, :], 1, 0), axis=1).astype(jnp.int32)


def draw_doc_ids(key, part):
    return doc_table(key)


def draw_vis_qkv(key, part):
    array_shape = (PATCHES, 3, VD)
    query_factor = jnp.where(jnp.arange(3)[None, :, None] == 0, 2.5, 1.0)
    drawn = jnp.clip(jax.random.normal(key, array_shape, jnp.float32), -4.0, 4.0) * query_factor
    return drawn.astype(jnp.bfloat16)


def language_fields(key):
    group = H // KVH
    kv_key = jax.random.fold_in(key, 21)
    query_key = jax.random.fold_in(key, 22)
    kv_all = jnp.clip(jax.random.normal(kv_key, (SEQ, KVH, 2, HD), jnp.float32), -4.0, 4.0)
    query_all = jnp.clip(2.0 * jax.random.normal(query_key, (SEQ, KVH, group, HD), jnp.float32), -8.0, 8.0)
    return (kv_all.astype(jnp.bfloat16), query_all.reshape(SEQ, H * HD).astype(jnp.bfloat16))


def draw_text_kv(key, part):
    return language_fields(key)[0]


def draw_queries(key, part):
    return language_fields(key)[1]


def block_scale(rng, dims, cuts, smallest, top_value):
    def one(dim, shards_of):
        heights = jax.random.uniform(jax.random.fold_in(jax.random.fold_in(rng, 6), dim), (shards_of,), jnp.float32, smallest / len(cuts), top_value / len(cuts))
        return jnp.repeat(jnp.exp(heights), dims[dim] // shards_of).reshape((-1,) + (1,) * (len(dims) - dim - 1))

    loudness = one(*cuts[0])
    for cut in cuts[1:]:
        loudness = loudness * one(*cut)
    return loudness


def scatter_about(rng, extent, scale, most, split=(), held_as=jnp.bfloat16):
    values = jax.random.normal(rng, extent, jnp.float32) * scale
    if len(split) > 0:
        values = block_scale(rng, extent, split, -0.22, 0.18) * values
    return jnp.clip(values, min=-most, max=most).astype(held_as)


def setup_inputs(seed: int = 0, part: int = 0) -> dict:
    seeds = jax.random.split(jax.random.key(seed), 12)
    part_splits = jax.random.split(jax.random.fold_in(seeds[11], part), 12)
    return {
        "vis_qkv": draw_vis_qkv(jax.random.fold_in(jax.random.fold_in(seeds[11], part), 71), part),
        "vis_resid": scatter_about(part_splits[1], (PATCHES, VD), 0.3, 1.796875, ((0, 8), (1, 2))),
        "vis_out_w": scatter_about(seeds[2], (VD, VD), VD ** -0.5, 0.15625, ((1, 2),)),
        "merge_gain": jnp.clip(0.5 + 1.0 * jax.random.uniform(seeds[3], (VD,), jnp.float32) ** block_scale(seeds[3], (VD,), ((0, 2),), -0.2, 0.2), 0.5, 1.5),
        "merge_bias": scatter_about(seeds[4], (VD,), 0.5, 3.0, ((0, 2),), jnp.float32),
        "vis_kv_w": scatter_about(seeds[5], (4, VD, KVH * 2 * HD), (4 * VD) ** -0.5, 0.078125, ((1, 2),)),
        "frame_host": draw_frame_host(jax.random.fold_in(jax.random.fold_in(seeds[11], part), 71), part),
        "vis_pos": draw_vis_pos(jax.random.fold_in(jax.random.fold_in(seeds[11], part), 71), part),
        "doc_ids": draw_doc_ids(jax.random.fold_in(jax.random.fold_in(seeds[11], part), 71), part),
        "text_kv": draw_text_kv(jax.random.fold_in(jax.random.fold_in(seeds[11], part), 71), part),
        "queries": draw_queries(jax.random.fold_in(jax.random.fold_in(seeds[11], part), 71), part),
    }


def frame_attention(frame_fields):
    head_dim = VD // VH
    fields = frame_fields.astype(jnp.float32)
    scores = jnp.einsum('qhd,khd->hqk', fields[:, 0], fields[:, 1]) / math.sqrt(head_dim)
    row_max = lax.optimization_barrier(jnp.max(scores, axis=2, keepdims=True))
    exponent = jnp.exp(scores - row_max)
    denominator = lax.optimization_barrier(jnp.sum(exponent, axis=2, keepdims=True))
    weights = lax.optimization_barrier(exponent.astype(jnp.bfloat16))
    mixed = jnp.einsum('hqk,khd->qhd', weights.astype(jnp.float32), fields[:, 2])
    return (mixed / jnp.transpose(denominator, (1, 0, 2))).astype(jnp.bfloat16)

def vision_part(vis_qkv, vis_resid, vis_out_w, merge_gain, merge_bias, vis_kv_w):
    head_dim = VD // VH
    framed = vis_qkv.reshape(FRAMES, FP, 3, VH, head_dim)
    context = lax.map(frame_attention, framed).reshape(PATCHES, VD)
    hidden = vis_resid.astype(jnp.float32) + jnp.dot(context, vis_out_w, preferred_element_type=jnp.float32)
    mean_value = lax.optimization_barrier(jnp.mean(hidden, axis=1, keepdims=True))
    variance = lax.optimization_barrier(jnp.mean(jnp.square(hidden - mean_value), axis=1, keepdims=True))
    normed = ((hidden - mean_value) * lax.rsqrt(variance + 1e-06) * merge_gain + merge_bias).astype(jnp.bfloat16)
    merged = normed.reshape(VTOK, 4 * VD)
    weight_flat = vis_kv_w.reshape(4 * VD, KVH * 2 * HD)
    return jnp.dot(merged, weight_flat, preferred_element_type=jnp.float32).astype(jnp.bfloat16)

def language_block(query_block, kv_prefix, allowed):

    def one_head(packed):
        query_head, key_head, value_head = packed
        scores = jnp.einsum('tgd,sd->tgs', query_head.astype(jnp.float32), key_head.astype(jnp.float32)) / math.sqrt(HD)
        scores = jnp.where(allowed[:, None, :], scores, -jnp.inf)
        row_max = lax.optimization_barrier(jnp.max(scores, axis=2, keepdims=True))
        exponent = jnp.exp(scores - row_max)
        denominator = lax.optimization_barrier(jnp.sum(exponent, axis=2, keepdims=True))
        weights = lax.optimization_barrier(exponent.astype(jnp.bfloat16))
        mixed = jnp.einsum('tgs,sd->tgd', weights.astype(jnp.float32), value_head.astype(jnp.float32))
        return (mixed / denominator).astype(jnp.bfloat16)
    heads_out = lax.map(one_head, (jnp.transpose(query_block, (1, 0, 2, 3)), jnp.transpose(kv_prefix[:, :, 0], (1, 0, 2)), jnp.transpose(kv_prefix[:, :, 1], (1, 0, 2))))
    return jnp.transpose(heads_out, (1, 0, 2, 3)).reshape(query_block.shape[0], H * HD)

def reference(vis_qkv, vis_resid, vis_out_w, merge_gain, merge_bias, vis_kv_w, frame_host, vis_pos, doc_ids, text_kv, queries):
    vision_kv = vision_part(vis_qkv, vis_resid, vis_out_w, merge_gain, merge_bias, vis_kv_w)
    frame_index = jnp.arange(FRAMES, dtype=jnp.int32)
    same_host = frame_host[:, None] == frame_host[None, :]
    earlier = frame_index[None, :] < frame_index[:, None]
    host_rank = lax.optimization_barrier(jnp.sum(jnp.where(same_host & earlier, 1, 0), axis=1)).astype(jnp.int32)
    layout_row = (frame_host * FRAMES_DEV + host_rank).astype(jnp.int32)
    by_frame = vision_kv.reshape(FRAMES, FT, KVH * 2 * HD)[layout_row]
    places = (vis_pos[:, None] + jnp.arange(FT, dtype=jnp.int32)[None, :]).reshape(VTOK).astype(jnp.int32)
    keys_values = text_kv.reshape(SEQ, KVH * 2 * HD).at[places].set(by_frame.reshape(VTOK, KVH * 2 * HD))
    keys_values = keys_values.reshape(SEQ, KVH, 2, HD)
    group = H // KVH
    query_all = queries.reshape(SEQ, KVH, group, HD)
    block_rows = math.gcd(SEQ, 512)
    position = jnp.arange(SEQ, dtype=jnp.int32)
    pieces = []
    for block_index in range(SEQ // block_rows):
        lower = block_index * block_rows
        upper = lower + block_rows
        allowed = (position[:upper][None, :] <= position[lower:upper][:, None]) & (doc_ids[:upper][None, :] == doc_ids[lower:upper][:, None])
        pieces.append(language_block(query_all[lower:upper], keys_values[:upper], allowed))
    return jnp.concatenate(pieces, axis=0)
```

```python
import functools
import math

import jax
import jax.numpy as jnp
from jax import lax
from jax.experimental import pallas as pl
from jax.experimental.pallas import tpu as pltpu
from jax.sharding import PartitionSpec as P

VD = 1280
VH = 16
HD = 128
H = 32
KVH = 8
FT = 128
FP = 4 * FT
GROUP = H // KVH
LANES = 128

MASKED = -1e30
FLOOR = -1e29
TINY = 1e-30
VMEM_LIMIT = 16 * 1024 * 1024
MERGE_VMEM = 52 * 1024 * 1024
LANGUAGE_VMEM = 52 * 1024 * 1024


def contract_last(a, b):
    return lax.dot_general(a, b, (((1,), (1,)), ((), ())), preferred_element_type=jnp.float32)


def shifted(block, axis, distance):
    count = lax.axis_size(axis)
    return lax.ppermute(block, axis, [(i, (i + distance) % count) for i in range(count)])


def to_next_row(block, rows):
    return lax.ppermute(
        block,
        "ctx",
        [(2 * row + side, 2 * ((row + 1) % rows) + side) for row in range(rows) for side in range(2)],
    )


def to_other_side(block, rows):
    return lax.ppermute(
        block, "ctx", [(2 * row + side, 2 * row + 1 - side) for row in range(rows) for side in range(2)]
    )


class Ring:
    def __init__(self, block, rows):
        self.rows = rows
        self.blocks = [block]
        self.start(block)

    def start(self, block):
        self.moving = to_next_row(block, self.rows) if len(self.blocks) < 2 * self.rows - 1 else None
        self.blocks.append(to_other_side(block, self.rows))

    def advance(self, beside):
        if self.moving is None:
            return beside
        held, self.blocks[-1], beside = lax.optimization_barrier(
            (self.moving, self.blocks[-1], beside)
        )
        self.blocks.append(held)
        self.start(held)
        return beside

    def all(self):
        while self.moving is not None:
            self.advance(())
        return self.blocks


def block_sources(device, rows):
    index = jnp.arange(2 * rows, dtype=jnp.int32)
    row = (device // 2 + rows - index // 2) % rows
    return 2 * row + (device % 2 + index) % 2


def vit_kernel(q_ref, k_ref, v_ref, after_ref, o_ref, *, heads, dim):
    width = q_ref.shape[2]
    to_exp = 1.0 / math.sqrt(dim)
    tiles = {}
    for g in range(heads):
        first, last = g * dim, (g + 1) * dim
        low = first // LANES * LANES
        high = min(width, -(-last // LANES) * LANES)
        lane = lax.broadcasted_iota(jnp.int32, (1, high - low), 1) + low
        inside = (lane >= first) & (lane < last)
        keep = jnp.where(inside, 1.0, 0.0).astype(jnp.bfloat16)
        rest = jnp.where(inside, 0.0, 1.0).astype(jnp.bfloat16)
        scores = contract_last(q_ref[0, :, low:high] * keep, k_ref[0, :, low:high])
        row_max = jnp.max(scores, axis=1, keepdims=True)
        weights = jnp.exp((scores - row_max) * to_exp).astype(jnp.bfloat16)
        mixed = jnp.dot(
            weights, v_ref[0, :, low:high] * keep + rest, preferred_element_type=jnp.float32
        )
        spare = 0 if low < first else last - low
        mixed = mixed / mixed[:, spare : spare + 1]
        for at in range(low, high, LANES):
            end = min(at + LANES, high)
            piece = mixed[:, at - low : end - low]
            if at in tiles:
                piece = jnp.where(inside[:, at - low : end - low], piece, tiles[at])
            tiles[at] = piece
    for at, piece in tiles.items():
        o_ref[:, at : at + piece.shape[1]] = piece.astype(o_ref.dtype)


def vit_attention(fields, after, part, part_count):
    _, patches, width = fields.shape
    frames = patches // FP
    rows = FP // part_count
    dim = VD // VH
    heads = width // dim
    return pl.pallas_call(
        functools.partial(vit_kernel, heads=heads, dim=dim),
        grid=(frames,),
        in_specs=[
            pl.BlockSpec((1, rows, width), lambda f: (0, f * part_count + part, 0)),
            pl.BlockSpec((1, FP, width), lambda f: (1, f, 0)),
            pl.BlockSpec((1, FP, width), lambda f: (2, f, 0)),
            pl.BlockSpec(memory_space=pl.ANY),
        ],
        out_specs=pl.BlockSpec((rows, width), lambda f: (f, 0)),
        out_shape=jax.ShapeDtypeStruct((frames * rows, width), jnp.bfloat16),
        compiler_params=pltpu.CompilerParams(vmem_limit_bytes=VMEM_LIMIT),
        cost_estimate=pl.CostEstimate(flops=1024, bytes_accessed=1024, transcendentals=0),
    )(fields, fields, fields, after)


def merge_kernel(block_ref, x_ref, w_ref, o_ref, held_ref, rows_ref, sems, *, step):
    tokens, columns = o_ref.shape
    patches = x_ref.shape[0]
    steps = columns // step

    def weights_in(n):
        source = w_ref.at[:, :, pl.ds(pl.multiple_of(block_ref[0] * columns + n * step, step), step)]
        return pltpu.make_async_copy(source, held_ref.at[n], sems.at[n])

    for n in range(steps):
        weights_in(n).start()
    token = lax.broadcasted_iota(jnp.int32, (tokens, patches), 0)
    patch = lax.broadcasted_iota(jnp.int32, (tokens, patches), 1)
    for j in range(4):
        pick = jnp.where(patch == 4 * token + j, 1.0, 0.0).astype(jnp.bfloat16)
        rows_ref[j] = jnp.dot(pick, x_ref[...], preferred_element_type=jnp.float32).astype(
            jnp.bfloat16
        )
    for n in range(steps):
        weights_in(n).wait()
        total = jnp.zeros((tokens, step), jnp.float32)
        for j in range(4):
            total = total + jnp.dot(
                rows_ref[j], held_ref[n, j], preferred_element_type=jnp.float32
            )
        o_ref[:, n * step : (n + 1) * step] = total.astype(o_ref.dtype)


def merged_columns(normed, weights, block, columns, dtype):
    patches, width = normed.shape
    tokens = patches // 4
    step = min(columns, 256)
    steps = columns // step
    return pl.pallas_call(
        functools.partial(merge_kernel, step=step),
        in_specs=[
            pl.BlockSpec(memory_space=pltpu.SMEM),
            pl.BlockSpec(memory_space=pltpu.VMEM),
            pl.BlockSpec(memory_space=pl.ANY),
        ],
        out_specs=pl.BlockSpec(memory_space=pltpu.VMEM),
        out_shape=jax.ShapeDtypeStruct((tokens, columns), dtype),
        scratch_shapes=[
            pltpu.VMEM((steps, 4, width, step), jnp.bfloat16),
            pltpu.VMEM((4, tokens, width), jnp.bfloat16),
            pltpu.SemaphoreType.DMA((steps,)),
        ],
        compiler_params=pltpu.CompilerParams(vmem_limit_bytes=MERGE_VMEM),
        cost_estimate=pl.CostEstimate(
            flops=2 * tokens * 4 * width * columns,
            bytes_accessed=4 * width * columns * 2 + patches * width * 2,
            transcendentals=0,
        ),
    )(jnp.reshape(block, (1,)), normed, weights)


def attend_kernel(bounds_ref, rank_ref, slot_pos_ref, low_ref, q_ref, *rest, blocks, final):
    block_refs, rest = rest[:blocks], rest[blocks:]
    kv_ref, query_ref, bias_ref, score_ref, max_ref, acc_ref = rest[-6:]
    rows = low_ref.shape[0]
    scale = 1.0 / math.sqrt(HD)
    first_pair, full_first, full_last, last_pair, first_pos = (bounds_ref[i] for i in range(5))
    lane = lax.broadcasted_iota(jnp.int32, (rows, FT), 1)

    for i, block_ref in enumerate(block_refs):
        kv_ref[pl.ds(pl.multiple_of(rank_ref[i] * FT, FT), FT)] = block_ref[...]
    for g in range(GROUP):
        query_ref[g * rows : (g + 1) * rows] = q_ref[:, g * HD : (g + 1) * HD]

    def mask(pair):
        query_pos = first_pos + lax.broadcasted_iota(jnp.int32, (rows, FT), 0)
        for half in range(2):
            key_pos = slot_pos_ref[2 * pair + half] + lane
            allowed = (key_pos <= query_pos) & (key_pos >= low_ref[...])
            bias_ref[pair, :, half * FT : (half + 1) * FT] = jnp.where(allowed, 0.0, MASKED)

    @pl.when(pl.program_id(0) == 0)
    def _():
        pl.loop(first_pair, full_first)(mask)
        pl.loop(full_last, last_pair)(mask)

    max_ref[...] = jnp.full_like(max_ref, FLOOR)

    def score(pair, masked):
        keys = kv_ref[pl.ds(pl.multiple_of(pair * 2 * FT, 2 * FT), 2 * FT), :HD]
        scores = contract_last(query_ref[...], keys) * scale
        if masked:
            scores = scores.reshape(GROUP, rows, 2 * FT) + bias_ref[pair][None]
            scores = scores.reshape(GROUP * rows, 2 * FT)
        score_ref[pair] = scores
        max_ref[...] = jnp.maximum(max_ref[...], jnp.maximum(scores[:, :FT], scores[:, FT:]))

    pl.loop(first_pair, full_first)(functools.partial(score, masked=True))
    pl.loop(full_first, full_last)(functools.partial(score, masked=False))
    pl.loop(full_last, last_pair)(functools.partial(score, masked=True))

    row_max = jnp.max(max_ref[...], axis=1, keepdims=True)
    if final:
        acc_in_ref, log_in_ref, out_ref = rest[:3]
        logs = jnp.concatenate([log_in_ref[0, :, g : g + 1] for g in range(GROUP)], axis=0)
        row_max = jnp.maximum(row_max, logs)
        weight = jnp.broadcast_to(jnp.exp(logs - row_max), (GROUP * rows, HD))
        for g in range(GROUP):
            here = slice(g * rows, (g + 1) * rows)
            acc_ref[here, :HD] = acc_in_ref[:, g * HD : (g + 1) * HD] * weight[here]
        acc_ref[:, HD:] = weight
    else:
        acc_out_ref, log_out_ref = rest[:2]
        acc_ref[...] = jnp.zeros_like(acc_ref)
    max_ref[...] = jnp.broadcast_to(row_max, max_ref.shape)

    @pl.loop(first_pair, last_pair)
    def _(pair):
        values = kv_ref[pl.ds(pl.multiple_of(pair * 2 * FT, 2 * FT), 2 * FT), HD:]
        values = jnp.concatenate([values, jnp.ones_like(values)], axis=1)
        weights = [
            jnp.exp(score_ref[pair, :, half * FT : (half + 1) * FT] - max_ref[...])
            for half in range(2)
        ]
        weights = jnp.concatenate([each.astype(jnp.bfloat16) for each in weights], axis=1)
        acc_ref[...] += jnp.dot(weights, values, preferred_element_type=jnp.float32)

    if final:
        mixed = acc_ref[:, :HD] / acc_ref[:, HD:]
        for g in range(GROUP):
            out_ref[:, g * HD : (g + 1) * HD] = mixed[g * rows : (g + 1) * rows].astype(
                out_ref.dtype
            )
    else:
        total = jnp.maximum(acc_ref[:, HD:], TINY)
        mixed = acc_ref[:, :HD] / total
        logs = max_ref[...] + jnp.log(total)
        packed = jnp.zeros((rows, FT), jnp.float32)
        for g in range(GROUP):
            here = slice(g * rows, (g + 1) * rows)
            acc_out_ref[:, g * HD : (g + 1) * HD] = mixed[here]
            packed = jnp.where(lane == g, logs[here], packed)
        log_out_ref[0] = packed


def attend(queries, blocks, bounds, rank, slot_pos, low, state=None, head_range=None):
    rows = queries.shape[0]
    columns = blocks[0].shape[1]
    slots = len(blocks)
    pairs = slots // 2
    final = head_range is None
    start, stop = (0, columns // (2 * HD)) if final else head_range
    heads = stop - start
    wide = GROUP * HD
    tall = GROUP * rows
    acc_spec = pl.BlockSpec((rows, wide), lambda h, *_: (0, h))
    log_spec = pl.BlockSpec((1, rows, FT), lambda h, *_: (h, 0, 0))
    in_specs = [
        pl.BlockSpec((rows, FT), lambda h, *_: (0, 0)),
        pl.BlockSpec((rows, wide), lambda h, *_: (0, start + h)),
    ] + [pl.BlockSpec((FT, 2 * HD), lambda h, *_: (0, start + h))] * slots
    if final:
        in_specs += [acc_spec, log_spec]
        out_specs = acc_spec
        out_shape = jax.ShapeDtypeStruct((rows, heads * wide), jnp.bfloat16)
    else:
        out_specs = [acc_spec, log_spec]
        out_shape = [
            jax.ShapeDtypeStruct((rows, heads * wide), jnp.float32),
            jax.ShapeDtypeStruct((heads, rows, FT), jnp.float32),
        ]
    grid_spec = pltpu.PrefetchScalarGridSpec(
        num_scalar_prefetch=3,
        grid=(heads,),
        in_specs=in_specs,
        out_specs=out_specs,
        scratch_shapes=[
            pltpu.VMEM((slots * FT, 2 * HD), jnp.bfloat16),
            pltpu.VMEM((tall, HD), jnp.bfloat16),
            pltpu.VMEM((pairs, rows, 2 * FT), jnp.float32),
            pltpu.VMEM((pairs, tall, 2 * FT), jnp.float32),
            pltpu.VMEM((tall, FT), jnp.float32),
            pltpu.VMEM((tall, 2 * HD), jnp.float32),
        ],
    )
    cells = heads * tall * slots * FT
    return pl.pallas_call(
        functools.partial(attend_kernel, blocks=slots, final=final),
        grid_spec=grid_spec,
        out_shape=out_shape,
        compiler_params=pltpu.CompilerParams(vmem_limit_bytes=LANGUAGE_VMEM),
        cost_estimate=pl.CostEstimate(
            flops=6 * cells * HD,
            bytes_accessed=2 * slots * FT * columns + 8 * heads * tall * FT,
            transcendentals=cells,
        ),
    )(bounds, rank, slot_pos, low, queries, *blocks, *(state or ()))


def pair_bounds(slot_pos, first_pos, last_pos, lowest, highest):
    first, second = slot_pos[0::2], slot_pos[1::2] + (FT - 1)
    begin = jnp.sum((second < lowest).astype(jnp.int32))
    end = jnp.maximum(begin, jnp.sum((first <= last_pos).astype(jnp.int32)))
    full_begin = jnp.clip(jnp.sum((first < highest).astype(jnp.int32)), begin, end)
    full_end = jnp.clip(jnp.sum((second <= first_pos).astype(jnp.int32)), full_begin, end)
    return jnp.stack([begin, full_begin, full_end, end, first_pos]).astype(jnp.int32)


def shards(
    vis_qkv,
    vis_resid,
    vis_out_w,
    merge_gain,
    merge_bias,
    vis_kv_w,
    frame_host,
    vis_pos,
    doc_ids,
    text_kv,
    queries,
):
    device = lax.axis_index("ctx")
    tp_index = lax.axis_index("tp")
    tp_size = lax.axis_size("tp")
    per_device = queries.shape[0]
    patches = vis_qkv.shape[0]
    width = vis_qkv.shape[2]
    frames_dev = patches // FP
    local_kv = vis_kv_w.shape[2] // tp_size
    positions = doc_ids.shape[0]
    frames = vis_pos.shape[0]

    peers = lax.axis_size("ctx")
    rows = peers // 2
    first_pos = device * per_device

    fields = jnp.transpose(vis_qkv, (1, 0, 2))
    part_count = 2 if frames_dev == 1 else 1
    part_rows = patches // part_count
    text_low = text_kv[:FT].reshape(FT, local_kv)
    text_high = text_kv[FT:].reshape(FT, local_kv)
    handed = shifted(text_high, "ctx", peers // 2)
    contexts = [vit_attention(fields, text_high, part, part_count) for part in range(part_count)]
    first_frame = jnp.any(vis_pos == first_pos)
    second_frame = jnp.any(vis_pos == first_pos + FT)
    arrived = [
        [shifted(context, "tp", distance) for distance in range(1, tp_size)]
        for context in contexts
    ]

    def out_rows(distance):
        source = lax.rem(tp_index + tp_size - distance, tp_size)
        return lax.dynamic_slice_in_dim(vis_out_w, source * width, width, axis=0)

    hidden_parts = []
    for part in range(part_count):
        hidden = vis_resid[part * part_rows : (part + 1) * part_rows].astype(jnp.float32)
        for distance in range(tp_size):
            block = contexts[part] if distance == 0 else arrived[part][distance - 1]
            hidden = hidden + jnp.dot(
                block, out_rows(distance), preferred_element_type=jnp.float32
            )
        if part == 0:
            handed, hidden = lax.optimization_barrier((handed, hidden))
            text_block = jnp.where(
                first_frame, jnp.where(second_frame, handed, text_high), text_low
            )
            text = Ring(text_block, rows)
        hidden_parts.append(hidden)
    hidden = jnp.concatenate(hidden_parts, axis=0)
    sums = jnp.stack([jnp.sum(hidden, axis=1), jnp.sum(hidden * hidden, axis=1)])
    others = [shifted(sums, "tp", distance) for distance in range(1, tp_size)]
    sums = text.advance(sums)
    row_sum, row_squares = functools.reduce(jnp.add, others, sums)
    mean_value = row_sum / VD
    variance = row_squares / VD - mean_value * mean_value
    normed = (hidden - mean_value[:, None]) * lax.rsqrt(variance + 1e-06)[
        :, None
    ] * merge_gain + merge_bias
    normed = normed.astype(jnp.bfloat16)

    received = []
    for distance in range(1, tp_size):
        block = lax.rem(tp_index + distance, tp_size)
        part = merged_columns(normed, vis_kv_w, block, local_kv, jnp.bfloat16)
        received.append(shifted(part, "tp", distance))
    normed = text.advance(normed)
    own = merged_columns(normed, vis_kv_w, tp_index, local_kv, jnp.float32)
    own = text.advance(own)
    for part in received:
        own = own + part.astype(jnp.float32)
    sources = block_sources(device, rows)
    frame_ids = jnp.arange(frames, dtype=jnp.int32)
    frame_rank = jnp.sum(
        jnp.where(frame_host[None, :] == sources[:, None], frame_ids[None, :], 0), axis=1
    ).astype(jnp.int32)
    slot_start = jnp.arange(positions // FT, dtype=jnp.int32) * FT
    is_text = jnp.all(slot_start[:, None] != vis_pos[None, :], axis=1)
    text_rank = jnp.sum(
        jnp.where(is_text[None, :] & (slot_start[None, :] < slot_start[:, None]), 1, 0), axis=1
    )
    text_ids = jnp.arange(positions // FT - frames, dtype=jnp.int32)
    text_pos = jnp.sum(
        jnp.where(
            is_text[None, :] & (text_rank[None, :] == text_ids[:, None]), slot_start[None, :], 0
        ),
        axis=1,
    ).astype(jnp.int32)
    owner = text_pos // per_device
    handed_on = jnp.all(vis_pos[None, :] // per_device != owner[:, None], axis=1) & (
        text_pos % per_device != 0
    )
    holder = jnp.where(handed_on, (owner + peers // 2) % peers, owner)
    held_rank = jnp.sum(
        jnp.where(holder[None, :] == sources[:, None], text_ids[None, :], 0), axis=1
    ).astype(jnp.int32)
    query_doc = lax.dynamic_slice_in_dim(doc_ids, first_pos, per_device)
    low = jnp.sum((doc_ids[None, :] < query_doc[:, None]).astype(jnp.int32), axis=1)
    lowest = jnp.sum((doc_ids < query_doc[0]).astype(jnp.int32))
    highest = jnp.sum((doc_ids < query_doc[-1]).astype(jnp.int32))
    low = jnp.broadcast_to(low[:, None], (per_device, FT))
    last_pos = first_pos + per_device - 1
    text_bounds = pair_bounds(text_pos, first_pos, last_pos, lowest, highest)
    vision_bounds = pair_bounds(vis_pos, first_pos, last_pos, lowest, highest)

    text_blocks = text.all()
    heads = local_kv // (2 * HD)
    vision = Ring(own.astype(jnp.bfloat16), rows)
    for _ in range(1, rows - 1):
        vision.advance(())
    text_blocks = vision.advance(text_blocks)
    state = attend(
        queries, text_blocks, text_bounds, held_rank, text_pos, low, head_range=(0, heads)
    )
    return attend(queries, vision.all(), vision_bounds, frame_rank, vis_pos, low, state)


def solution(mesh):
    return jax.shard_map(
        shards,
        mesh=mesh,
        in_specs=(
            P(("dp", "ctx"), None, "tp"),
            P(("dp", "ctx"), "tp"),
            P(None, "tp"),
            P("tp"),
            P("tp"),
            P(None, "tp", None),
            P("dp"),
            P("dp"),
            P("dp"),
            P(("dp", "ctx"), "tp", None, None),
            P(("dp", "ctx"), "tp"),
        ),
        out_specs=P(("dp", "ctx"), "tp"),
        check_vma=False,
    )
```

```python
import functools
import math

import jax
import jax.numpy as jnp
from jax import lax
from jax.experimental import pallas as pl
from jax.experimental.pallas import tpu as pltpu
from jax.sharding import PartitionSpec as P

VD = 1280
VH = 16
HD = 128
H = 32
KVH = 8
FT = 128
FP = 4 * FT
GROUP = H // KVH
DOCS = 4
LANES = 128

MASKED = -1e30
FLOOR = -1e29
TINY = 1e-30
VMEM_LIMIT = 16 * 1024 * 1024
MERGE_VMEM = 52 * 1024 * 1024
LANGUAGE_VMEM = 52 * 1024 * 1024


def contract_last(a, b):
    return lax.dot_general(a, b, (((1,), (1,)), ((), ())), preferred_element_type=jnp.float32)


def shifted(block, axis, distance):
    count = lax.axis_size(axis)
    return lax.ppermute(block, axis, [(i, (i + distance) % count) for i in range(count)])


def to_next_row(block, rows):
    return lax.ppermute(
        block,
        "ctx",
        [(2 * row + side, 2 * ((row + 1) % rows) + side) for row in range(rows) for side in range(2)],
    )


def to_other_side(block, rows):
    return lax.ppermute(
        block, "ctx", [(2 * row + side, 2 * row + 1 - side) for row in range(rows) for side in range(2)]
    )


class Ring:
    def __init__(self, block, rows):
        self.rows = rows
        self.blocks = [block]
        self.start(block)

    def start(self, block):
        self.moving = to_next_row(block, self.rows) if len(self.blocks) < 2 * self.rows - 1 else None
        self.blocks.append(to_other_side(block, self.rows))

    def advance(self, beside):
        if self.moving is None:
            return beside
        held, self.blocks[-1], beside = lax.optimization_barrier(
            (self.moving, self.blocks[-1], beside)
        )
        self.blocks.append(held)
        self.start(held)
        return beside

    def all(self):
        while self.moving is not None:
            self.advance(())
        return self.blocks


def vit_kernel(q_ref, k_ref, v_ref, after_ref, o_ref, *, heads, dim):
    width = q_ref.shape[2]
    to_exp = 1.0 / math.sqrt(dim)
    tiles = {}
    for g in range(heads):
        first, last = g * dim, (g + 1) * dim
        low = first // LANES * LANES
        high = min(width, -(-last // LANES) * LANES)
        lane = lax.broadcasted_iota(jnp.int32, (1, high - low), 1) + low
        inside = (lane >= first) & (lane < last)
        keep = jnp.where(inside, 1.0, 0.0).astype(jnp.bfloat16)
        rest = jnp.where(inside, 0.0, 1.0).astype(jnp.bfloat16)
        scores = contract_last(q_ref[0, :, low:high] * keep, k_ref[0, :, low:high])
        row_max = jnp.max(scores, axis=1, keepdims=True)
        weights = jnp.exp((scores - row_max) * to_exp).astype(jnp.bfloat16)
        mixed = jnp.dot(
            weights, v_ref[0, :, low:high] * keep + rest, preferred_element_type=jnp.float32
        )
        spare = 0 if low < first else last - low
        mixed = mixed / mixed[:, spare : spare + 1]
        for at in range(low, high, LANES):
            end = min(at + LANES, high)
            piece = mixed[:, at - low : end - low]
            if at in tiles:
                piece = jnp.where(inside[:, at - low : end - low], piece, tiles[at])
            tiles[at] = piece
    for at, piece in tiles.items():
        o_ref[:, at : at + piece.shape[1]] = piece.astype(o_ref.dtype)


def vit_attention(fields, after, part, part_count):
    _, patches, width = fields.shape
    frames = patches // FP
    rows = FP // part_count
    dim = VD // VH
    heads = width // dim
    return pl.pallas_call(
        functools.partial(vit_kernel, heads=heads, dim=dim),
        grid=(frames,),
        in_specs=[
            pl.BlockSpec((1, rows, width), lambda f: (0, f * part_count + part, 0)),
            pl.BlockSpec((1, FP, width), lambda f: (1, f, 0)),
            pl.BlockSpec((1, FP, width), lambda f: (2, f, 0)),
            pl.BlockSpec(memory_space=pl.ANY),
        ],
        out_specs=pl.BlockSpec((rows, width), lambda f: (f, 0)),
        out_shape=jax.ShapeDtypeStruct((frames * rows, width), jnp.bfloat16),
        compiler_params=pltpu.CompilerParams(vmem_limit_bytes=VMEM_LIMIT),
        cost_estimate=pl.CostEstimate(flops=1024, bytes_accessed=1024, transcendentals=0),
    )(fields, fields, fields, after)


def merge_kernel(block_ref, x_ref, w_ref, o_ref, held_ref, rows_ref, sems, *, step):
    tokens, columns = o_ref.shape
    patches = x_ref.shape[0]
    steps = columns // step

    def weights_in(n):
        source = w_ref.at[:, :, pl.ds(pl.multiple_of(block_ref[0] * columns + n * step, step), step)]
        return pltpu.make_async_copy(source, held_ref.at[n], sems.at[n])

    for n in range(steps):
        weights_in(n).start()
    token = lax.broadcasted_iota(jnp.int32, (tokens, patches), 0)
    patch = lax.broadcasted_iota(jnp.int32, (tokens, patches), 1)
    for j in range(4):
        pick = jnp.where(patch == 4 * token + j, 1.0, 0.0).astype(jnp.bfloat16)
        rows_ref[j] = jnp.dot(pick, x_ref[...], preferred_element_type=jnp.float32).astype(
            jnp.bfloat16
        )
    for n in range(steps):
        weights_in(n).wait()
        total = jnp.zeros((tokens, step), jnp.float32)
        for j in range(4):
            total = total + jnp.dot(
                rows_ref[j], held_ref[n, j], preferred_element_type=jnp.float32
            )
        o_ref[:, n * step : (n + 1) * step] = total.astype(o_ref.dtype)


def merged_columns(normed, weights, block, columns, dtype):
    patches, width = normed.shape
    tokens = patches // 4
    step = min(columns, 256)
    steps = columns // step
    return pl.pallas_call(
        functools.partial(merge_kernel, step=step),
        in_specs=[
            pl.BlockSpec(memory_space=pltpu.SMEM),
            pl.BlockSpec(memory_space=pltpu.VMEM),
            pl.BlockSpec(memory_space=pl.ANY),
        ],
        out_specs=pl.BlockSpec(memory_space=pltpu.VMEM),
        out_shape=jax.ShapeDtypeStruct((tokens, columns), dtype),
        scratch_shapes=[
            pltpu.VMEM((steps, 4, width, step), jnp.bfloat16),
            pltpu.VMEM((4, tokens, width), jnp.bfloat16),
            pltpu.SemaphoreType.DMA((steps,)),
        ],
        compiler_params=pltpu.CompilerParams(vmem_limit_bytes=MERGE_VMEM),
        cost_estimate=pl.CostEstimate(
            flops=2 * tokens * 4 * width * columns,
            bytes_accessed=4 * width * columns * 2 + patches * width * 2,
            transcendentals=0,
        ),
    )(jnp.reshape(block, (1,)), normed, weights)


def tables_kernel(
    device_ref, vis_pos_ref, frame_host_ref, doc_ref,
    choice_ref, text_ref, text_rank_ref, text_pos_ref, vision_ref, vision_rank_ref,
    *, peers, per_device,
):
    device = device_ref[0]
    rows = peers // 2
    frames, texts = vis_pos_ref.shape[0], text_pos_ref.shape[0]
    slots_each = per_device // FT
    first_pos = device * per_device
    last_pos = first_pos + per_device - 1
    starts = [
        jnp.sum(jnp.where(doc_ref[...] < d, 1.0, 0.0)).astype(jnp.int32) for d in range(1, DOCS)
    ]

    def first_key(pos):
        return functools.reduce(jnp.maximum, [jnp.where(s <= pos, s, 0) for s in starts])

    lowest, highest = first_key(first_pos), first_key(last_pos)

    def block_from(source):
        hop = lax.rem(device // 2 + rows - source // 2, rows)
        return 2 * hop + jnp.where(lax.rem(source, 2) == lax.rem(device, 2), 0, 1)

    def one_frame(f, _):
        vision_rank_ref[block_from(frame_host_ref[f])] = f
        return 0

    lax.fori_loop(0, frames, one_frame, 0)

    def one_slot(slot, carry):
        frame, text, before_is_text, own = carry
        pos = slot * FT
        is_frame = (frame < frames) & (vis_pos_ref[jnp.minimum(frame, frames - 1)] == pos)
        owner = slot // slots_each
        second = lax.rem(slot, slots_each) != 0
        partner = lax.rem(owner + peers // 2, peers)
        holder = jnp.where(second & (before_is_text == 1), partner, owner)

        @pl.when(jnp.logical_not(is_frame))
        def _():
            text_pos_ref[text] = pos
            text_rank_ref[block_from(holder)] = text

        flag = jnp.where(is_frame, 1, 0)
        own = own + jnp.where(pos == first_pos, flag, 0) + jnp.where(pos == first_pos + FT, 2 * flag, 0)
        return frame + flag, text + 1 - flag, 1 - flag, own

    zero = jnp.int32(0)
    _, _, _, own = lax.fori_loop(0, peers * slots_each, one_slot, (zero, zero, zero, zero))
    choice_ref[0] = jnp.where(own == 3, 2, jnp.where(own == 1, 1, 0))

    for table_ref, pos_ref, count in (
        (text_ref, text_pos_ref, texts),
        (vision_ref, vis_pos_ref, frames),
    ):

        def one_pair(pair, sums):
            first, last = pos_ref[2 * pair], pos_ref[2 * pair + 1] + FT - 1
            tests = (last < lowest, first <= last_pos, first < highest, last <= first_pos)
            return tuple(s + jnp.where(t, 1, 0) for s, t in zip(sums, tests))

        begin, end, full, whole = lax.fori_loop(0, count // 2, one_pair, (zero,) * 4)
        end = jnp.maximum(begin, end)
        full = jnp.clip(full, begin, end)
        whole = jnp.clip(whole, full, end)
        for i, value in enumerate([begin, full, whole, end, first_pos] + starts):
            table_ref[i] = value


def tables(device, vis_pos, frame_host, doc_ids, peers, per_device):
    frames = vis_pos.shape[0]
    texts = doc_ids.shape[0] // FT - frames
    scalars = pl.BlockSpec(memory_space=pltpu.SMEM)
    lengths = (1, 4 + DOCS, texts, texts, 4 + DOCS, frames)
    return pl.pallas_call(
        functools.partial(tables_kernel, peers=peers, per_device=per_device),
        in_specs=[scalars] * 3 + [pl.BlockSpec(memory_space=pltpu.VMEM)],
        out_specs=[scalars] * len(lengths),
        out_shape=[jax.ShapeDtypeStruct((length,), jnp.int32) for length in lengths],
    )(jnp.reshape(device, (1,)), vis_pos, frame_host, doc_ids.reshape(-1, LANES))


def attend_kernel(
    table_ref, rank_ref, slot_pos_ref, q_ref, *rest, blocks, rows, final, first_head, heads
):
    block_refs, rest = rest[:blocks], rest[blocks:]
    if final:
        acc_refs, log_refs, out_ref = rest[:heads], rest[heads : 2 * heads], rest[2 * heads]
        held_acc_ref, held_log_ref, result_ref = rest[2 * heads + 1 : 2 * heads + 4]
    else:
        acc_out_ref, log_out_ref = rest[:2]
    kv_ref, held_q_ref, query_ref, bias_ref, score_ref, max_ref, acc_ref, sems = rest[-8:]
    scale = 1.0 / math.sqrt(HD)
    wide = GROUP * HD
    first_pair, full_first, full_last, last_pair, first_pos = (table_ref[i] for i in range(5))
    starts = [table_ref[i] for i in range(5, 4 + DOCS)]
    lane = lax.broadcasted_iota(jnp.int32, (rows, FT), 1)

    kv_lanes = slice(first_head * 2 * HD, (first_head + heads) * 2 * HD)
    copies = [
        (q_ref.at[:, first_head * wide : (first_head + heads) * wide], held_q_ref)
    ]
    for i, block_ref in enumerate(block_refs):
        there = pl.ds(pl.multiple_of(rank_ref[i] * FT, FT), FT)
        copies.append((block_ref.at[:, kv_lanes], kv_ref.at[there]))
    early = len(copies)
    if final:
        for h in range(heads):
            copies += [(acc_refs[h], held_acc_ref.at[h]), (log_refs[h], held_log_ref.at[h])]
    copies = [pltpu.make_async_copy(*pair, sems.at[i]) for i, pair in enumerate(copies)]
    for copy in copies:
        copy.start()

    def mask(pair):
        query_pos = first_pos + lax.broadcasted_iota(jnp.int32, (rows, FT), 0)
        low = functools.reduce(jnp.maximum, [jnp.where(s <= query_pos, s, 0) for s in starts])
        for half in range(2):
            key_pos = slot_pos_ref[2 * pair + half] + lane
            allowed = (key_pos <= query_pos) & (key_pos >= low)
            bias_ref[pair, :, half * FT : (half + 1) * FT] = jnp.where(allowed, 0.0, MASKED)

    pl.loop(first_pair, full_first)(mask)
    pl.loop(full_last, last_pair)(mask)
    for copy in copies[:early]:
        copy.wait()

    for h in range(heads):
        for g in range(GROUP):
            at = h * wide + g * HD
            query_ref[g * rows : (g + 1) * rows] = held_q_ref[:, at : at + HD]
        max_ref[...] = jnp.full_like(max_ref, FLOOR)

        def score(pair, masked):
            here = pl.ds(pl.multiple_of(pair * 2 * FT, 2 * FT), 2 * FT)
            keys = kv_ref[here, 2 * h * HD : (2 * h + 1) * HD]
            scores = contract_last(query_ref[...], keys) * scale
            if masked:
                scores = scores.reshape(GROUP, rows, 2 * FT) + bias_ref[pair][None]
                scores = scores.reshape(GROUP * rows, 2 * FT)
            score_ref[pair] = scores
            max_ref[...] = jnp.maximum(
                max_ref[...], jnp.maximum(scores[:, :FT], scores[:, FT:])
            )

        pl.loop(first_pair, full_first)(functools.partial(score, masked=True))
        pl.loop(full_first, full_last)(functools.partial(score, masked=False))
        pl.loop(full_last, last_pair)(functools.partial(score, masked=True))

        row_max = jnp.max(max_ref[...], axis=1, keepdims=True)
        if final:
            for copy in copies[early + 2 * h : early + 2 * h + 2]:
                copy.wait()
            logs = jnp.concatenate([held_log_ref[h, :, g : g + 1] for g in range(GROUP)], axis=0)
            row_max = jnp.maximum(row_max, logs)
            weight = jnp.broadcast_to(jnp.exp(logs - row_max), (GROUP * rows, HD))
            for g in range(GROUP):
                here = slice(g * rows, (g + 1) * rows)
                acc_ref[here, :HD] = held_acc_ref[h, :, g * HD : (g + 1) * HD] * weight[here]
            acc_ref[:, HD:] = weight
        else:
            acc_ref[...] = jnp.zeros_like(acc_ref)
        max_ref[...] = jnp.broadcast_to(row_max, max_ref.shape)

        @pl.loop(first_pair, last_pair)
        def _(pair):
            here = pl.ds(pl.multiple_of(pair * 2 * FT, 2 * FT), 2 * FT)
            values = kv_ref[here, (2 * h + 1) * HD : (2 * h + 2) * HD]
            values = jnp.concatenate([values, jnp.ones_like(values)], axis=1)
            weights = [
                jnp.exp(score_ref[pair, :, half * FT : (half + 1) * FT] - max_ref[...])
                for half in range(2)
            ]
            weights = jnp.concatenate([each.astype(jnp.bfloat16) for each in weights], axis=1)
            acc_ref[...] += jnp.dot(weights, values, preferred_element_type=jnp.float32)

        if final:
            mixed = acc_ref[:, :HD] / acc_ref[:, HD:]
            for g in range(GROUP):
                result_ref[h, :, g * HD : (g + 1) * HD] = mixed[
                    g * rows : (g + 1) * rows
                ].astype(result_ref.dtype)
            pltpu.make_async_copy(
                result_ref.at[h], out_ref.at[:, h * wide : (h + 1) * wide], sems.at[h]
            ).start()
        else:
            total = jnp.maximum(acc_ref[:, HD:], TINY)
            mixed = acc_ref[:, :HD] / total
            logs = max_ref[...] + jnp.log(total)
            packed = jnp.zeros((rows, FT), jnp.float32)
            for g in range(GROUP):
                here = slice(g * rows, (g + 1) * rows)
                acc_out_ref[:, g * HD : (g + 1) * HD] = mixed[here]
                packed = jnp.where(lane == g, logs[here], packed)
            log_out_ref[...] = packed
    if final:
        for h in range(heads):
            pltpu.make_async_copy(
                result_ref.at[h], out_ref.at[:, h * wide : (h + 1) * wide], sems.at[h]
            ).wait()


def attend(queries, blocks, table, rank, slot_pos, states=None, head=None):
    rows = queries.shape[0]
    columns = blocks[0].shape[1]
    slots = len(blocks)
    pairs = slots // 2
    final = head is None
    first_head, heads = (0, columns // (2 * HD)) if final else (head, 1)
    wide = GROUP * HD
    tall = GROUP * rows
    anywhere = pl.BlockSpec(memory_space=pl.ANY)
    whole = pl.BlockSpec(memory_space=pltpu.VMEM)
    scalars = pl.BlockSpec(memory_space=pltpu.SMEM)
    scratch = [
        pltpu.VMEM((slots * FT, heads * 2 * HD), jnp.bfloat16),
        pltpu.VMEM((rows, heads * wide), jnp.bfloat16),
        pltpu.VMEM((tall, HD), jnp.bfloat16),
        pltpu.VMEM((pairs, rows, 2 * FT), jnp.float32),
        pltpu.VMEM((pairs, tall, 2 * FT), jnp.float32),
        pltpu.VMEM((tall, FT), jnp.float32),
        pltpu.VMEM((tall, 2 * HD), jnp.float32),
        pltpu.SemaphoreType.DMA((1 + slots + 2 * heads,)),
    ]
    arrays = []
    if final:
        arrays = [acc for acc, _ in states] + [logs for _, logs in states]
        out_specs = anywhere
        out_shape = jax.ShapeDtypeStruct((rows, heads * wide), jnp.bfloat16)
        scratch = [
            pltpu.VMEM((heads, rows, wide), jnp.float32),
            pltpu.VMEM((heads, rows, FT), jnp.float32),
            pltpu.VMEM((heads, rows, wide), jnp.bfloat16),
        ] + scratch
    else:
        out_specs = [whole] * 2
        out_shape = [
            jax.ShapeDtypeStruct((rows, wide), jnp.float32),
            jax.ShapeDtypeStruct((rows, FT), jnp.float32),
        ]
    cells = heads * tall * slots * FT
    return pl.pallas_call(
        functools.partial(
            attend_kernel,
            blocks=slots,
            rows=rows,
            final=final,
            first_head=first_head,
            heads=heads,
        ),
        in_specs=[scalars] * 3 + [anywhere] * (1 + slots + len(arrays)),
        out_specs=out_specs,
        out_shape=out_shape,
        scratch_shapes=scratch,
        compiler_params=pltpu.CompilerParams(vmem_limit_bytes=LANGUAGE_VMEM),
        cost_estimate=pl.CostEstimate(
            flops=6 * cells * HD,
            bytes_accessed=2 * slots * FT * columns + 8 * heads * tall * FT,
            transcendentals=cells,
        ),
    )(table, rank, slot_pos, queries, *blocks, *arrays)


def shards(
    vis_qkv,
    vis_resid,
    vis_out_w,
    merge_gain,
    merge_bias,
    vis_kv_w,
    frame_host,
    vis_pos,
    doc_ids,
    text_kv,
    queries,
):
    device = lax.axis_index("ctx")
    tp_index = lax.axis_index("tp")
    tp_size = lax.axis_size("tp")
    per_device = queries.shape[0]
    patches = vis_qkv.shape[0]
    width = vis_qkv.shape[2]
    frames_dev = patches // FP
    local_kv = vis_kv_w.shape[2] // tp_size
    positions = doc_ids.shape[0]
    frames = vis_pos.shape[0]

    peers = lax.axis_size("ctx")
    rows = peers // 2
    first_pos = device * per_device

    fields = jnp.transpose(vis_qkv, (1, 0, 2))
    part_count = 2 if frames_dev == 1 else 1
    part_rows = patches // part_count
    text_low = text_kv[:FT].reshape(FT, local_kv)
    text_high = text_kv[FT:].reshape(FT, local_kv)
    handed = shifted(text_high, "ctx", peers // 2)
    contexts = []
    for part in range(part_count):
        after = text_high if part == 0 else contexts[-1]
        contexts.append(vit_attention(fields, after, part, part_count))
    vis_pos_then, _ = lax.optimization_barrier((vis_pos, contexts[-1]))
    choice, text_table, text_rank, text_pos, vision_table, vision_rank = tables(
        device, vis_pos_then, frame_host, doc_ids, peers, per_device
    )
    choice = choice[0]
    arrived = [
        [shifted(context, "tp", distance) for distance in range(1, tp_size)]
        for context in contexts
    ]

    def out_rows(distance):
        source = lax.rem(tp_index + tp_size - distance, tp_size)
        return lax.dynamic_slice_in_dim(vis_out_w, source * width, width, axis=0)

    hidden_parts = []
    for part in range(part_count):
        hidden = vis_resid[part * part_rows : (part + 1) * part_rows].astype(jnp.float32)
        for distance in range(tp_size):
            block = contexts[part] if distance == 0 else arrived[part][distance - 1]
            hidden = hidden + jnp.dot(
                block, out_rows(distance), preferred_element_type=jnp.float32
            )
        if part == 0:
            handed, hidden = lax.optimization_barrier((handed, hidden))
            text_block = jnp.where(
                choice == 2, handed, jnp.where(choice == 1, text_high, text_low)
            )
            text = Ring(text_block, rows)
        hidden_parts.append(hidden)
    hidden = jnp.concatenate(hidden_parts, axis=0)
    sums = jnp.stack([jnp.sum(hidden, axis=1), jnp.sum(hidden * hidden, axis=1)])
    others = [shifted(sums, "tp", distance) for distance in range(1, tp_size)]
    sums = text.advance(sums)
    row_sum, row_squares = functools.reduce(jnp.add, others, sums)
    mean_value = row_sum / VD
    variance = row_squares / VD - mean_value * mean_value
    normed = (hidden - mean_value[:, None]) * lax.rsqrt(variance + 1e-06)[
        :, None
    ] * merge_gain + merge_bias
    normed = normed.astype(jnp.bfloat16)

    received = []
    for distance in range(1, tp_size):
        block = lax.rem(tp_index + distance, tp_size)
        part = merged_columns(normed, vis_kv_w, block, local_kv, jnp.bfloat16)
        received.append(shifted(part, "tp", distance))
    normed = text.advance(normed)
    own = merged_columns(normed, vis_kv_w, tp_index, local_kv, jnp.float32)
    own = text.advance(own)
    for part in received:
        own = own + part.astype(jnp.float32)
    text_blocks = text.all()
    heads = local_kv // (2 * HD)
    vision = Ring(own.astype(jnp.bfloat16), rows)
    states = []
    for hop in range(1, rows):
        if hop > 1 and len(states) < heads:
            states.append(
                attend(queries, text_blocks, text_table, text_rank, text_pos, head=len(states))
            )
            text_blocks, states = vision.advance((text_blocks, states))
        elif hop == 1:
            text_blocks = vision.advance(text_blocks)
        else:
            vision.advance(())
    while len(states) < heads:
        states.append(
            attend(queries, text_blocks, text_table, text_rank, text_pos, head=len(states))
        )
    return attend(queries, vision.all(), vision_table, vision_rank, vis_pos, states)


def solution(mesh):
    return jax.shard_map(
        shards,
        mesh=mesh,
        in_specs=(
            P(("dp", "ctx"), None, "tp"),
            P(("dp", "ctx"), "tp"),
            P(None, "tp"),
            P("tp"),
            P("tp"),
            P(None, "tp", None),
            P("dp"),
            P("dp"),
            P("dp"),
            P(("dp", "ctx"), "tp", None, None),
            P(("dp", "ctx"), "tp"),
        ),
        out_specs=P(("dp", "ctx"), "tp"),
        check_vma=False,
    )
```

```python
import functools
import math

import jax
import jax.numpy as jnp
from jax import lax
from jax.experimental import pallas as pl
from jax.experimental.pallas import tpu as pltpu
from jax.sharding import PartitionSpec as P

VD = 1280
VH = 16
HD = 128
H = 32
KVH = 8
FT = 128
FP = 4 * FT
GROUP = H // KVH
DOCS = 4
LANES = 128

MASKED = -1e30
VMEM_LIMIT = 16 * 1024 * 1024
MERGE_VMEM = 52 * 1024 * 1024
LANGUAGE_VMEM = 52 * 1024 * 1024


def contract_last(a, b):
    return lax.dot_general(a, b, (((1,), (1,)), ((), ())), preferred_element_type=jnp.float32)


def shifted(block, axis, distance):
    count = lax.axis_size(axis)
    return lax.ppermute(block, axis, [(i, (i + distance) % count) for i in range(count)])


def to_next_row(block, rows):
    return lax.ppermute(
        block,
        "ctx",
        [(2 * row + side, 2 * ((row + 1) % rows) + side) for row in range(rows) for side in range(2)],
    )


def to_other_side(block, rows):
    return lax.ppermute(
        block, "ctx", [(2 * row + side, 2 * row + 1 - side) for row in range(rows) for side in range(2)]
    )


class Ring:
    def __init__(self, block, rows):
        self.rows = rows
        self.blocks = [block]
        self.start(block)

    def start(self, block):
        self.moving = to_next_row(block, self.rows) if len(self.blocks) < 2 * self.rows - 1 else None
        self.blocks.append(to_other_side(block, self.rows))

    def advance(self, beside, lag=0):
        if self.moving is None:
            return beside
        if len(self.blocks) > 2 * lag:
            at = len(self.blocks) - 1 - 2 * lag
            held, self.blocks[at], beside = lax.optimization_barrier(
                (self.moving, self.blocks[at], beside)
            )
        else:
            held, beside = lax.optimization_barrier((self.moving, beside))
        self.blocks.append(held)
        self.start(held)
        return beside

    def all(self):
        while self.moving is not None:
            self.advance(())
        return self.blocks


def vit_kernel(q_ref, k_ref, v_ref, after_ref, o_ref, *, heads, dim):
    width = q_ref.shape[2]
    to_exp = 1.0 / math.sqrt(dim)
    tiles = {}
    for g in range(heads):
        first, last = g * dim, (g + 1) * dim
        low = first // LANES * LANES
        high = min(width, -(-last // LANES) * LANES)
        lane = lax.broadcasted_iota(jnp.int32, (1, high - low), 1) + low
        inside = (lane >= first) & (lane < last)
        keep = jnp.where(inside, 1.0, 0.0).astype(jnp.bfloat16)
        rest = jnp.where(inside, 0.0, 1.0).astype(jnp.bfloat16)
        scores = contract_last(q_ref[0, :, low:high] * keep, k_ref[0, :, low:high])
        row_max = jnp.max(scores, axis=1, keepdims=True)
        weights = jnp.exp((scores - row_max) * to_exp).astype(jnp.bfloat16)
        mixed = jnp.dot(
            weights, v_ref[0, :, low:high] * keep + rest, preferred_element_type=jnp.float32
        )
        spare = 0 if low < first else last - low
        mixed = mixed / mixed[:, spare : spare + 1]
        for at in range(low, high, LANES):
            end = min(at + LANES, high)
            piece = mixed[:, at - low : end - low]
            if at in tiles:
                piece = jnp.where(inside[:, at - low : end - low], piece, tiles[at])
            tiles[at] = piece
    for at, piece in tiles.items():
        o_ref[:, at : at + piece.shape[1]] = piece.astype(o_ref.dtype)


def vit_attention(fields, after, part, part_count):
    _, patches, width = fields.shape
    frames = patches // FP
    rows = FP // part_count
    dim = VD // VH
    heads = width // dim
    return pl.pallas_call(
        functools.partial(vit_kernel, heads=heads, dim=dim),
        grid=(frames,),
        in_specs=[
            pl.BlockSpec((1, rows, width), lambda f: (0, f * part_count + part, 0)),
            pl.BlockSpec((1, FP, width), lambda f: (1, f, 0)),
            pl.BlockSpec((1, FP, width), lambda f: (2, f, 0)),
            pl.BlockSpec(memory_space=pl.ANY),
        ],
        out_specs=pl.BlockSpec((rows, width), lambda f: (f, 0)),
        out_shape=jax.ShapeDtypeStruct((frames * rows, width), jnp.bfloat16),
        compiler_params=pltpu.CompilerParams(vmem_limit_bytes=VMEM_LIMIT),
        cost_estimate=pl.CostEstimate(flops=1024, bytes_accessed=1024, transcendentals=0),
    )(fields, fields, fields, after)


def merge_kernel(block_ref, x_ref, w_ref, o_ref, held_ref, rows_ref, sems, *, step):
    tokens, columns = o_ref.shape
    patches = x_ref.shape[0]
    steps = columns // step

    def weights_in(n):
        source = w_ref.at[:, :, pl.ds(pl.multiple_of(block_ref[0] * columns + n * step, step), step)]
        return pltpu.make_async_copy(source, held_ref.at[n], sems.at[n])

    for n in range(steps):
        weights_in(n).start()
    token = lax.broadcasted_iota(jnp.int32, (tokens, patches), 0)
    patch = lax.broadcasted_iota(jnp.int32, (tokens, patches), 1)
    for j in range(4):
        pick = jnp.where(patch == 4 * token + j, 1.0, 0.0).astype(jnp.bfloat16)
        rows_ref[j] = jnp.dot(pick, x_ref[...], preferred_element_type=jnp.float32).astype(
            jnp.bfloat16
        )
    for n in range(steps):
        weights_in(n).wait()
        total = jnp.zeros((tokens, step), jnp.float32)
        for j in range(4):
            total = total + jnp.dot(
                rows_ref[j], held_ref[n, j], preferred_element_type=jnp.float32
            )
        o_ref[:, n * step : (n + 1) * step] = total.astype(o_ref.dtype)


def merged_columns(normed, weights, block, columns, dtype):
    patches, width = normed.shape
    tokens = patches // 4
    step = min(columns, 256)
    steps = columns // step
    return pl.pallas_call(
        functools.partial(merge_kernel, step=step),
        in_specs=[
            pl.BlockSpec(memory_space=pltpu.SMEM),
            pl.BlockSpec(memory_space=pltpu.VMEM),
            pl.BlockSpec(memory_space=pl.ANY),
        ],
        out_specs=pl.BlockSpec(memory_space=pltpu.VMEM),
        out_shape=jax.ShapeDtypeStruct((tokens, columns), dtype),
        scratch_shapes=[
            pltpu.VMEM((steps, 4, width, step), jnp.bfloat16),
            pltpu.VMEM((4, tokens, width), jnp.bfloat16),
            pltpu.SemaphoreType.DMA((steps,)),
        ],
        compiler_params=pltpu.CompilerParams(vmem_limit_bytes=MERGE_VMEM),
        cost_estimate=pl.CostEstimate(
            flops=2 * tokens * 4 * width * columns,
            bytes_accessed=4 * width * columns * 2 + patches * width * 2,
            transcendentals=0,
        ),
    )(jnp.reshape(block, (1,)), normed, weights)


def tables_kernel(
    device_ref, vis_pos_ref, frame_host_ref, doc_ref, choice_ref, place_ref, bounds_ref,
    *, peers, per_device,
):
    device = device_ref[0]
    rows = peers // 2
    frames = vis_pos_ref.shape[0]
    slots_each = per_device // FT
    first_pos = device * per_device
    starts = [
        jnp.sum(jnp.where(doc_ref[...] < d, 1.0, 0.0)).astype(jnp.int32) for d in range(1, DOCS)
    ]
    for i, value in enumerate([first_pos] + starts):
        bounds_ref[i] = value

    def block_from(source):
        hop = lax.rem(device // 2 + rows - source // 2, rows)
        return 2 * hop + jnp.where(lax.rem(source, 2) == lax.rem(device, 2), 0, 1)

    def one_slot(slot, carry):
        frame, before_is_text, own = carry
        pos = slot * FT
        here = jnp.minimum(frame, frames - 1)
        is_frame = (frame < frames) & (vis_pos_ref[here] == pos)
        owner = slot // slots_each
        second = lax.rem(slot, slots_each) != 0
        partner = lax.rem(owner + peers // 2, peers)
        holder = jnp.where(second & (before_is_text == 1), partner, owner)
        source = jnp.where(is_frame, frame_host_ref[here], holder)
        place_ref[block_from(source) + jnp.where(is_frame, peers, 0)] = pos
        flag = jnp.where(is_frame, 1, 0)
        own = own + jnp.where(pos == first_pos, flag, 0) + jnp.where(pos == first_pos + FT, 2 * flag, 0)
        return frame + flag, 1 - flag, own

    zero = jnp.int32(0)
    _, _, own = lax.fori_loop(0, peers * slots_each, one_slot, (zero, zero, zero))
    choice_ref[0] = jnp.where(own == 3, 2, jnp.where(own == 1, 1, 0))


def tables(device, vis_pos, frame_host, doc_ids, peers, per_device):
    scalars = pl.BlockSpec(memory_space=pltpu.SMEM)
    lengths = (1, 2 * peers, DOCS)
    return pl.pallas_call(
        functools.partial(tables_kernel, peers=peers, per_device=per_device),
        in_specs=[scalars] * 3 + [pl.BlockSpec(memory_space=pltpu.VMEM)],
        out_specs=[scalars] * len(lengths),
        out_shape=[jax.ShapeDtypeStruct((length,), jnp.int32) for length in lengths],
    )(jnp.reshape(device, (1,)), vis_pos, frame_host, doc_ids.reshape(-1, LANES))


def attend_kernel(bounds_ref, place_ref, q_ref, *rest, slots, heads):
    slot_refs, out_ref = rest[:slots], rest[slots]
    kv_ref, held_q_ref, query_ref, bias_ref, score_ref, max_ref, acc_ref, result_ref = rest[
        slots + 1 : slots + 9
    ]
    slot_sems, query_sems, out_sems = rest[slots + 9 :]
    rows = q_ref.shape[0]
    scale = 1.0 / math.sqrt(HD)
    wide = GROUP * HD
    first_pos = bounds_ref[0]
    starts = [bounds_ref[i] for i in range(1, DOCS)]

    def first_key(pos):
        return functools.reduce(jnp.maximum, [jnp.where(s <= pos, s, 0) for s in starts])

    last = first_pos // rows
    first = first_key(first_pos) // rows
    whole = jnp.minimum((first_key(first_pos + rows - 1) + rows - 1) // rows, last)

    cuts = [(0, 1)] + [(1, heads)] * (heads > 1)

    def slot_copy(i, cut):
        begin, end = cuts[cut]
        lanes = slice(begin * 2 * HD, end * 2 * HD)
        there = pl.ds(pl.multiple_of(place_ref[i], FT), FT)
        return pltpu.make_async_copy(
            slot_refs[i].at[:, lanes], kv_ref.at[there, lanes], slot_sems.at[cut, i]
        )

    def query_copy(cut):
        begin, end = cuts[cut]
        lanes = slice(begin * wide, end * wide)
        return pltpu.make_async_copy(
            q_ref.at[:, lanes], held_q_ref.at[:, lanes], query_sems.at[cut]
        )

    def wanted(i):
        block = place_ref[i] // rows
        return (block >= first) & (block <= last)

    def all_slots(cut, act):
        for i in range(slots):
            pl.when(wanted(i))(functools.partial(act, i, cut))

    for cut in range(len(cuts)):
        query_copy(cut).start()
        all_slots(cut, lambda i, cut: slot_copy(i, cut).start())

    def mask(block):
        query_pos = first_pos + lax.broadcasted_iota(jnp.int32, (rows, FT), 0)
        low = first_key(query_pos)
        for at in range(0, rows, FT):
            key_pos = block * rows + at + lax.broadcasted_iota(jnp.int32, (rows, FT), 1)
            allowed = (key_pos <= query_pos) & (key_pos >= low)
            bias_ref[block, :, at : at + FT] = jnp.where(allowed, 0.0, MASKED)

    pl.loop(first, whole)(mask)
    mask(last)

    def result_copy(h):
        return pltpu.make_async_copy(
            result_ref.at[h], out_ref.at[:, h * wide : (h + 1) * wide], out_sems.at[h]
        )

    for h in range(heads):
        if h < len(cuts):
            query_copy(h).wait()
            all_slots(h, lambda i, cut: slot_copy(i, cut).wait())
        for g in range(GROUP):
            at = h * wide + g * HD
            query_ref[g * rows : (g + 1) * rows] = held_q_ref[:, at : at + HD]

        def score(block, masked, initial):
            here = pl.ds(pl.multiple_of(block * rows, rows), rows)
            keys = kv_ref[here, 2 * h * HD : (2 * h + 1) * HD]
            scores = contract_last(query_ref[...], keys) * scale
            if masked:
                scores = scores.reshape(GROUP, rows, rows) + bias_ref[block][None]
                scores = scores.reshape(GROUP * rows, rows)
            score_ref[block] = scores
            parts = [scores[:, at : at + FT] for at in range(0, rows, FT)]
            if not initial:
                parts.append(max_ref[...])
            max_ref[...] = functools.reduce(jnp.maximum, parts)

        score(last, masked=True, initial=True)
        pl.loop(first, whole)(functools.partial(score, masked=True, initial=False))
        pl.loop(whole, last)(functools.partial(score, masked=False, initial=False))
        row_max = jnp.max(max_ref[...], axis=1, keepdims=True)
        max_ref[...] = jnp.broadcast_to(row_max, max_ref.shape)

        def mix(block):
            here = pl.ds(pl.multiple_of(block * rows, rows), rows)
            values = kv_ref[here, (2 * h + 1) * HD : (2 * h + 2) * HD]
            values = jnp.concatenate([values, jnp.ones_like(values)], axis=1)
            weights = [
                jnp.exp(score_ref[block, :, at : at + FT] - max_ref[...]).astype(jnp.bfloat16)
                for at in range(0, rows, FT)
            ]
            weights = jnp.concatenate(weights, axis=1)
            return jnp.dot(weights, values, preferred_element_type=jnp.float32)

        acc_ref[...] = mix(last)

        @pl.loop(first, last)
        def _(block):
            acc_ref[...] += mix(block)

        mixed = acc_ref[:, :HD] / acc_ref[:, HD:]
        for g in range(GROUP):
            result_ref[h, :, g * HD : (g + 1) * HD] = mixed[g * rows : (g + 1) * rows].astype(
                result_ref.dtype
            )
        result_copy(h).start()
    for h in range(heads):
        result_copy(h).wait()


def attend(queries, slots, bounds, place):
    rows = queries.shape[0]
    columns = slots[0].shape[1]
    heads = columns // (2 * HD)
    blocks = len(slots) * FT // rows
    wide = GROUP * HD
    tall = GROUP * rows
    anywhere = pl.BlockSpec(memory_space=pl.ANY)
    scalars = pl.BlockSpec(memory_space=pltpu.SMEM)
    cells = heads * tall * blocks * rows
    return pl.pallas_call(
        functools.partial(attend_kernel, slots=len(slots), heads=heads),
        in_specs=[scalars] * 2 + [anywhere] * (1 + len(slots)),
        out_specs=anywhere,
        out_shape=jax.ShapeDtypeStruct(queries.shape, jnp.bfloat16),
        scratch_shapes=[
            pltpu.VMEM((len(slots) * FT, columns), jnp.bfloat16),
            pltpu.VMEM(queries.shape, jnp.bfloat16),
            pltpu.VMEM((tall, HD), jnp.bfloat16),
            pltpu.VMEM((blocks, rows, rows), jnp.float32),
            pltpu.VMEM((blocks, tall, rows), jnp.float32),
            pltpu.VMEM((tall, FT), jnp.float32),
            pltpu.VMEM((tall, 2 * HD), jnp.float32),
            pltpu.VMEM((heads, rows, wide), jnp.bfloat16),
            pltpu.SemaphoreType.DMA((2, len(slots))),
            pltpu.SemaphoreType.DMA((2,)),
            pltpu.SemaphoreType.DMA((heads,)),
        ],
        compiler_params=pltpu.CompilerParams(vmem_limit_bytes=LANGUAGE_VMEM),
        cost_estimate=pl.CostEstimate(
            flops=6 * cells * HD,
            bytes_accessed=2 * len(slots) * FT * columns + 4 * rows * heads * wide,
            transcendentals=cells,
        ),
    )(bounds, place, queries, *slots)


def shards(
    vis_qkv,
    vis_resid,
    vis_out_w,
    merge_gain,
    merge_bias,
    vis_kv_w,
    frame_host,
    vis_pos,
    doc_ids,
    text_kv,
    queries,
):
    device = lax.axis_index("ctx")
    tp_index = lax.axis_index("tp")
    tp_size = lax.axis_size("tp")
    per_device = queries.shape[0]
    patches = vis_qkv.shape[0]
    width = vis_qkv.shape[2]
    frames_dev = patches // FP
    local_kv = vis_kv_w.shape[2] // tp_size
    positions = doc_ids.shape[0]
    frames = vis_pos.shape[0]

    peers = lax.axis_size("ctx")
    rows = peers // 2
    first_pos = device * per_device

    fields = jnp.transpose(vis_qkv, (1, 0, 2))
    part_count = 2 if frames_dev == 1 else 1
    part_rows = patches // part_count
    text_low, text_high = text_kv[:FT], text_kv[FT:]
    handed = shifted(text_high, "ctx", peers // 2)
    contexts = []
    for part in range(part_count):
        after = text_high if part == 0 else contexts[-1]
        contexts.append(vit_attention(fields, after, part, part_count))
    vis_pos, _ = lax.optimization_barrier((vis_pos, contexts[-1]))
    choice, place, bounds = tables(device, vis_pos, frame_host, doc_ids, peers, per_device)
    arrived = [
        [shifted(context, "tp", distance) for distance in range(1, tp_size)]
        for context in contexts
    ]

    def out_rows(distance):
        source = lax.rem(tp_index + tp_size - distance, tp_size)
        return lax.dynamic_slice_in_dim(vis_out_w, source * width, width, axis=0)

    hidden_parts = []
    for part in range(part_count):
        resid = vis_resid[part * part_rows : (part + 1) * part_rows].astype(jnp.float32)
        own_part = jnp.dot(contexts[part], out_rows(0), preferred_element_type=jnp.float32)
        hidden_parts.append(resid + own_part)
    handed, hidden_parts[-1] = lax.optimization_barrier((handed, hidden_parts[-1]))
    text_block = jnp.where(
        choice[0] == 2, handed, jnp.where(choice[0] == 1, text_high, text_low)
    )
    text = Ring(text_block.reshape(FT, local_kv), rows)
    for part in range(part_count):
        for distance in range(1, tp_size):
            hidden_parts[part] = hidden_parts[part] + jnp.dot(
                arrived[part][distance - 1], out_rows(distance), preferred_element_type=jnp.float32
            )
    hidden = jnp.concatenate(hidden_parts, axis=0)
    sums = jnp.stack([jnp.sum(hidden, axis=1), jnp.sum(hidden * hidden, axis=1)])
    others = [shifted(sums, "tp", distance) for distance in range(1, tp_size)]
    sums = text.advance(sums)
    row_sum, row_squares = functools.reduce(jnp.add, others, sums)
    mean_value = row_sum / VD
    variance = row_squares / VD - mean_value * mean_value
    normed = (hidden - mean_value[:, None]) * lax.rsqrt(variance + 1e-06)[
        :, None
    ] * merge_gain + merge_bias
    normed = normed.astype(jnp.bfloat16)

    received = []
    for distance in range(1, tp_size):
        block = lax.rem(tp_index + distance, tp_size)
        part = merged_columns(normed, vis_kv_w, block, local_kv, jnp.bfloat16)
        received.append(shifted(part, "tp", distance))
    text.advance(part)
    own = merged_columns(normed, vis_kv_w, tp_index, local_kv, jnp.float32)
    own = text.advance(own)
    text_blocks = text.all()
    for part in received:
        own = own + part.astype(jnp.float32)
    vision = Ring(own.astype(jnp.bfloat16), rows)
    for hop in range(1, rows):
        if hop == 1:
            text_blocks[-1] = vision.advance(text_blocks[-1], lag=1)
        else:
            vision.advance((), lag=1)
    return attend(queries, text_blocks + vision.all(), bounds, place)


def solution(mesh):
    return jax.shard_map(
        shards,
        mesh=mesh,
        in_specs=(
            P(("dp", "ctx"), None, "tp"),
            P(("dp", "ctx"), "tp"),
            P(None, "tp"),
            P("tp"),
            P("tp"),
            P(None, "tp", None),
            P("dp"),
            P("dp"),
            P("dp"),
            P(("dp", "ctx"), "tp", None, None),
            P(("dp", "ctx"), "tp"),
        ),
        out_specs=P(("dp", "ctx"), "tp"),
        check_vma=False,
    )
```

```python
import functools
import math

import jax
import jax.numpy as jnp
from jax import lax
from jax.experimental import pallas as pl
from jax.experimental.pallas import tpu as pltpu
from jax.sharding import PartitionSpec as P

VD = 1280
VH = 16
HD = 128
H = 32
KVH = 8
FT = 128
FP = 4 * FT
GROUP = H // KVH
DOCS = 4
LANES = 128

MASKED = -1e30
VMEM_LIMIT = 16 * 1024 * 1024
MERGE_VMEM = 52 * 1024 * 1024
LANGUAGE_VMEM = 52 * 1024 * 1024


def contract_last(a, b):
    return lax.dot_general(a, b, (((1,), (1,)), ((), ())), preferred_element_type=jnp.float32)


def shifted(block, axis, distance):
    count = lax.axis_size(axis)
    return lax.ppermute(block, axis, [(i, (i + distance) % count) for i in range(count)])


def ring_place(row, rows):
    return jnp.where(row % 2 == 1, (row + 1) // 2, (rows - row // 2) % rows)


def to_next_row(block, rows):
    order = [0] + list(range(1, rows, 2)) + list(range(rows - 2, 0, -2))
    after = dict(zip(order, order[1:] + order[:1]))
    return lax.ppermute(
        block,
        "ctx",
        [(2 * row + side, 2 * after[row] + side) for row in range(rows) for side in range(2)],
    )


def to_other_side(block, rows):
    return lax.ppermute(
        block, "ctx", [(2 * row + side, 2 * row + 1 - side) for row in range(rows) for side in range(2)]
    )


class Ring:
    def __init__(self, block, rows):
        self.rows = rows
        self.blocks = [block]
        self.start(block)

    def start(self, block):
        self.moving = to_next_row(block, self.rows) if len(self.blocks) < 2 * self.rows - 1 else None
        self.blocks.append(to_other_side(block, self.rows))

    def advance(self, beside, lag=0):
        if self.moving is None:
            return beside
        if len(self.blocks) > 2 * lag:
            at = len(self.blocks) - 1 - 2 * lag
            held, self.blocks[at], beside = lax.optimization_barrier(
                (self.moving, self.blocks[at], beside)
            )
        else:
            held, beside = lax.optimization_barrier((self.moving, beside))
        self.blocks.append(held)
        self.start(held)
        return beside

    def all(self):
        while self.moving is not None:
            self.advance(())
        return self.blocks


def vit_kernel(q_ref, k_ref, v_ref, after_ref, o_ref, *, heads, dim):
    width = q_ref.shape[2]
    to_exp = 1.0 / math.sqrt(dim)
    tiles = {}
    for g in range(heads):
        first, last = g * dim, (g + 1) * dim
        low = first // LANES * LANES
        high = min(width, -(-last // LANES) * LANES)
        lane = lax.broadcasted_iota(jnp.int32, (1, high - low), 1) + low
        inside = (lane >= first) & (lane < last)
        keep = jnp.where(inside, 1.0, 0.0).astype(jnp.bfloat16)
        rest = jnp.where(inside, 0.0, 1.0).astype(jnp.bfloat16)
        scores = contract_last(q_ref[0, :, low:high] * keep, k_ref[0, :, low:high])
        row_max = jnp.max(scores, axis=1, keepdims=True)
        weights = jnp.exp((scores - row_max) * to_exp).astype(jnp.bfloat16)
        mixed = jnp.dot(
            weights, v_ref[0, :, low:high] * keep + rest, preferred_element_type=jnp.float32
        )
        spare = 0 if low < first else last - low
        mixed = mixed / mixed[:, spare : spare + 1]
        for at in range(low, high, LANES):
            end = min(at + LANES, high)
            piece = mixed[:, at - low : end - low]
            if at in tiles:
                piece = jnp.where(inside[:, at - low : end - low], piece, tiles[at])
            tiles[at] = piece
    for at, piece in tiles.items():
        o_ref[:, at : at + piece.shape[1]] = piece.astype(o_ref.dtype)


def vit_attention(fields, after, part, part_count):
    _, patches, width = fields.shape
    frames = patches // FP
    rows = FP // part_count
    dim = VD // VH
    heads = width // dim
    return pl.pallas_call(
        functools.partial(vit_kernel, heads=heads, dim=dim),
        grid=(frames,),
        in_specs=[
            pl.BlockSpec((1, rows, width), lambda f: (0, f * part_count + part, 0)),
            pl.BlockSpec((1, FP, width), lambda f: (1, f, 0)),
            pl.BlockSpec((1, FP, width), lambda f: (2, f, 0)),
            pl.BlockSpec(memory_space=pl.ANY),
        ],
        out_specs=pl.BlockSpec((rows, width), lambda f: (f, 0)),
        out_shape=jax.ShapeDtypeStruct((frames * rows, width), jnp.bfloat16),
        compiler_params=pltpu.CompilerParams(vmem_limit_bytes=VMEM_LIMIT),
        cost_estimate=pl.CostEstimate(flops=1024, bytes_accessed=1024, transcendentals=0),
    )(fields, fields, fields, after)


def merge_kernel(block_ref, x_ref, w_ref, o_ref, held_ref, rows_ref, sems, *, step):
    tokens, columns = o_ref.shape
    patches = x_ref.shape[0]
    steps = columns // step

    def weights_in(n):
        source = w_ref.at[:, :, pl.ds(pl.multiple_of(block_ref[0] * columns + n * step, step), step)]
        return pltpu.make_async_copy(source, held_ref.at[n], sems.at[n])

    for n in range(steps):
        weights_in(n).start()
    token = lax.broadcasted_iota(jnp.int32, (tokens, patches), 0)
    patch = lax.broadcasted_iota(jnp.int32, (tokens, patches), 1)
    for j in range(4):
        pick = jnp.where(patch == 4 * token + j, 1.0, 0.0).astype(jnp.bfloat16)
        rows_ref[j] = jnp.dot(pick, x_ref[...], preferred_element_type=jnp.float32).astype(
            jnp.bfloat16
        )
    for n in range(steps):
        weights_in(n).wait()
        total = jnp.zeros((tokens, step), jnp.float32)
        for j in range(4):
            total = total + jnp.dot(
                rows_ref[j], held_ref[n, j], preferred_element_type=jnp.float32
            )
        o_ref[:, n * step : (n + 1) * step] = total.astype(o_ref.dtype)


def merged_columns(normed, weights, block, columns, dtype):
    patches, width = normed.shape
    tokens = patches // 4
    step = min(columns, 256)
    steps = columns // step
    return pl.pallas_call(
        functools.partial(merge_kernel, step=step),
        in_specs=[
            pl.BlockSpec(memory_space=pltpu.SMEM),
            pl.BlockSpec(memory_space=pltpu.VMEM),
            pl.BlockSpec(memory_space=pl.ANY),
        ],
        out_specs=pl.BlockSpec(memory_space=pltpu.VMEM),
        out_shape=jax.ShapeDtypeStruct((tokens, columns), dtype),
        scratch_shapes=[
            pltpu.VMEM((steps, 4, width, step), jnp.bfloat16),
            pltpu.VMEM((4, tokens, width), jnp.bfloat16),
            pltpu.SemaphoreType.DMA((steps,)),
        ],
        compiler_params=pltpu.CompilerParams(vmem_limit_bytes=MERGE_VMEM),
        cost_estimate=pl.CostEstimate(
            flops=2 * tokens * 4 * width * columns,
            bytes_accessed=4 * width * columns * 2 + patches * width * 2,
            transcendentals=0,
        ),
    )(jnp.reshape(block, (1,)), normed, weights)


def tables_kernel(
    device_ref, vis_pos_ref, frame_host_ref, doc_ref, choice_ref, place_ref, bounds_ref,
    *, peers, per_device,
):
    device = device_ref[0]
    rows = peers // 2
    frames = vis_pos_ref.shape[0]
    slots_each = per_device // FT
    first_pos = device * per_device
    starts = [
        jnp.sum(jnp.where(doc_ref[...] < d, 1.0, 0.0)).astype(jnp.int32) for d in range(1, DOCS)
    ]
    for i, value in enumerate([first_pos] + starts):
        bounds_ref[i] = value

    def block_from(source):
        hop = lax.rem(ring_place(device // 2, rows) + rows - ring_place(source // 2, rows), rows)
        return 2 * hop + jnp.where(lax.rem(source, 2) == lax.rem(device, 2), 0, 1)

    def one_slot(slot, carry):
        frame, before_is_text, own = carry
        pos = slot * FT
        here = jnp.minimum(frame, frames - 1)
        is_frame = (frame < frames) & (vis_pos_ref[here] == pos)
        owner = slot // slots_each
        second = lax.rem(slot, slots_each) != 0
        partner = lax.rem(owner + peers // 2, peers)
        holder = jnp.where(second & (before_is_text == 1), partner, owner)
        source = jnp.where(is_frame, frame_host_ref[here], holder)
        place_ref[block_from(source) + jnp.where(is_frame, peers, 0)] = pos
        flag = jnp.where(is_frame, 1, 0)
        own = own + jnp.where(pos == first_pos, flag, 0) + jnp.where(pos == first_pos + FT, 2 * flag, 0)
        return frame + flag, 1 - flag, own

    zero = jnp.int32(0)
    _, _, own = lax.fori_loop(0, peers * slots_each, one_slot, (zero, zero, zero))
    choice_ref[0] = jnp.where(own == 3, 2, jnp.where(own == 1, 1, 0))


def tables(device, vis_pos, frame_host, doc_ids, peers, per_device):
    scalars = pl.BlockSpec(memory_space=pltpu.SMEM)
    lengths = (1, 2 * peers, DOCS)
    return pl.pallas_call(
        functools.partial(tables_kernel, peers=peers, per_device=per_device),
        in_specs=[scalars] * 3 + [pl.BlockSpec(memory_space=pltpu.VMEM)],
        out_specs=[scalars] * len(lengths),
        out_shape=[jax.ShapeDtypeStruct((length,), jnp.int32) for length in lengths],
    )(jnp.reshape(device, (1,)), vis_pos, frame_host, doc_ids.reshape(-1, LANES))


def attend_kernel(bounds_ref, place_ref, q_ref, *rest, slots, heads):
    slot_refs, out_ref = rest[:slots], rest[slots]
    kv_ref, held_q_ref, query_ref, bias_ref, score_ref, max_ref, acc_ref, result_ref = rest[
        slots + 1 : slots + 9
    ]
    slot_sems, query_sems, out_sems = rest[slots + 9 :]
    rows = q_ref.shape[0]
    scale = 1.0 / math.sqrt(HD)
    wide = GROUP * HD
    first_pos = bounds_ref[0]
    starts = [bounds_ref[i] for i in range(1, DOCS)]

    def first_key(pos):
        return functools.reduce(jnp.maximum, [jnp.where(s <= pos, s, 0) for s in starts])

    last = first_pos // rows
    first = first_key(first_pos) // rows
    whole = jnp.minimum((first_key(first_pos + rows - 1) + rows - 1) // rows, last)

    cuts = [(0, 1)] + [(1, heads)] * (heads > 1)

    def slot_copy(i, cut):
        begin, end = cuts[cut]
        lanes = slice(begin * 2 * HD, end * 2 * HD)
        there = pl.ds(pl.multiple_of(place_ref[i], FT), FT)
        return pltpu.make_async_copy(
            slot_refs[i].at[:, lanes], kv_ref.at[there, lanes], slot_sems.at[cut, i]
        )

    def query_copy(cut):
        begin, end = cuts[cut]
        lanes = slice(begin * wide, end * wide)
        return pltpu.make_async_copy(
            q_ref.at[:, lanes], held_q_ref.at[:, lanes], query_sems.at[cut]
        )

    def wanted(i):
        block = place_ref[i] // rows
        return (block >= first) & (block <= last)

    def all_slots(cut, act):
        for i in range(slots):
            pl.when(wanted(i))(functools.partial(act, i, cut))

    for cut in range(len(cuts)):
        query_copy(cut).start()
        all_slots(cut, lambda i, cut: slot_copy(i, cut).start())

    def mask(block):
        query_pos = first_pos + lax.broadcasted_iota(jnp.int32, (rows, FT), 0)
        low = first_key(query_pos)
        for at in range(0, rows, FT):
            key_pos = block * rows + at + lax.broadcasted_iota(jnp.int32, (rows, FT), 1)
            allowed = (key_pos <= query_pos) & (key_pos >= low)
            bias_ref[block, :, at : at + FT] = jnp.where(allowed, 0.0, MASKED)

    pl.loop(first, whole)(mask)
    mask(last)

    def result_copy(h):
        return pltpu.make_async_copy(
            result_ref.at[h], out_ref.at[:, h * wide : (h + 1) * wide], out_sems.at[h]
        )

    for h in range(heads):
        if h < len(cuts):
            query_copy(h).wait()
            all_slots(h, lambda i, cut: slot_copy(i, cut).wait())
        for g in range(GROUP):
            at = h * wide + g * HD
            query_ref[g * rows : (g + 1) * rows] = held_q_ref[:, at : at + HD]

        def score(block, masked, initial):
            here = pl.ds(pl.multiple_of(block * rows, rows), rows)
            keys = kv_ref[here, 2 * h * HD : (2 * h + 1) * HD]
            scores = contract_last(query_ref[...], keys) * scale
            if masked:
                scores = scores.reshape(GROUP, rows, rows) + bias_ref[block][None]
                scores = scores.reshape(GROUP * rows, rows)
            score_ref[block] = scores
            parts = [scores[:, at : at + FT] for at in range(0, rows, FT)]
            if not initial:
                parts.append(max_ref[...])
            max_ref[...] = functools.reduce(jnp.maximum, parts)

        score(last, masked=True, initial=True)
        pl.loop(first, whole)(functools.partial(score, masked=True, initial=False))
        pl.loop(whole, last)(functools.partial(score, masked=False, initial=False))
        row_max = jnp.max(max_ref[...], axis=1, keepdims=True)
        max_ref[...] = jnp.broadcast_to(row_max, max_ref.shape)

        def mix(block):
            here = pl.ds(pl.multiple_of(block * rows, rows), rows)
            values = kv_ref[here, (2 * h + 1) * HD : (2 * h + 2) * HD]
            values = jnp.concatenate([values, jnp.ones_like(values)], axis=1)
            weights = [
                jnp.exp(score_ref[block, :, at : at + FT] - max_ref[...]).astype(jnp.bfloat16)
                for at in range(0, rows, FT)
            ]
            weights = jnp.concatenate(weights, axis=1)
            return jnp.dot(weights, values, preferred_element_type=jnp.float32)

        acc_ref[...] = mix(last)

        @pl.loop(first, last)
        def _(block):
            acc_ref[...] += mix(block)

        mixed = acc_ref[:, :HD] / acc_ref[:, HD:]
        for g in range(GROUP):
            result_ref[h, :, g * HD : (g + 1) * HD] = mixed[g * rows : (g + 1) * rows].astype(
                result_ref.dtype
            )
        result_copy(h).start()
    for h in range(heads):
        result_copy(h).wait()


def attend(queries, slots, bounds, place):
    rows = queries.shape[0]
    columns = slots[0].shape[1]
    heads = columns // (2 * HD)
    blocks = len(slots) * FT // rows
    wide = GROUP * HD
    tall = GROUP * rows
    anywhere = pl.BlockSpec(memory_space=pl.ANY)
    scalars = pl.BlockSpec(memory_space=pltpu.SMEM)
    cells = heads * tall * blocks * rows
    return pl.pallas_call(
        functools.partial(attend_kernel, slots=len(slots), heads=heads),
        in_specs=[scalars] * 2 + [anywhere] * (1 + len(slots)),
        out_specs=anywhere,
        out_shape=jax.ShapeDtypeStruct(queries.shape, jnp.bfloat16),
        scratch_shapes=[
            pltpu.VMEM((len(slots) * FT, columns), jnp.bfloat16),
            pltpu.VMEM(queries.shape, jnp.bfloat16),
            pltpu.VMEM((tall, HD), jnp.bfloat16),
            pltpu.VMEM((blocks, rows, rows), jnp.float32),
            pltpu.VMEM((blocks, tall, rows), jnp.float32),
            pltpu.VMEM((tall, FT), jnp.float32),
            pltpu.VMEM((tall, 2 * HD), jnp.float32),
            pltpu.VMEM((heads, rows, wide), jnp.bfloat16),
            pltpu.SemaphoreType.DMA((2, len(slots))),
            pltpu.SemaphoreType.DMA((2,)),
            pltpu.SemaphoreType.DMA((heads,)),
        ],
        compiler_params=pltpu.CompilerParams(vmem_limit_bytes=LANGUAGE_VMEM),
        cost_estimate=pl.CostEstimate(
            flops=6 * cells * HD,
            bytes_accessed=2 * len(slots) * FT * columns + 4 * rows * heads * wide,
            transcendentals=cells,
        ),
    )(bounds, place, queries, *slots)


def shards(
    vis_qkv,
    vis_resid,
    vis_out_w,
    merge_gain,
    merge_bias,
    vis_kv_w,
    frame_host,
    vis_pos,
    doc_ids,
    text_kv,
    queries,
):
    device = lax.axis_index("ctx")
    tp_index = lax.axis_index("tp")
    tp_size = lax.axis_size("tp")
    per_device = queries.shape[0]
    patches = vis_qkv.shape[0]
    width = vis_qkv.shape[2]
    frames_dev = patches // FP
    local_kv = vis_kv_w.shape[2] // tp_size
    positions = doc_ids.shape[0]
    frames = vis_pos.shape[0]

    peers = lax.axis_size("ctx")
    rows = peers // 2
    first_pos = device * per_device

    fields = jnp.transpose(vis_qkv, (1, 0, 2))
    part_count = 2 if frames_dev == 1 else 1
    part_rows = patches // part_count
    text_low, text_high = text_kv[:FT], text_kv[FT:]
    handed = shifted(text_high, "ctx", peers // 2)
    contexts = []
    for part in range(part_count):
        after = text_high if part == 0 else contexts[-1]
        contexts.append(vit_attention(fields, after, part, part_count))
    vis_pos, _ = lax.optimization_barrier((vis_pos, contexts[-1]))
    choice, place, bounds = tables(device, vis_pos, frame_host, doc_ids, peers, per_device)
    arrived = [
        [shifted(context, "tp", distance) for distance in range(1, tp_size)]
        for context in contexts
    ]

    def out_rows(distance):
        source = lax.rem(tp_index + tp_size - distance, tp_size)
        return lax.dynamic_slice_in_dim(vis_out_w, source * width, width, axis=0)

    hidden_parts = []
    for part in range(part_count):
        resid = vis_resid[part * part_rows : (part + 1) * part_rows].astype(jnp.float32)
        own_part = jnp.dot(contexts[part], out_rows(0), preferred_element_type=jnp.float32)
        hidden_parts.append(resid + own_part)
    handed, hidden_parts[-1] = lax.optimization_barrier((handed, hidden_parts[-1]))
    text_block = jnp.where(
        choice[0] == 2, handed, jnp.where(choice[0] == 1, text_high, text_low)
    )
    text = Ring(text_block.reshape(FT, local_kv), rows)
    for part in range(part_count):
        for distance in range(1, tp_size):
            hidden_parts[part] = hidden_parts[part] + jnp.dot(
                arrived[part][distance - 1], out_rows(distance), preferred_element_type=jnp.float32
            )
    hidden = jnp.concatenate(hidden_parts, axis=0)
    sums = jnp.stack([jnp.sum(hidden, axis=1), jnp.sum(hidden * hidden, axis=1)])
    others = [shifted(sums, "tp", distance) for distance in range(1, tp_size)]
    sums = text.advance(sums)
    row_sum, row_squares = functools.reduce(jnp.add, others, sums)
    mean_value = row_sum / VD
    variance = row_squares / VD - mean_value * mean_value
    normed = (hidden - mean_value[:, None]) * lax.rsqrt(variance + 1e-06)[
        :, None
    ] * merge_gain + merge_bias
    normed = normed.astype(jnp.bfloat16)

    received = []
    for distance in range(1, tp_size):
        block = lax.rem(tp_index + distance, tp_size)
        part = merged_columns(normed, vis_kv_w, block, local_kv, jnp.bfloat16)
        received.append(shifted(part, "tp", distance))
    text.advance(part)
    own = merged_columns(normed, vis_kv_w, tp_index, local_kv, jnp.float32)
    own = text.advance(own)
    text_blocks = text.all()
    for part in received:
        own = own + part.astype(jnp.float32)
    vision = Ring(own.astype(jnp.bfloat16), rows)
    for hop in range(1, rows):
        if hop == 1:
            text_blocks[-1] = vision.advance(text_blocks[-1], lag=1)
        else:
            vision.advance((), lag=1)
    return attend(queries, text_blocks + vision.all(), bounds, place)


def solution(mesh):
    return jax.shard_map(
        shards,
        mesh=mesh,
        in_specs=(
            P(("dp", "ctx"), None, "tp"),
            P(("dp", "ctx"), "tp"),
            P(None, "tp"),
            P("tp"),
            P("tp"),
            P(None, "tp", None),
            P("dp"),
            P("dp"),
            P("dp"),
            P(("dp", "ctx"), "tp", None, None),
            P(("dp", "ctx"), "tp"),
        ),
        out_specs=P(("dp", "ctx"), "tp"),
        check_vma=False,
    )
```

```python
import functools
import math

import jax
import jax.numpy as jnp
from jax import lax
from jax.experimental import pallas as pl
from jax.experimental.pallas import tpu as pltpu
from jax.sharding import PartitionSpec as P

VD = 1280
VH = 16
HD = 128
H = 32
KVH = 8
FT = 128
FP = 4 * FT
GROUP = H // KVH
DOCS = 4
LANES = 128

MASKED = -1e30
VMEM_LIMIT = 16 * 1024 * 1024
MERGE_VMEM = 52 * 1024 * 1024
LANGUAGE_VMEM = 52 * 1024 * 1024


def contract_last(a, b):
    return lax.dot_general(a, b, (((1,), (1,)), ((), ())), preferred_element_type=jnp.float32)


def shifted(block, axis, distance):
    count = lax.axis_size(axis)
    return lax.ppermute(block, axis, [(i, (i + distance) % count) for i in range(count)])


def ring_place(row, rows):
    return jnp.where(row % 2 == 1, (row + 1) // 2, (rows - row // 2) % rows)


def to_next_row(block, rows):
    order = [0] + list(range(1, rows, 2)) + list(range(rows - 2, 0, -2))
    after = dict(zip(order, order[1:] + order[:1]))
    return lax.ppermute(
        block,
        "ctx",
        [(2 * row + side, 2 * after[row] + side) for row in range(rows) for side in range(2)],
    )


def to_other_side(block, rows):
    return lax.ppermute(
        block, "ctx", [(2 * row + side, 2 * row + 1 - side) for row in range(rows) for side in range(2)]
    )


class Ring:
    def __init__(self, block, rows):
        self.rows = rows
        self.blocks = [block]
        self.start(block)

    def start(self, block):
        self.moving = to_next_row(block, self.rows) if len(self.blocks) < 2 * self.rows - 1 else None
        self.blocks.append(to_other_side(block, self.rows))

    def advance(self, beside, lag=0):
        if self.moving is None:
            return beside
        if len(self.blocks) > 2 * lag:
            at = len(self.blocks) - 1 - 2 * lag
            held, self.blocks[at], beside = lax.optimization_barrier(
                (self.moving, self.blocks[at], beside)
            )
        else:
            held, beside = lax.optimization_barrier((self.moving, beside))
        self.blocks.append(held)
        self.start(held)
        return beside

    def all(self):
        while self.moving is not None:
            self.advance(())
        return self.blocks


def vit_kernel(q_ref, k_ref, v_ref, after_ref, o_ref, *, heads, dim):
    width = q_ref.shape[2]
    to_exp = 1.0 / math.sqrt(dim)
    tiles = {}
    for g in range(heads):
        first, last = g * dim, (g + 1) * dim
        low = first // LANES * LANES
        high = min(width, -(-last // LANES) * LANES)
        lane = lax.broadcasted_iota(jnp.int32, (1, high - low), 1) + low
        inside = (lane >= first) & (lane < last)
        keep = jnp.where(inside, 1.0, 0.0).astype(jnp.bfloat16)
        rest = jnp.where(inside, 0.0, 1.0).astype(jnp.bfloat16)
        scores = contract_last(q_ref[0, :, low:high] * keep, k_ref[0, :, low:high])
        row_max = jnp.max(scores, axis=1, keepdims=True)
        weights = jnp.exp((scores - row_max) * to_exp).astype(jnp.bfloat16)
        mixed = jnp.dot(
            weights, v_ref[0, :, low:high] * keep + rest, preferred_element_type=jnp.float32
        )
        spare = 0 if low < first else last - low
        mixed = mixed / mixed[:, spare : spare + 1]
        for at in range(low, high, LANES):
            end = min(at + LANES, high)
            piece = mixed[:, at - low : end - low]
            if at in tiles:
                piece = jnp.where(inside[:, at - low : end - low], piece, tiles[at])
            tiles[at] = piece
    for at, piece in tiles.items():
        o_ref[:, at : at + piece.shape[1]] = piece.astype(o_ref.dtype)


def vit_attention(fields, after, part, part_count):
    _, patches, width = fields.shape
    frames = patches // FP
    rows = FP // part_count
    dim = VD // VH
    heads = width // dim
    return pl.pallas_call(
        functools.partial(vit_kernel, heads=heads, dim=dim),
        grid=(frames,),
        in_specs=[
            pl.BlockSpec((1, rows, width), lambda f: (0, f * part_count + part, 0)),
            pl.BlockSpec((1, FP, width), lambda f: (1, f, 0)),
            pl.BlockSpec((1, FP, width), lambda f: (2, f, 0)),
            pl.BlockSpec(memory_space=pl.ANY),
        ],
        out_specs=pl.BlockSpec((rows, width), lambda f: (f, 0)),
        out_shape=jax.ShapeDtypeStruct((frames * rows, width), jnp.bfloat16),
        compiler_params=pltpu.CompilerParams(vmem_limit_bytes=VMEM_LIMIT),
        cost_estimate=pl.CostEstimate(flops=1024, bytes_accessed=1024, transcendentals=0),
    )(fields, fields, fields, after)


def merge_kernel(block_ref, x_ref, w_ref, o_ref, held_ref, rows_ref, sems, *, step):
    tokens, columns = o_ref.shape
    patches = x_ref.shape[0]
    steps = columns // step

    def weights_in(n):
        source = w_ref.at[:, :, pl.ds(pl.multiple_of(block_ref[0] * columns + n * step, step), step)]
        return pltpu.make_async_copy(source, held_ref.at[n], sems.at[n])

    for n in range(steps):
        weights_in(n).start()
    token = lax.broadcasted_iota(jnp.int32, (tokens, patches), 0)
    patch = lax.broadcasted_iota(jnp.int32, (tokens, patches), 1)
    for j in range(4):
        pick = jnp.where(patch == 4 * token + j, 1.0, 0.0).astype(jnp.bfloat16)
        rows_ref[j] = jnp.dot(pick, x_ref[...], preferred_element_type=jnp.float32).astype(
            jnp.bfloat16
        )
    for n in range(steps):
        weights_in(n).wait()
        total = jnp.zeros((tokens, step), jnp.float32)
        for j in range(4):
            total = total + jnp.dot(
                rows_ref[j], held_ref[n, j], preferred_element_type=jnp.float32
            )
        o_ref[:, n * step : (n + 1) * step] = total.astype(o_ref.dtype)


def merged_columns(normed, weights, block, columns, dtype):
    patches, width = normed.shape
    tokens = patches // 4
    step = min(columns, 256)
    steps = columns // step
    return pl.pallas_call(
        functools.partial(merge_kernel, step=step),
        in_specs=[
            pl.BlockSpec(memory_space=pltpu.SMEM),
            pl.BlockSpec(memory_space=pltpu.VMEM),
            pl.BlockSpec(memory_space=pl.ANY),
        ],
        out_specs=pl.BlockSpec(memory_space=pltpu.VMEM),
        out_shape=jax.ShapeDtypeStruct((tokens, columns), dtype),
        scratch_shapes=[
            pltpu.VMEM((steps, 4, width, step), jnp.bfloat16),
            pltpu.VMEM((4, tokens, width), jnp.bfloat16),
            pltpu.SemaphoreType.DMA((steps,)),
        ],
        compiler_params=pltpu.CompilerParams(vmem_limit_bytes=MERGE_VMEM),
        cost_estimate=pl.CostEstimate(
            flops=2 * tokens * 4 * width * columns,
            bytes_accessed=4 * width * columns * 2 + patches * width * 2,
            transcendentals=0,
        ),
    )(jnp.reshape(block, (1,)), normed, weights)


def tables_kernel(
    device_ref, vis_pos_ref, frame_host_ref, doc_ref, place_ref, bounds_ref,
    *, peers, per_device,
):
    device = device_ref[0]
    rows = peers // 2
    frames = vis_pos_ref.shape[0]
    slots_each = per_device // FT
    first_pos = device * per_device
    starts = [
        jnp.sum(jnp.where(doc_ref[...] < d, 1.0, 0.0)).astype(jnp.int32) for d in range(1, DOCS)
    ]
    for i, value in enumerate([first_pos] + starts):
        bounds_ref[i] = value

    def block_from(source):
        hop = lax.rem(ring_place(device // 2, rows) + rows - ring_place(source // 2, rows), rows)
        return 2 * hop + jnp.where(lax.rem(source, 2) == lax.rem(device, 2), 0, 1)

    def one_slot(slot, carry):
        frame, before_is_text = carry
        pos = slot * FT
        here = jnp.minimum(frame, frames - 1)
        is_frame = (frame < frames) & (vis_pos_ref[here] == pos)
        owner = slot // slots_each
        second = lax.rem(slot, slots_each) != 0
        partner = lax.rem(owner + peers // 2, peers)
        holder = jnp.where(second & (before_is_text == 1), partner, owner)
        source = jnp.where(is_frame, frame_host_ref[here], holder)
        flag = jnp.where(is_frame, 1, 0)
        place_ref[block_from(source) + peers * flag] = pos
        return frame + flag, 1 - flag

    lax.fori_loop(0, peers * slots_each, one_slot, (jnp.int32(0), jnp.int32(0)))


def tables(device, vis_pos, frame_host, doc_ids, peers, per_device):
    scalars = pl.BlockSpec(memory_space=pltpu.SMEM)
    lengths = (2 * peers, DOCS)
    return pl.pallas_call(
        functools.partial(tables_kernel, peers=peers, per_device=per_device),
        in_specs=[scalars] * 3 + [pl.BlockSpec(memory_space=pltpu.VMEM)],
        out_specs=[scalars] * len(lengths),
        out_shape=[jax.ShapeDtypeStruct((length,), jnp.int32) for length in lengths],
    )(jnp.reshape(device, (1,)), vis_pos, frame_host, doc_ids.reshape(-1, LANES))


def attend_kernel(bounds_ref, place_ref, q_ref, *rest, slots, heads):
    slot_refs, out_ref = rest[:slots], rest[slots]
    kv_ref, held_q_ref, query_ref, bias_ref, score_ref, max_ref, acc_ref, result_ref = rest[
        slots + 1 : slots + 9
    ]
    slot_sems, query_sems, out_sems = rest[slots + 9 :]
    rows = q_ref.shape[0]
    scale = 1.0 / math.sqrt(HD)
    wide = GROUP * HD
    first_pos = bounds_ref[0]
    starts = [bounds_ref[i] for i in range(1, DOCS)]

    def first_key(pos):
        return functools.reduce(jnp.maximum, [jnp.where(s <= pos, s, 0) for s in starts])

    last = first_pos // rows
    first = first_key(first_pos) // rows
    whole = jnp.minimum((first_key(first_pos + rows - 1) + rows - 1) // rows, last)

    cuts = [(0, 1)] + [(1, heads)] * (heads > 1)

    def slot_copy(i, cut):
        begin, end = cuts[cut]
        lanes = slice(begin * 2 * HD, end * 2 * HD)
        there = pl.ds(pl.multiple_of(place_ref[i], FT), FT)
        return pltpu.make_async_copy(
            slot_refs[i].at[:, lanes], kv_ref.at[there, lanes], slot_sems.at[cut, i]
        )

    def query_copy(cut):
        begin, end = cuts[cut]
        lanes = slice(begin * wide, end * wide)
        return pltpu.make_async_copy(
            q_ref.at[:, lanes], held_q_ref.at[:, lanes], query_sems.at[cut]
        )

    def wanted(i):
        block = place_ref[i] // rows
        return (block >= first) & (block <= last)

    def all_slots(cut, act):
        for i in range(slots):
            pl.when(wanted(i))(functools.partial(act, i, cut))

    for cut in range(len(cuts)):
        query_copy(cut).start()
        all_slots(cut, lambda i, cut: slot_copy(i, cut).start())

    def mask(block):
        query_pos = first_pos + lax.broadcasted_iota(jnp.int32, (rows, FT), 0)
        low = first_key(query_pos)
        for at in range(0, rows, FT):
            key_pos = block * rows + at + lax.broadcasted_iota(jnp.int32, (rows, FT), 1)
            allowed = (key_pos <= query_pos) & (key_pos >= low)
            bias_ref[block, :, at : at + FT] = jnp.where(allowed, 0.0, MASKED)

    pl.loop(first, whole)(mask)
    mask(last)

    def result_copy(h):
        return pltpu.make_async_copy(
            result_ref.at[h], out_ref.at[:, h * wide : (h + 1) * wide], out_sems.at[h]
        )

    for h in range(heads):
        if h < len(cuts):
            query_copy(h).wait()
            all_slots(h, lambda i, cut: slot_copy(i, cut).wait())
        for g in range(GROUP):
            at = h * wide + g * HD
            query_ref[g * rows : (g + 1) * rows] = held_q_ref[:, at : at + HD]

        def score(block, masked, initial):
            here = pl.ds(pl.multiple_of(block * rows, rows), rows)
            keys = kv_ref[here, 2 * h * HD : (2 * h + 1) * HD]
            scores = contract_last(query_ref[...], keys) * scale
            if masked:
                scores = scores.reshape(GROUP, rows, rows) + bias_ref[block][None]
                scores = scores.reshape(GROUP * rows, rows)
            score_ref[block] = scores
            parts = [scores[:, at : at + FT] for at in range(0, rows, FT)]
            if not initial:
                parts.append(max_ref[...])
            max_ref[...] = functools.reduce(jnp.maximum, parts)

        score(last, masked=True, initial=True)
        pl.loop(first, whole)(functools.partial(score, masked=True, initial=False))
        pl.loop(whole, last)(functools.partial(score, masked=False, initial=False))
        row_max = jnp.max(max_ref[...], axis=1, keepdims=True)
        max_ref[...] = jnp.broadcast_to(row_max, max_ref.shape)

        def mix(block):
            here = pl.ds(pl.multiple_of(block * rows, rows), rows)
            values = kv_ref[here, (2 * h + 1) * HD : (2 * h + 2) * HD]
            values = jnp.concatenate([values, jnp.ones_like(values)], axis=1)
            weights = [
                jnp.exp(score_ref[block, :, at : at + FT] - max_ref[...]).astype(jnp.bfloat16)
                for at in range(0, rows, FT)
            ]
            weights = jnp.concatenate(weights, axis=1)
            return jnp.dot(weights, values, preferred_element_type=jnp.float32)

        acc_ref[...] = mix(last)

        @pl.loop(first, last)
        def _(block):
            acc_ref[...] += mix(block)

        mixed = acc_ref[:, :HD] / acc_ref[:, HD:]
        for g in range(GROUP):
            result_ref[h, :, g * HD : (g + 1) * HD] = mixed[g * rows : (g + 1) * rows].astype(
                result_ref.dtype
            )
        result_copy(h).start()
    for h in range(heads):
        result_copy(h).wait()


def attend(queries, slots, bounds, place):
    rows = queries.shape[0]
    columns = slots[0].shape[1]
    heads = columns // (2 * HD)
    blocks = len(slots) * FT // rows
    wide = GROUP * HD
    tall = GROUP * rows
    anywhere = pl.BlockSpec(memory_space=pl.ANY)
    scalars = pl.BlockSpec(memory_space=pltpu.SMEM)
    cells = heads * tall * blocks * rows
    return pl.pallas_call(
        functools.partial(attend_kernel, slots=len(slots), heads=heads),
        in_specs=[scalars] * 2 + [anywhere] * (1 + len(slots)),
        out_specs=anywhere,
        out_shape=jax.ShapeDtypeStruct(queries.shape, jnp.bfloat16),
        scratch_shapes=[
            pltpu.VMEM((len(slots) * FT, columns), jnp.bfloat16),
            pltpu.VMEM(queries.shape, jnp.bfloat16),
            pltpu.VMEM((tall, HD), jnp.bfloat16),
            pltpu.VMEM((blocks, rows, rows), jnp.float32),
            pltpu.VMEM((blocks, tall, rows), jnp.float32),
            pltpu.VMEM((tall, FT), jnp.float32),
            pltpu.VMEM((tall, 2 * HD), jnp.float32),
            pltpu.VMEM((heads, rows, wide), jnp.bfloat16),
            pltpu.SemaphoreType.DMA((2, len(slots))),
            pltpu.SemaphoreType.DMA((2,)),
            pltpu.SemaphoreType.DMA((heads,)),
        ],
        compiler_params=pltpu.CompilerParams(vmem_limit_bytes=LANGUAGE_VMEM),
        cost_estimate=pl.CostEstimate(
            flops=6 * cells * HD,
            bytes_accessed=2 * len(slots) * FT * columns + 4 * rows * heads * wide,
            transcendentals=cells,
        ),
    )(bounds, place, queries, *slots)


def shards(
    vis_qkv,
    vis_resid,
    vis_out_w,
    merge_gain,
    merge_bias,
    vis_kv_w,
    frame_host,
    vis_pos,
    doc_ids,
    text_kv,
    queries,
):
    device = lax.axis_index("ctx")
    tp_index = lax.axis_index("tp")
    tp_size = lax.axis_size("tp")
    per_device = queries.shape[0]
    patches = vis_qkv.shape[0]
    width = vis_qkv.shape[2]
    frames_dev = patches // FP
    local_kv = vis_kv_w.shape[2] // tp_size
    positions = doc_ids.shape[0]
    frames = vis_pos.shape[0]

    peers = lax.axis_size("ctx")
    rows = peers // 2
    first_pos = device * per_device

    fields = jnp.transpose(vis_qkv, (1, 0, 2))
    part_count = 2 if frames_dev == 1 else 1
    part_rows = patches // part_count
    text_low, text_high = text_kv[:FT], text_kv[FT:]
    handed = shifted(text_high, "ctx", peers // 2)
    contexts = []
    for part in range(part_count):
        after = text_high if part == 0 else contexts[-1]
        contexts.append(vit_attention(fields, after, part, part_count))
    arrived = [
        [shifted(context, "tp", distance) for distance in range(1, tp_size)]
        for context in contexts
    ]

    def out_rows(distance):
        source = lax.rem(tp_index + tp_size - distance, tp_size)
        return lax.dynamic_slice_in_dim(vis_out_w, source * width, width, axis=0)

    hidden_parts = []
    for part in range(part_count):
        resid = vis_resid[part * part_rows : (part + 1) * part_rows].astype(jnp.float32)
        own_part = jnp.dot(contexts[part], out_rows(0), preferred_element_type=jnp.float32)
        hidden_parts.append(resid + own_part)
    handed, hidden_parts[-1] = lax.optimization_barrier((handed, hidden_parts[-1]))
    first_frame = jnp.any(vis_pos == first_pos)
    second_frame = jnp.any(vis_pos == first_pos + FT)
    text_block = jnp.where(first_frame, jnp.where(second_frame, handed, text_high), text_low)
    text = Ring(text_block.reshape(FT, local_kv), rows)
    for part in range(part_count):
        for distance in range(1, tp_size):
            hidden_parts[part] = hidden_parts[part] + jnp.dot(
                arrived[part][distance - 1], out_rows(distance), preferred_element_type=jnp.float32
            )
        hidden_parts = lax.optimization_barrier(hidden_parts)
    hidden = jnp.concatenate(hidden_parts, axis=0)
    sums = jnp.stack([jnp.sum(hidden, axis=1), jnp.sum(hidden * hidden, axis=1)])
    others = [shifted(sums, "tp", distance) for distance in range(1, tp_size)]
    sums = text.advance(sums)
    row_sum, row_squares = functools.reduce(jnp.add, others, sums)
    mean_value = row_sum / VD
    variance = row_squares / VD - mean_value * mean_value
    normed = (hidden - mean_value[:, None]) * lax.rsqrt(variance + 1e-06)[
        :, None
    ] * merge_gain + merge_bias
    normed = normed.astype(jnp.bfloat16)

    received = []
    for distance in range(1, tp_size):
        block = lax.rem(tp_index + distance, tp_size)
        part = merged_columns(normed, vis_kv_w, block, local_kv, jnp.bfloat16)
        received.append(shifted(part, "tp", distance))
    own = merged_columns(normed, vis_kv_w, tp_index, local_kv, jnp.float32)
    own = text.advance(own)
    for part in received:
        own = own + part.astype(jnp.float32)
    own = own.astype(jnp.bfloat16)
    vision = Ring(own, rows)
    vis_pos, own = lax.optimization_barrier((vis_pos, own))
    place, bounds = tables(device, vis_pos, frame_host, doc_ids, peers, per_device)
    for hop in range(1, rows):
        if hop == 1:
            vision.moving = text.advance(vision.moving)
        place, bounds = vision.advance((place, bounds), lag=1)
    return attend(queries, text.all() + vision.all(), bounds, place)


def solution(mesh):
    return jax.shard_map(
        shards,
        mesh=mesh,
        in_specs=(
            P(("dp", "ctx"), None, "tp"),
            P(("dp", "ctx"), "tp"),
            P(None, "tp"),
            P("tp"),
            P("tp"),
            P(None, "tp", None),
            P("dp"),
            P("dp"),
            P("dp"),
            P(("dp", "ctx"), "tp", None, None),
            P(("dp", "ctx"), "tp"),
        ),
        out_specs=P(("dp", "ctx"), "tp"),
        check_vma=False,
    )
```

```python
import functools
import math

import jax
import jax.numpy as jnp
from jax import lax
from jax.experimental import pallas as pl
from jax.experimental.pallas import tpu as pltpu
from jax.sharding import PartitionSpec as P

VD = 1280
VH = 16
HD = 128
H = 32
KVH = 8
FT = 128
GROUP = H // KVH
DOCS = 4
LANES = 128

MASKED = -1e30
VMEM_LIMIT = 16 * 1024 * 1024
MERGE_VMEM = 52 * 1024 * 1024
LANGUAGE_VMEM = 52 * 1024 * 1024


def contract_last(a, b):
    return lax.dot_general(a, b, (((1,), (1,)), ((), ())), preferred_element_type=jnp.float32)


def shifted(block, axis, distance):
    count = lax.axis_size(axis)
    return lax.ppermute(block, axis, [(i, (i + distance) % count) for i in range(count)])


def ring_place(row, rows):
    return jnp.where(row % 2 == 1, (row + 1) // 2, (rows - row // 2) % rows)


def to_next_row(block, rows):
    order = [0] + list(range(1, rows, 2)) + list(range(rows - 2, 0, -2))
    after = dict(zip(order, order[1:] + order[:1]))
    return lax.ppermute(
        block,
        "ctx",
        [(2 * row + side, 2 * after[row] + side) for row in range(rows) for side in range(2)],
    )


def to_other_side(block, rows):
    return lax.ppermute(
        block, "ctx", [(2 * row + side, 2 * row + 1 - side) for row in range(rows) for side in range(2)]
    )


class Ring:
    def __init__(self, block, rows):
        self.rows = rows
        self.blocks = [block]
        self.start(block)

    def start(self, block):
        self.moving = to_next_row(block, self.rows) if len(self.blocks) < 2 * self.rows - 1 else None
        self.blocks.append(to_other_side(block, self.rows))

    def advance(self, beside, lag=0):
        if self.moving is None:
            return beside
        if len(self.blocks) > 2 * lag:
            at = len(self.blocks) - 1 - 2 * lag
            held, self.blocks[at], beside = lax.optimization_barrier(
                (self.moving, self.blocks[at], beside)
            )
        else:
            held, beside = lax.optimization_barrier((self.moving, beside))
        self.blocks.append(held)
        self.start(held)
        return beside

    def all(self):
        while self.moving is not None:
            self.advance(())
        return self.blocks


def vit_kernel(index_ref, q_ref, k_ref, v_ref, after_ref, *rest, heads, dim):
    o_ref = rest[0]
    if len(rest) > 1:
        earlier_ref, weight_ref, resid_ref, o_ref, low_ref, high_ref = rest
    width = q_ref.shape[2]
    to_exp = 1.0 / math.sqrt(dim)
    tiles = {}
    for g in range(heads):
        first, last = g * dim, (g + 1) * dim
        low = first // LANES * LANES
        high = min(width, -(-last // LANES) * LANES)
        lane = lax.broadcasted_iota(jnp.int32, (1, high - low), 1) + low
        inside = (lane >= first) & (lane < last)
        keep = jnp.where(inside, 1.0, 0.0).astype(jnp.bfloat16)
        other = jnp.where(inside, 0.0, 1.0).astype(jnp.bfloat16)
        scores = contract_last(q_ref[0, :, low:high] * keep, k_ref[0, :, low:high])
        row_max = jnp.max(scores, axis=1, keepdims=True)
        weights = jnp.exp((scores - row_max) * to_exp).astype(jnp.bfloat16)
        mixed = jnp.dot(
            weights, v_ref[0, :, low:high] * keep + other, preferred_element_type=jnp.float32
        )
        spare = 0 if low < first else last - low
        mixed = mixed / mixed[:, spare : spare + 1]
        for at in range(low, high, LANES):
            end = min(at + LANES, high)
            piece = mixed[:, at - low : end - low]
            if at in tiles:
                piece = jnp.where(inside[:, at - low : end - low], piece, tiles[at])
            tiles[at] = piece
    for at, piece in tiles.items():
        o_ref[:, at : at + piece.shape[1]] = piece.astype(o_ref.dtype)
    if len(rest) > 1:
        rows = o_ref.shape[0]
        for part, (context, hidden_ref) in enumerate([(earlier_ref, low_ref), (o_ref, high_ref)]):
            here = slice(part * rows, (part + 1) * rows)
            hidden_ref[...] = resid_ref[here].astype(jnp.float32) + jnp.dot(
                context[...], weight_ref[...], preferred_element_type=jnp.float32
            )


def vit_attention(fields, after, part, tp_index, projection=None):
    _, patches, width = fields.shape
    rows = patches // 2
    dim = VD // VH
    one = pl.BlockSpec((rows, width), lambda f, _: (0, 0))
    in_specs = [
        pl.BlockSpec((1, rows, width), lambda f, _: (0, part, 0)),
        pl.BlockSpec((1, patches, width), lambda f, _: (1, 0, 0)),
        pl.BlockSpec((1, patches, width), lambda f, _: (2, 0, 0)),
        pl.BlockSpec(memory_space=pl.ANY),
    ]
    out_specs = [one]
    out_shape = [jax.ShapeDtypeStruct((rows, width), jnp.bfloat16)]
    if projection:
        in_specs += [
            one,
            pl.BlockSpec((width, width), lambda f, index: (index[0], 0)),
            pl.BlockSpec((patches, width), lambda f, _: (0, 0)),
        ]
        out_specs += [one, one]
        out_shape += [jax.ShapeDtypeStruct((rows, width), jnp.float32)] * 2
    return pl.pallas_call(
        functools.partial(vit_kernel, heads=width // dim, dim=dim),
        grid_spec=pltpu.PrefetchScalarGridSpec(
            num_scalar_prefetch=1, grid=(1,), in_specs=in_specs, out_specs=out_specs
        ),
        out_shape=out_shape,
        compiler_params=pltpu.CompilerParams(
            vmem_limit_bytes=VMEM_LIMIT
        ),
        cost_estimate=pl.CostEstimate(flops=1024, bytes_accessed=1024, transcendentals=0),
    )(jnp.reshape(tp_index, (1,)), fields, fields, fields, after, *(projection or ()))


def merge_kernel(block_ref, x_ref, w_ref, o_ref, held_ref, rows_ref, sems, *, step):
    tokens, columns = o_ref.shape
    patches = x_ref.shape[0]
    steps = columns // step

    def weights_in(n):
        source = w_ref.at[:, :, pl.ds(pl.multiple_of(block_ref[0] * columns + n * step, step), step)]
        return pltpu.make_async_copy(source, held_ref.at[n], sems.at[n])

    for n in range(steps):
        weights_in(n).start()
    token = lax.broadcasted_iota(jnp.int32, (tokens, patches), 0)
    patch = lax.broadcasted_iota(jnp.int32, (tokens, patches), 1)
    for j in range(4):
        pick = jnp.where(patch == 4 * token + j, 1.0, 0.0).astype(jnp.bfloat16)
        rows_ref[j] = jnp.dot(pick, x_ref[...], preferred_element_type=jnp.float32).astype(
            jnp.bfloat16
        )
    for n in range(steps):
        weights_in(n).wait()
        total = jnp.zeros((tokens, step), jnp.float32)
        for j in range(4):
            total = total + jnp.dot(
                rows_ref[j], held_ref[n, j], preferred_element_type=jnp.float32
            )
        o_ref[:, n * step : (n + 1) * step] = total.astype(o_ref.dtype)


def merged_columns(normed, weights, block, columns, dtype):
    patches, width = normed.shape
    tokens = patches // 4
    step = min(columns, 256)
    steps = columns // step
    return pl.pallas_call(
        functools.partial(merge_kernel, step=step),
        in_specs=[
            pl.BlockSpec(memory_space=pltpu.SMEM),
            pl.BlockSpec(memory_space=pltpu.VMEM),
            pl.BlockSpec(memory_space=pl.ANY),
        ],
        out_specs=pl.BlockSpec(memory_space=pltpu.VMEM),
        out_shape=jax.ShapeDtypeStruct((tokens, columns), dtype),
        scratch_shapes=[
            pltpu.VMEM((steps, 4, width, step), jnp.bfloat16),
            pltpu.VMEM((4, tokens, width), jnp.bfloat16),
            pltpu.SemaphoreType.DMA((steps,)),
        ],
        compiler_params=pltpu.CompilerParams(vmem_limit_bytes=MERGE_VMEM),
        cost_estimate=pl.CostEstimate(
            flops=2 * tokens * 4 * width * columns,
            bytes_accessed=4 * width * columns * 2 + patches * width * 2,
            transcendentals=0,
        ),
    )(jnp.reshape(block, (1,)), normed, weights)


def tables_kernel(
    device_ref, vis_pos_ref, frame_host_ref, doc_ref, place_ref, *, peers, per_device,
):
    device = device_ref[0]
    rows = peers // 2
    frames = vis_pos_ref.shape[0]
    slots_each = per_device // FT
    first_pos = device * per_device
    starts = [
        jnp.sum(jnp.where(doc_ref[...] < d, 1.0, 0.0)).astype(jnp.int32) for d in range(1, DOCS)
    ]
    for i, value in enumerate([first_pos] + starts):
        place_ref[2 * peers + i] = value

    def block_from(source):
        hop = lax.rem(ring_place(device // 2, rows) + rows - ring_place(source // 2, rows), rows)
        return 2 * hop + jnp.where(lax.rem(source, 2) == lax.rem(device, 2), 0, 1)

    def one_slot(slot, carry):
        frame, before_is_text = carry
        pos = slot * FT
        here = jnp.minimum(frame, frames - 1)
        is_frame = (frame < frames) & (vis_pos_ref[here] == pos)
        owner = slot // slots_each
        second = lax.rem(slot, slots_each) != 0
        partner = lax.rem(owner + peers // 2, peers)
        holder = jnp.where(second & (before_is_text == 1), partner, owner)
        source = jnp.where(is_frame, frame_host_ref[here], holder)
        flag = jnp.where(is_frame, 1, 0)
        place_ref[block_from(source) + peers * flag] = pos
        return frame + flag, 1 - flag

    lax.fori_loop(0, peers * slots_each, one_slot, (jnp.int32(0), jnp.int32(0)))


def tables(device, vis_pos, frame_host, doc_ids, peers, per_device):
    scalars = pl.BlockSpec(memory_space=pltpu.SMEM)
    return pl.pallas_call(
        functools.partial(tables_kernel, peers=peers, per_device=per_device),
        in_specs=[scalars] * 3 + [pl.BlockSpec(memory_space=pltpu.VMEM)],
        out_specs=scalars,
        out_shape=jax.ShapeDtypeStruct((2 * peers + DOCS,), jnp.int32),
    )(jnp.reshape(device, (1,)), vis_pos, frame_host, doc_ids.reshape(-1, LANES))


def attend_kernel(place_ref, q_ref, *rest, slots, heads):
    slot_refs, out_ref = rest[:slots], rest[slots]
    kv_ref, held_q_ref, query_ref, bias_ref, score_ref, max_ref, acc_ref, result_ref = rest[
        slots + 1 : slots + 9
    ]
    slot_sems, query_sems, out_sems = rest[slots + 9 :]
    rows = q_ref.shape[0]
    scale = 1.0 / math.sqrt(HD)
    wide = GROUP * HD
    first_pos = place_ref[slots]
    starts = [place_ref[slots + i] for i in range(1, DOCS)]

    def first_key(pos):
        return functools.reduce(jnp.maximum, [jnp.where(s <= pos, s, 0) for s in starts])

    last = first_pos // rows
    first = first_key(first_pos) // rows
    paired = first + (last - first) % 2
    masked_pairs = (jnp.maximum(first_key(first_pos + rows - 1) - paired * rows, 0) + 2 * rows - 1) // (
        2 * rows
    )
    pairs = (last - paired) // 2
    masked_pairs = jnp.minimum(masked_pairs, pairs)

    cuts = [(0, 1)] + [(1, heads)] * (heads > 1)

    def slot_copy(i, cut):
        begin, end = cuts[cut]
        lanes = slice(begin * 2 * HD, end * 2 * HD)
        there = pl.ds(pl.multiple_of(place_ref[i], FT), FT)
        return pltpu.make_async_copy(
            slot_refs[i].at[:, lanes], kv_ref.at[there, lanes], slot_sems.at[cut, i]
        )

    def query_copy(cut):
        begin, end = cuts[cut]
        lanes = slice(begin * wide, end * wide)
        return pltpu.make_async_copy(
            q_ref.at[:, lanes], held_q_ref.at[:, lanes], query_sems.at[cut]
        )

    def wanted(i):
        block = place_ref[i] // rows
        return (block >= first) & (block <= last)

    def all_slots(cut, act):
        for i in range(slots):
            pl.when(wanted(i))(functools.partial(act, i, cut))

    for cut in range(len(cuts)):
        query_copy(cut).start()
        all_slots(cut, lambda i, cut: slot_copy(i, cut).start())

    def mask(block):
        query_pos = first_pos + lax.broadcasted_iota(jnp.int32, (rows, FT), 0)
        low = first_key(query_pos)
        for at in range(0, rows, FT):
            key_pos = block * rows + at + lax.broadcasted_iota(jnp.int32, (rows, FT), 1)
            allowed = (key_pos <= query_pos) & (key_pos >= low)
            bias_ref[block, :, at : at + FT] = jnp.where(allowed, 0.0, MASKED)

    pl.loop(first, paired + 2 * masked_pairs)(mask)
    mask(last)

    def result_copy(h):
        return pltpu.make_async_copy(
            result_ref.at[h], out_ref.at[:, h * wide : (h + 1) * wide], out_sems.at[h]
        )

    for h in range(heads):
        if h < len(cuts):
            query_copy(h).wait()
            all_slots(h, lambda i, cut: slot_copy(i, cut).wait())
        for g in range(GROUP):
            at = h * wide + g * HD
            query_ref[g * rows : (g + 1) * rows] = held_q_ref[:, at : at + HD]

        def score(block, count, masked, initial):
            here = pl.ds(pl.multiple_of(block * rows, rows), count * rows)
            keys = kv_ref[here, 2 * h * HD : (2 * h + 1) * HD]
            scores = contract_last(query_ref[...], keys) * scale
            parts = []
            for i in range(count):
                part = scores[:, i * rows : (i + 1) * rows]
                if masked:
                    part = part.reshape(GROUP, rows, rows) + bias_ref[block + i][None]
                    part = part.reshape(GROUP * rows, rows)
                score_ref[block + i] = part
                parts += [part[:, at : at + FT] for at in range(0, rows, FT)]
            if not initial:
                parts.append(max_ref[...])
            max_ref[...] = functools.reduce(jnp.maximum, parts)

        def mix(block, count):
            here = pl.ds(pl.multiple_of(block * rows, rows), count * rows)
            values = kv_ref[here, (2 * h + 1) * HD : (2 * h + 2) * HD]
            values = jnp.concatenate([values, jnp.ones_like(values)], axis=1)
            weights = [
                jnp.exp((score_ref[block + i, :, at : at + FT] - max_ref[...]).astype(jnp.bfloat16))
                for i in range(count)
                for at in range(0, rows, FT)
            ]
            weights = jnp.concatenate(weights, axis=1)
            return jnp.dot(weights, values, preferred_element_type=jnp.float32)

        score(last, 1, masked=True, initial=True)

        @pl.when(paired > first)
        def _():
            score(first, 1, masked=True, initial=False)

        @pl.loop(0, masked_pairs)
        def _(pair):
            score(paired + 2 * pair, 2, masked=True, initial=False)

        @pl.loop(masked_pairs, pairs)
        def _(pair):
            score(paired + 2 * pair, 2, masked=False, initial=False)

        row_max = jnp.max(max_ref[...], axis=1, keepdims=True)
        max_ref[...] = jnp.broadcast_to(row_max, max_ref.shape)

        acc_ref[...] = mix(last, 1)

        @pl.when(paired > first)
        def _():
            acc_ref[...] += mix(first, 1)

        @pl.loop(0, pairs)
        def _(pair):
            acc_ref[...] += mix(paired + 2 * pair, 2)

        mixed = acc_ref[:, :HD] / acc_ref[:, HD:]
        for g in range(GROUP):
            result_ref[h, :, g * HD : (g + 1) * HD] = mixed[g * rows : (g + 1) * rows].astype(
                result_ref.dtype
            )
        result_copy(h).start()
    for h in range(heads):
        result_copy(h).wait()


def attend(queries, slots, place):
    rows = queries.shape[0]
    columns = slots[0].shape[1]
    heads = columns // (2 * HD)
    blocks = len(slots) * FT // rows
    wide = GROUP * HD
    tall = GROUP * rows
    anywhere = pl.BlockSpec(memory_space=pl.ANY)
    scalars = pl.BlockSpec(memory_space=pltpu.SMEM)
    cells = heads * tall * blocks * rows
    return pl.pallas_call(
        functools.partial(attend_kernel, slots=len(slots), heads=heads),
        in_specs=[scalars] + [anywhere] * (1 + len(slots)),
        out_specs=anywhere,
        out_shape=jax.ShapeDtypeStruct(queries.shape, jnp.bfloat16),
        scratch_shapes=[
            pltpu.VMEM((len(slots) * FT, columns), jnp.bfloat16),
            pltpu.VMEM(queries.shape, jnp.bfloat16),
            pltpu.VMEM((tall, HD), jnp.bfloat16),
            pltpu.VMEM((blocks, rows, rows), jnp.float32),
            pltpu.VMEM((blocks, tall, rows), jnp.float32),
            pltpu.VMEM((tall, FT), jnp.float32),
            pltpu.VMEM((tall, 2 * HD), jnp.float32),
            pltpu.VMEM((heads, rows, wide), jnp.bfloat16),
            pltpu.SemaphoreType.DMA((2, len(slots))),
            pltpu.SemaphoreType.DMA((2,)),
            pltpu.SemaphoreType.DMA((heads,)),
        ],
        compiler_params=pltpu.CompilerParams(vmem_limit_bytes=LANGUAGE_VMEM),
        cost_estimate=pl.CostEstimate(
            flops=6 * cells * HD,
            bytes_accessed=2 * len(slots) * FT * columns + 4 * rows * heads * wide,
            transcendentals=cells,
        ),
    )(place, queries, *slots)


def shards(
    vis_qkv,
    vis_resid,
    vis_out_w,
    merge_gain,
    merge_bias,
    vis_kv_w,
    frame_host,
    vis_pos,
    doc_ids,
    text_kv,
    queries,
):
    device = lax.axis_index("ctx")
    tp_index = lax.axis_index("tp")
    tp_size = lax.axis_size("tp")
    per_device = queries.shape[0]
    patches = vis_qkv.shape[0]
    width = vis_qkv.shape[2]
    local_kv = vis_kv_w.shape[2] // tp_size
    positions = doc_ids.shape[0]
    frames = vis_pos.shape[0]

    peers = lax.axis_size("ctx")
    rows = peers // 2
    first_pos = device * per_device

    fields = jnp.transpose(vis_qkv, (1, 0, 2))
    part_count = 2
    part_rows = patches // part_count
    text_low, text_high = text_kv[:FT], text_kv[FT:]
    handed = shifted(text_high, "ctx", peers // 2)
    (first_context,) = vit_attention(fields, text_high, 0, tp_index)
    second_context, low_rows, high_rows = vit_attention(
        fields, first_context, 1, tp_index, (first_context, vis_out_w, vis_resid)
    )
    contexts = [first_context, second_context]
    arrived = [
        [shifted(context, "tp", distance) for distance in range(1, tp_size)]
        for context in contexts
    ]

    def out_rows(distance):
        source = lax.rem(tp_after + tp_size - distance, tp_size)
        return lax.dynamic_slice_in_dim(vis_out_w, source * width, width, axis=0)

    handed, low_rows = lax.optimization_barrier((handed, low_rows))
    hidden_parts = [low_rows, high_rows]
    first_frame = jnp.any(vis_pos == first_pos)
    second_frame = jnp.any(vis_pos == first_pos + FT)
    text_block = jnp.where(first_frame, jnp.where(second_frame, handed, text_high), text_low)
    text = Ring(text_block.reshape(FT, local_kv), rows)
    tp_after = tp_index
    for part in range(part_count):
        for distance in range(1, tp_size):
            hidden_parts[part] = hidden_parts[part] + jnp.dot(
                arrived[part][distance - 1], out_rows(distance), preferred_element_type=jnp.float32
            )
        if part == 0:
            hidden_parts, tp_after = lax.optimization_barrier((hidden_parts, tp_index))
    hidden = jnp.concatenate(hidden_parts, axis=0)
    sums = jnp.stack([jnp.sum(hidden, axis=1), jnp.sum(hidden * hidden, axis=1)])
    others = [shifted(sums, "tp", distance) for distance in range(1, tp_size)]
    sums = text.advance(sums)
    row_sum, row_squares = functools.reduce(jnp.add, others, sums)
    mean_value = row_sum / VD
    variance = row_squares / VD - mean_value * mean_value
    normed = (hidden - mean_value[:, None]) * lax.rsqrt(variance + 1e-06)[
        :, None
    ] * merge_gain + merge_bias
    normed = normed.astype(jnp.bfloat16)

    received = []
    for distance in range(1, tp_size):
        block = lax.rem(tp_index + distance, tp_size)
        part = merged_columns(normed, vis_kv_w, block, local_kv, jnp.bfloat16)
        received.append(shifted(part, "tp", distance))
    own = merged_columns(normed, vis_kv_w, tp_index, local_kv, jnp.float32)
    own = text.advance(own)
    for part in received:
        own = own + part.astype(jnp.float32)
    own = own.astype(jnp.bfloat16)
    vision = Ring(own, rows)
    vis_pos, own = lax.optimization_barrier((vis_pos, own))
    place = tables(device, vis_pos, frame_host, doc_ids, peers, per_device)
    for hop in range(1, rows):
        if hop == 1:
            vision.moving, place = text.advance((vision.moving, place))
        vision.advance((), lag=1)
    return attend(queries, text.all() + vision.all(), place)


def solution(mesh):
    return jax.shard_map(
        shards,
        mesh=mesh,
        in_specs=(
            P(("dp", "ctx"), None, "tp"),
            P(("dp", "ctx"), "tp"),
            P(None, "tp"),
            P("tp"),
            P("tp"),
            P(None, "tp", None),
            P("dp"),
            P("dp"),
            P("dp"),
            P(("dp", "ctx"), "tp", None, None),
            P(("dp", "ctx"), "tp"),
        ),
        out_specs=P(("dp", "ctx"), "tp"),
        check_vma=False,
    )
```

```python
import functools
import math

import jax
import jax.numpy as jnp
from jax import lax
from jax.experimental import pallas as pl
from jax.experimental.pallas import tpu as pltpu
from jax.sharding import PartitionSpec as P

VD = 1280
VH = 16
HD = 128
H = 32
KVH = 8
FT = 128
GROUP = H // KVH
DOCS = 4
LANES = 128

MASKED = -1e30
VMEM_LIMIT = 16 * 1024 * 1024
MERGE_VMEM = 52 * 1024 * 1024
LANGUAGE_VMEM = 58 * 1024 * 1024


def contract_last(a, b):
    return lax.dot_general(a, b, (((1,), (1,)), ((), ())), preferred_element_type=jnp.float32)


def shifted(block, axis, distance):
    count = lax.axis_size(axis)
    return lax.ppermute(block, axis, [(i, (i + distance) % count) for i in range(count)])


def ring_place(row, rows):
    return jnp.where(row % 2 == 1, (row + 1) // 2, (rows - row // 2) % rows)


def to_next_row(block, rows):
    order = [0] + list(range(1, rows, 2)) + list(range(rows - 2, 0, -2))
    after = dict(zip(order, order[1:] + order[:1]))
    return lax.ppermute(
        block,
        "ctx",
        [(2 * row + side, 2 * after[row] + side) for row in range(rows) for side in range(2)],
    )


def to_other_side(block, rows):
    return lax.ppermute(
        block, "ctx", [(2 * row + side, 2 * row + 1 - side) for row in range(rows) for side in range(2)]
    )


class Ring:
    def __init__(self, block, rows):
        self.rows = rows
        self.blocks = [block]
        self.start(block)

    def start(self, block):
        self.moving = to_next_row(block, self.rows) if len(self.blocks) < 2 * self.rows - 1 else None
        self.blocks.append(to_other_side(block, self.rows))

    def advance(self, beside, lag=0):
        if self.moving is None:
            return beside
        if len(self.blocks) > 2 * lag:
            at = len(self.blocks) - 1 - 2 * lag
            held, self.blocks[at], beside = lax.optimization_barrier(
                (self.moving, self.blocks[at], beside)
            )
        else:
            held, beside = lax.optimization_barrier((self.moving, beside))
        self.blocks.append(held)
        self.start(held)
        return beside

    def all(self):
        while self.moving is not None:
            self.advance(())
        return self.blocks


def vit_kernel(index_ref, q_ref, k_ref, v_ref, after_ref, *rest, heads, dim):
    o_ref = rest[0]
    if len(rest) > 1:
        earlier_ref, weight_ref, resid_ref, o_ref, low_ref, high_ref = rest
    width = q_ref.shape[2]
    to_exp = 1.0 / math.sqrt(dim)
    tiles = {}
    for g in range(heads):
        first, last = g * dim, (g + 1) * dim
        low = first // LANES * LANES
        high = min(width, -(-last // LANES) * LANES)
        lane = lax.broadcasted_iota(jnp.int32, (1, high - low), 1) + low
        inside = (lane >= first) & (lane < last)
        keep = jnp.where(inside, 1.0, 0.0).astype(jnp.bfloat16)
        other = jnp.where(inside, 0.0, 1.0).astype(jnp.bfloat16)
        scores = contract_last(q_ref[0, :, low:high] * keep, k_ref[0, :, low:high])
        row_max = jnp.max(scores, axis=1, keepdims=True)
        weights = jnp.exp((scores - row_max) * to_exp).astype(jnp.bfloat16)
        mixed = jnp.dot(
            weights, v_ref[0, :, low:high] * keep + other, preferred_element_type=jnp.float32
        )
        spare = 0 if low < first else last - low
        mixed = mixed / mixed[:, spare : spare + 1]
        for at in range(low, high, LANES):
            end = min(at + LANES, high)
            piece = mixed[:, at - low : end - low]
            if at in tiles:
                piece = jnp.where(inside[:, at - low : end - low], piece, tiles[at])
            tiles[at] = piece
    for at, piece in tiles.items():
        o_ref[:, at : at + piece.shape[1]] = piece.astype(o_ref.dtype)
    if len(rest) > 1:
        rows = o_ref.shape[0]
        for part, (context, hidden_ref) in enumerate([(earlier_ref, low_ref), (o_ref, high_ref)]):
            here = slice(part * rows, (part + 1) * rows)
            hidden_ref[...] = resid_ref[here].astype(jnp.float32) + jnp.dot(
                context[...], weight_ref[...], preferred_element_type=jnp.float32
            )


def vit_attention(fields, after, part, tp_index, projection=None):
    _, patches, width = fields.shape
    rows = patches // 2
    dim = VD // VH
    one = pl.BlockSpec((rows, width), lambda f, _: (0, 0))
    in_specs = [
        pl.BlockSpec((1, rows, width), lambda f, _: (0, part, 0)),
        pl.BlockSpec((1, patches, width), lambda f, _: (1, 0, 0)),
        pl.BlockSpec((1, patches, width), lambda f, _: (2, 0, 0)),
        pl.BlockSpec(memory_space=pl.ANY),
    ]
    out_specs = [one]
    out_shape = [jax.ShapeDtypeStruct((rows, width), jnp.bfloat16)]
    if projection:
        in_specs += [
            one,
            pl.BlockSpec((width, width), lambda f, index: (index[0], 0)),
            pl.BlockSpec((patches, width), lambda f, _: (0, 0)),
        ]
        out_specs += [one, one]
        out_shape += [jax.ShapeDtypeStruct((rows, width), jnp.float32)] * 2
    return pl.pallas_call(
        functools.partial(vit_kernel, heads=width // dim, dim=dim),
        grid_spec=pltpu.PrefetchScalarGridSpec(
            num_scalar_prefetch=1, grid=(1,), in_specs=in_specs, out_specs=out_specs
        ),
        out_shape=out_shape,
        compiler_params=pltpu.CompilerParams(
            vmem_limit_bytes=VMEM_LIMIT
        ),
        cost_estimate=pl.CostEstimate(flops=1024, bytes_accessed=1024, transcendentals=0),
    )(jnp.reshape(tp_index, (1,)), fields, fields, fields, after, *(projection or ()))


def merge_kernel(block_ref, x_ref, w_ref, o_ref, held_ref, rows_ref, sems, *, step):
    tokens, columns = o_ref.shape
    patches = x_ref.shape[0]
    steps = columns // step

    def weights_in(n):
        source = w_ref.at[:, :, pl.ds(pl.multiple_of(block_ref[0] * columns + n * step, step), step)]
        return pltpu.make_async_copy(source, held_ref.at[n], sems.at[n])

    for n in range(steps):
        weights_in(n).start()
    token = lax.broadcasted_iota(jnp.int32, (tokens, patches), 0)
    patch = lax.broadcasted_iota(jnp.int32, (tokens, patches), 1)
    for j in range(4):
        pick = jnp.where(patch == 4 * token + j, 1.0, 0.0).astype(jnp.bfloat16)
        rows_ref[j] = jnp.dot(pick, x_ref[...], preferred_element_type=jnp.float32).astype(
            jnp.bfloat16
        )
    for n in range(steps):
        weights_in(n).wait()
        total = jnp.zeros((tokens, step), jnp.float32)
        for j in range(4):
            total = total + jnp.dot(
                rows_ref[j], held_ref[n, j], preferred_element_type=jnp.float32
            )
        o_ref[:, n * step : (n + 1) * step] = total.astype(o_ref.dtype)


def merged_columns(normed, weights, block, columns, dtype):
    patches, width = normed.shape
    tokens = patches // 4
    step = min(columns, 256)
    steps = columns // step
    return pl.pallas_call(
        functools.partial(merge_kernel, step=step),
        in_specs=[
            pl.BlockSpec(memory_space=pltpu.SMEM),
            pl.BlockSpec(memory_space=pltpu.VMEM),
            pl.BlockSpec(memory_space=pl.ANY),
        ],
        out_specs=pl.BlockSpec(memory_space=pltpu.VMEM),
        out_shape=jax.ShapeDtypeStruct((tokens, columns), dtype),
        scratch_shapes=[
            pltpu.VMEM((steps, 4, width, step), jnp.bfloat16),
            pltpu.VMEM((4, tokens, width), jnp.bfloat16),
            pltpu.SemaphoreType.DMA((steps,)),
        ],
        compiler_params=pltpu.CompilerParams(vmem_limit_bytes=MERGE_VMEM),
        cost_estimate=pl.CostEstimate(
            flops=2 * tokens * 4 * width * columns,
            bytes_accessed=4 * width * columns * 2 + patches * width * 2,
            transcendentals=0,
        ),
    )(jnp.reshape(block, (1,)), normed, weights)


def tables_kernel(
    device_ref, vis_pos_ref, frame_host_ref, doc_ref, place_ref, *, peers, per_device,
):
    device = device_ref[0]
    rows = peers // 2
    frames = vis_pos_ref.shape[0]
    slots_each = per_device // FT
    first_pos = device * per_device
    starts = [
        jnp.sum(jnp.where(doc_ref[...] < d, 1.0, 0.0)).astype(jnp.int32) for d in range(1, DOCS)
    ]
    for i, value in enumerate([first_pos] + starts):
        place_ref[2 * peers + i] = value

    def block_from(source):
        hop = lax.rem(ring_place(device // 2, rows) + rows - ring_place(source // 2, rows), rows)
        return 2 * hop + jnp.where(lax.rem(source, 2) == lax.rem(device, 2), 0, 1)

    def one_slot(slot, carry):
        frame, before_is_text = carry
        pos = slot * FT
        here = jnp.minimum(frame, frames - 1)
        is_frame = (frame < frames) & (vis_pos_ref[here] == pos)
        owner = slot // slots_each
        second = lax.rem(slot, slots_each) != 0
        partner = lax.rem(owner + peers // 2, peers)
        holder = jnp.where(second & (before_is_text == 1), partner, owner)
        source = jnp.where(is_frame, frame_host_ref[here], holder)
        flag = jnp.where(is_frame, 1, 0)
        place_ref[block_from(source) + peers * flag] = pos
        return frame + flag, 1 - flag

    lax.fori_loop(0, peers * slots_each, one_slot, (jnp.int32(0), jnp.int32(0)))


def tables(device, vis_pos, frame_host, doc_ids, peers, per_device):
    scalars = pl.BlockSpec(memory_space=pltpu.SMEM)
    return pl.pallas_call(
        functools.partial(tables_kernel, peers=peers, per_device=per_device),
        in_specs=[scalars] * 3 + [pl.BlockSpec(memory_space=pltpu.VMEM)],
        out_specs=scalars,
        out_shape=jax.ShapeDtypeStruct((2 * peers + DOCS,), jnp.int32),
    )(jnp.reshape(device, (1,)), vis_pos, frame_host, doc_ids.reshape(-1, LANES))


def attend_kernel(place_ref, q_ref, *rest, slots, heads):
    slot_refs, out_ref = rest[:slots], rest[slots]
    kv_ref, held_q_ref, query_ref, bias_ref, score_ref, max_ref, acc_ref, result_ref = rest[
        slots + 1 : slots + 9
    ]
    slot_sems, query_sems, out_sems = rest[slots + 9 :]
    rows = q_ref.shape[0]
    scale = 1.0 / math.sqrt(HD)
    wide = GROUP * HD
    first_pos = place_ref[slots]
    starts = [place_ref[slots + i] for i in range(1, DOCS)]

    def first_key(pos):
        return functools.reduce(jnp.maximum, [jnp.where(s <= pos, s, 0) for s in starts])

    last = first_pos // rows
    first = first_key(first_pos) // rows
    paired = first + (last - first) % 2
    masked_pairs = (jnp.maximum(first_key(first_pos + rows - 1) - paired * rows, 0) + 2 * rows - 1) // (
        2 * rows
    )
    pairs = (last - paired) // 2
    masked_pairs = jnp.minimum(masked_pairs, pairs)

    cuts = [(0, heads)]

    def slot_copy(i, cut):
        begin, end = cuts[cut]
        lanes = slice(begin * 2 * HD, end * 2 * HD)
        there = pl.ds(pl.multiple_of(place_ref[i], FT), FT)
        return pltpu.make_async_copy(
            slot_refs[i].at[:, lanes], kv_ref.at[there, lanes], slot_sems.at[cut, i]
        )

    def query_copy(cut):
        begin, end = cuts[cut]
        lanes = slice(begin * wide, end * wide)
        return pltpu.make_async_copy(
            q_ref.at[:, lanes], held_q_ref.at[:, lanes], query_sems.at[cut]
        )

    def wanted(i):
        block = place_ref[i] // rows
        return (block >= first) & (block <= last)

    def all_slots(cut, act):
        for i in range(slots):
            pl.when(wanted(i))(functools.partial(act, i, cut))

    for cut in range(len(cuts)):
        query_copy(cut).start()
        all_slots(cut, lambda i, cut: slot_copy(i, cut).start())

    def mask(block):
        query_pos = first_pos + lax.broadcasted_iota(jnp.int32, (rows, FT), 0)
        low = first_key(query_pos)
        for at in range(0, rows, FT):
            key_pos = block * rows + at + lax.broadcasted_iota(jnp.int32, (rows, FT), 1)
            allowed = (key_pos <= query_pos) & (key_pos >= low)
            bias_ref[block, :, at : at + FT] = jnp.where(allowed, 0.0, MASKED)

    pl.loop(first, paired + 2 * masked_pairs)(mask)
    mask(last)

    def result_copy(h):
        return pltpu.make_async_copy(
            result_ref.at[h], out_ref.at[:, h * wide : (h + 1) * wide], out_sems.at[h]
        )

    for cut in range(len(cuts)):
        query_copy(cut).wait()
        all_slots(cut, lambda i, cut: slot_copy(i, cut).wait())
    for h in range(heads):
        for g in range(GROUP):
            at = h * wide + g * HD
            query_ref[h, g * rows : (g + 1) * rows] = held_q_ref[:, at : at + HD]

    def score(block, count, masked, initial):
        here = pl.ds(pl.multiple_of(block * rows, rows), count * rows)
        for h in range(heads):
            keys = kv_ref[here, 2 * h * HD : (2 * h + 1) * HD]
            scores = contract_last(query_ref[h], keys) * scale
            parts = []
            for i in range(count):
                part = scores[:, i * rows : (i + 1) * rows]
                if masked:
                    part = part.reshape(GROUP, rows, rows) + bias_ref[block + i][None]
                    part = part.reshape(GROUP * rows, rows)
                score_ref[h, block + i] = part
                parts += [part[:, at : at + FT] for at in range(0, rows, FT)]
            if not initial:
                parts.append(max_ref[h])
            max_ref[h] = functools.reduce(jnp.maximum, parts)

    def mix(block, count, initial):
        here = pl.ds(pl.multiple_of(block * rows, rows), count * rows)
        for h in range(heads):
            values = kv_ref[here, (2 * h + 1) * HD : (2 * h + 2) * HD]
            values = jnp.concatenate([values, jnp.ones_like(values)], axis=1)
            weights = [
                jnp.exp(score_ref[h, block + i, :, at : at + FT] - max_ref[h]).astype(jnp.bfloat16)
                for i in range(count)
                for at in range(0, rows, FT)
            ]
            weights = jnp.concatenate(weights, axis=1)
            mixed = jnp.dot(weights, values, preferred_element_type=jnp.float32)
            acc_ref[h] = mixed if initial else acc_ref[h] + mixed

    score(last, 1, masked=True, initial=True)

    @pl.when(paired > first)
    def _():
        score(first, 1, masked=True, initial=False)

    @pl.loop(0, masked_pairs)
    def _(pair):
        score(paired + 2 * pair, 2, masked=True, initial=False)

    @pl.loop(masked_pairs, pairs)
    def _(pair):
        score(paired + 2 * pair, 2, masked=False, initial=False)

    for h in range(heads):
        row_max = jnp.max(max_ref[h], axis=1, keepdims=True)
        max_ref[h] = jnp.broadcast_to(row_max, (GROUP * rows, FT))

    mix(last, 1, initial=True)

    @pl.when(paired > first)
    def _():
        mix(first, 1, initial=False)

    @pl.loop(0, pairs)
    def _(pair):
        mix(paired + 2 * pair, 2, initial=False)

    for h in range(heads):
        mixed = acc_ref[h, :, :HD] / acc_ref[h, :, HD:]
        for g in range(GROUP):
            result_ref[h, :, g * HD : (g + 1) * HD] = mixed[g * rows : (g + 1) * rows].astype(
                result_ref.dtype
            )
        result_copy(h).start()
    for h in range(heads):
        result_copy(h).wait()


def attend(queries, slots, place):
    rows = queries.shape[0]
    columns = slots[0].shape[1]
    heads = columns // (2 * HD)
    blocks = len(slots) * FT // rows
    wide = GROUP * HD
    tall = GROUP * rows
    anywhere = pl.BlockSpec(memory_space=pl.ANY)
    scalars = pl.BlockSpec(memory_space=pltpu.SMEM)
    cells = heads * tall * blocks * rows
    return pl.pallas_call(
        functools.partial(attend_kernel, slots=len(slots), heads=heads),
        in_specs=[scalars] + [anywhere] * (1 + len(slots)),
        out_specs=anywhere,
        out_shape=jax.ShapeDtypeStruct(queries.shape, jnp.bfloat16),
        scratch_shapes=[
            pltpu.VMEM((len(slots) * FT, columns), jnp.bfloat16),
            pltpu.VMEM(queries.shape, jnp.bfloat16),
            pltpu.VMEM((heads, tall, HD), jnp.bfloat16),
            pltpu.VMEM((blocks, rows, rows), jnp.float32),
            pltpu.VMEM((heads, blocks, tall, rows), jnp.float32),
            pltpu.VMEM((heads, tall, FT), jnp.float32),
            pltpu.VMEM((heads, tall, 2 * HD), jnp.float32),
            pltpu.VMEM((heads, rows, wide), jnp.bfloat16),
            pltpu.SemaphoreType.DMA((2, len(slots))),
            pltpu.SemaphoreType.DMA((2,)),
            pltpu.SemaphoreType.DMA((heads,)),
        ],
        compiler_params=pltpu.CompilerParams(vmem_limit_bytes=LANGUAGE_VMEM),
        cost_estimate=pl.CostEstimate(
            flops=6 * cells * HD,
            bytes_accessed=2 * len(slots) * FT * columns + 4 * rows * heads * wide,
            transcendentals=cells,
        ),
    )(place, queries, *slots)


def shards(
    vis_qkv,
    vis_resid,
    vis_out_w,
    merge_gain,
    merge_bias,
    vis_kv_w,
    frame_host,
    vis_pos,
    doc_ids,
    text_kv,
    queries,
):
    device = lax.axis_index("ctx")
    tp_index = lax.axis_index("tp")
    tp_size = lax.axis_size("tp")
    per_device = queries.shape[0]
    patches = vis_qkv.shape[0]
    width = vis_qkv.shape[2]
    local_kv = vis_kv_w.shape[2] // tp_size
    positions = doc_ids.shape[0]
    frames = vis_pos.shape[0]

    peers = lax.axis_size("ctx")
    rows = peers // 2
    first_pos = device * per_device

    fields = jnp.transpose(vis_qkv, (1, 0, 2))
    part_count = 2
    part_rows = patches // part_count
    text_high = text_kv[FT:]
    handed = shifted(text_high, "ctx", peers // 2)
    (first_context,) = vit_attention(fields, text_high, 0, tp_index)
    second_context, low_rows, high_rows = vit_attention(
        fields, first_context, 1, tp_index, (first_context, vis_out_w, vis_resid)
    )
    contexts = [first_context, second_context]
    arrived = [
        [shifted(context, "tp", distance) for distance in range(1, tp_size)]
        for context in contexts
    ]

    def out_rows(distance):
        source = lax.rem(tp_after + tp_size - distance, tp_size)
        return lax.dynamic_slice_in_dim(vis_out_w, source * width, width, axis=0)

    vis_pos, text_kv, _ = lax.optimization_barrier((vis_pos, text_kv, second_context))
    first_frame = jnp.any(vis_pos == first_pos)
    second_frame = jnp.any(vis_pos == first_pos + FT)
    text_block = jnp.where(first_frame, text_kv[FT:], text_kv[:FT]).reshape(FT, local_kv)
    handed, text_block, _ = lax.optimization_barrier((handed, text_block, low_rows))
    text_block = jnp.where(
        first_frame & second_frame, handed.reshape(FT, local_kv), text_block
    )
    hidden_parts = [low_rows, high_rows]
    text = Ring(text_block, rows)
    tp_after = tp_index
    for part in range(part_count):
        for distance in range(1, tp_size):
            hidden_parts[part] = hidden_parts[part] + jnp.dot(
                arrived[part][distance - 1], out_rows(distance), preferred_element_type=jnp.float32
            )
        if part == 0:
            tp_after, _ = lax.optimization_barrier((tp_index, hidden_parts[0]))
    hidden = jnp.concatenate(hidden_parts, axis=0)
    sums = jnp.stack([jnp.sum(hidden, axis=1), jnp.sum(hidden * hidden, axis=1)])
    others = [shifted(sums, "tp", distance) for distance in range(1, tp_size)]
    sums = text.advance(sums)
    row_sum, row_squares = functools.reduce(jnp.add, others, sums)
    mean_value = row_sum / VD
    variance = row_squares / VD - mean_value * mean_value
    normed = (hidden - mean_value[:, None]) * lax.rsqrt(variance + 1e-06)[
        :, None
    ] * merge_gain + merge_bias
    normed = normed.astype(jnp.bfloat16)

    received = []
    for distance in range(1, tp_size):
        block = lax.rem(tp_index + distance, tp_size)
        part = merged_columns(normed, vis_kv_w, block, local_kv, jnp.bfloat16)
        received.append(shifted(part, "tp", distance))
    own = merged_columns(normed, vis_kv_w, tp_index, local_kv, jnp.float32)
    own = text.advance(own)
    for part in received:
        own = own + part.astype(jnp.float32)
    own = own.astype(jnp.bfloat16)
    vision = Ring(own, rows)
    vis_pos, own = lax.optimization_barrier((vis_pos, own))
    place = tables(device, vis_pos, frame_host, doc_ids, peers, per_device)
    for hop in range(1, rows):
        if hop == 1:
            vision.moving, place = text.advance((vision.moving, place))
        vision.advance((), lag=1)
    return attend(queries, text.all() + vision.all(), place)


def solution(mesh):
    return jax.shard_map(
        shards,
        mesh=mesh,
        in_specs=(
            P(("dp", "ctx"), None, "tp"),
            P(("dp", "ctx"), "tp"),
            P(None, "tp"),
            P("tp"),
            P("tp"),
            P(None, "tp", None),
            P("dp"),
            P("dp"),
            P("dp"),
            P(("dp", "ctx"), "tp", None, None),
            P(("dp", "ctx"), "tp"),
        ),
        out_specs=P(("dp", "ctx"), "tp"),
        check_vma=False,
    )
```

```python
import functools
import math

import jax
import jax.numpy as jnp
from jax import lax
from jax.experimental import pallas as pl
from jax.experimental.pallas import tpu as pltpu
from jax.sharding import PartitionSpec as P

VD = 1280
VH = 16
HD = 128
H = 32
KVH = 8
FT = 128
GROUP = H // KVH
DOCS = 4
LANES = 128

MASKED = -1e30
VMEM_LIMIT = 16 * 1024 * 1024
MERGE_VMEM = 52 * 1024 * 1024
LANGUAGE_VMEM = 58 * 1024 * 1024


def contract_last(a, b):
    return lax.dot_general(a, b, (((1,), (1,)), ((), ())), preferred_element_type=jnp.float32)


def shifted(block, axis, distance):
    count = lax.axis_size(axis)
    return lax.ppermute(block, axis, [(i, (i + distance) % count) for i in range(count)])


def ring_place(row, rows):
    return jnp.where(row % 2 == 1, (row + 1) // 2, (rows - row // 2) % rows)


def to_next_row(block, rows):
    order = [0] + list(range(1, rows, 2)) + list(range(rows - 2, 0, -2))
    after = dict(zip(order, order[1:] + order[:1]))
    return lax.ppermute(
        block,
        "ctx",
        [(2 * row + side, 2 * after[row] + side) for row in range(rows) for side in range(2)],
    )


def to_other_side(block, rows):
    return lax.ppermute(
        block, "ctx", [(2 * row + side, 2 * row + 1 - side) for row in range(rows) for side in range(2)]
    )


class Ring:
    def __init__(self, block, rows):
        self.rows = rows
        self.blocks = [block]
        self.start(block)

    def start(self, block):
        self.moving = to_next_row(block, self.rows) if len(self.blocks) < 2 * self.rows - 1 else None
        self.blocks.append(to_other_side(block, self.rows))

    def advance(self, beside, lag=0):
        if self.moving is None:
            return beside
        if len(self.blocks) > 2 * lag:
            at = len(self.blocks) - 1 - 2 * lag
            held, self.blocks[at], beside = lax.optimization_barrier(
                (self.moving, self.blocks[at], beside)
            )
        else:
            held, beside = lax.optimization_barrier((self.moving, beside))
        self.blocks.append(held)
        self.start(held)
        return beside

    def all(self):
        while self.moving is not None:
            self.advance(())
        return self.blocks


def vit_kernel(index_ref, q_ref, k_ref, v_ref, after_ref, *rest, heads, dim):
    o_ref = rest[0]
    if len(rest) > 1:
        earlier_ref, weight_ref, resid_ref, o_ref, low_ref, high_ref = rest
    width = q_ref.shape[2]
    to_exp = 1.0 / math.sqrt(dim)
    tiles = {}
    for g in range(heads):
        first, last = g * dim, (g + 1) * dim
        low = first // LANES * LANES
        high = min(width, -(-last // LANES) * LANES)
        lane = lax.broadcasted_iota(jnp.int32, (1, high - low), 1) + low
        inside = (lane >= first) & (lane < last)
        keep = jnp.where(inside, 1.0, 0.0).astype(jnp.bfloat16)
        other = jnp.where(inside, 0.0, 1.0).astype(jnp.bfloat16)
        scores = contract_last(q_ref[0, :, low:high] * keep, k_ref[0, :, low:high])
        row_max = jnp.max(scores, axis=1, keepdims=True)
        weights = jnp.exp((scores - row_max) * to_exp).astype(jnp.bfloat16)
        mixed = jnp.dot(
            weights, v_ref[0, :, low:high] * keep + other, preferred_element_type=jnp.float32
        )
        spare = 0 if low < first else last - low
        mixed = mixed / mixed[:, spare : spare + 1]
        for at in range(low, high, LANES):
            end = min(at + LANES, high)
            piece = mixed[:, at - low : end - low]
            if at in tiles:
                piece = jnp.where(inside[:, at - low : end - low], piece, tiles[at])
            tiles[at] = piece
    for at, piece in tiles.items():
        o_ref[:, at : at + piece.shape[1]] = piece.astype(o_ref.dtype)
    if len(rest) > 1:
        rows = o_ref.shape[0]
        for part, (context, hidden_ref) in enumerate([(earlier_ref, low_ref), (o_ref, high_ref)]):
            here = slice(part * rows, (part + 1) * rows)
            hidden_ref[...] = resid_ref[here].astype(jnp.float32) + jnp.dot(
                context[...], weight_ref[...], preferred_element_type=jnp.float32
            )


def vit_attention(fields, after, part, tp_index, projection=None):
    _, patches, width = fields.shape
    rows = patches // 2
    dim = VD // VH
    one = pl.BlockSpec((rows, width), lambda f, _: (0, 0))
    in_specs = [
        pl.BlockSpec((1, rows, width), lambda f, _: (0, part, 0)),
        pl.BlockSpec((1, patches, width), lambda f, _: (1, 0, 0)),
        pl.BlockSpec((1, patches, width), lambda f, _: (2, 0, 0)),
        pl.BlockSpec(memory_space=pl.ANY),
    ]
    out_specs = [one]
    out_shape = [jax.ShapeDtypeStruct((rows, width), jnp.bfloat16)]
    if projection:
        in_specs += [
            one,
            pl.BlockSpec((width, width), lambda f, index: (index[0], 0)),
            pl.BlockSpec((patches, width), lambda f, _: (0, 0)),
        ]
        out_specs += [one, one]
        out_shape += [jax.ShapeDtypeStruct((rows, width), jnp.float32)] * 2
    return pl.pallas_call(
        functools.partial(vit_kernel, heads=width // dim, dim=dim),
        grid_spec=pltpu.PrefetchScalarGridSpec(
            num_scalar_prefetch=1, grid=(1,), in_specs=in_specs, out_specs=out_specs
        ),
        out_shape=out_shape,
        compiler_params=pltpu.CompilerParams(
            vmem_limit_bytes=VMEM_LIMIT
        ),
        cost_estimate=pl.CostEstimate(flops=1024, bytes_accessed=1024, transcendentals=0),
    )(jnp.reshape(tp_index, (1,)), fields, fields, fields, after, *(projection or ()))


def merge_kernel(block_ref, x_ref, w_ref, o_ref, held_ref, rows_ref, sems, *, step):
    tokens, columns = o_ref.shape
    patches = x_ref.shape[0]
    steps = columns // step

    def weights_in(n):
        source = w_ref.at[:, :, pl.ds(pl.multiple_of(block_ref[0] * columns + n * step, step), step)]
        return pltpu.make_async_copy(source, held_ref.at[n], sems.at[n])

    for n in range(steps):
        weights_in(n).start()
    token = lax.broadcasted_iota(jnp.int32, (tokens, patches), 0)
    patch = lax.broadcasted_iota(jnp.int32, (tokens, patches), 1)
    for j in range(4):
        pick = jnp.where(patch == 4 * token + j, 1.0, 0.0).astype(jnp.bfloat16)
        rows_ref[j] = jnp.dot(pick, x_ref[...], preferred_element_type=jnp.float32).astype(
            jnp.bfloat16
        )
    for n in range(steps):
        weights_in(n).wait()
        total = jnp.zeros((tokens, step), jnp.float32)
        for j in range(4):
            total = total + jnp.dot(
                rows_ref[j], held_ref[n, j], preferred_element_type=jnp.float32
            )
        o_ref[:, n * step : (n + 1) * step] = total.astype(o_ref.dtype)


def merged_columns(normed, weights, block, columns, dtype):
    patches, width = normed.shape
    tokens = patches // 4
    step = min(columns, 256)
    steps = columns // step
    return pl.pallas_call(
        functools.partial(merge_kernel, step=step),
        in_specs=[
            pl.BlockSpec(memory_space=pltpu.SMEM),
            pl.BlockSpec(memory_space=pltpu.VMEM),
            pl.BlockSpec(memory_space=pl.ANY),
        ],
        out_specs=pl.BlockSpec(memory_space=pltpu.VMEM),
        out_shape=jax.ShapeDtypeStruct((tokens, columns), dtype),
        scratch_shapes=[
            pltpu.VMEM((steps, 4, width, step), jnp.bfloat16),
            pltpu.VMEM((4, tokens, width), jnp.bfloat16),
            pltpu.SemaphoreType.DMA((steps,)),
        ],
        compiler_params=pltpu.CompilerParams(vmem_limit_bytes=MERGE_VMEM),
        cost_estimate=pl.CostEstimate(flops=1024, bytes_accessed=1024, transcendentals=0),
    )(jnp.reshape(block, (1,)), normed, weights)


def tables_kernel(
    device_ref, vis_pos_ref, frame_host_ref, doc_ref, place_ref, *, peers, per_device,
):
    device = device_ref[0]
    rows = peers // 2
    frames = vis_pos_ref.shape[0]
    slots_each = per_device // FT
    first_pos = device * per_device
    starts = [
        jnp.sum(jnp.where(doc_ref[...] < d, 1.0, 0.0)).astype(jnp.int32) for d in range(1, DOCS)
    ]
    for i, value in enumerate([first_pos] + starts):
        place_ref[2 * peers + i] = value

    def block_from(source):
        hop = lax.rem(ring_place(device // 2, rows) + rows - ring_place(source // 2, rows), rows)
        return 2 * hop + jnp.where(lax.rem(source, 2) == lax.rem(device, 2), 0, 1)

    def one_slot(slot, carry):
        frame, before_is_text = carry
        pos = slot * FT
        here = jnp.minimum(frame, frames - 1)
        is_frame = (frame < frames) & (vis_pos_ref[here] == pos)
        owner = slot // slots_each
        second = lax.rem(slot, slots_each) != 0
        partner = lax.rem(owner + peers // 2, peers)
        holder = jnp.where(second & (before_is_text == 1), partner, owner)
        source = jnp.where(is_frame, frame_host_ref[here], holder)
        flag = jnp.where(is_frame, 1, 0)
        place_ref[block_from(source) + peers * flag] = pos
        return frame + flag, 1 - flag

    lax.fori_loop(0, peers * slots_each, one_slot, (jnp.int32(0), jnp.int32(0)))


def tables(device, vis_pos, frame_host, doc_ids, peers, per_device):
    scalars = pl.BlockSpec(memory_space=pltpu.SMEM)
    return pl.pallas_call(
        functools.partial(tables_kernel, peers=peers, per_device=per_device),
        in_specs=[scalars] * 3 + [pl.BlockSpec(memory_space=pltpu.VMEM)],
        out_specs=scalars,
        out_shape=jax.ShapeDtypeStruct((2 * peers + DOCS,), jnp.int32),
    )(jnp.reshape(device, (1,)), vis_pos, frame_host, doc_ids.reshape(-1, LANES))


def attend_kernel(place_ref, q_ref, *rest, slots, heads):
    slot_refs, out_ref = rest[:slots], rest[slots]
    kv_ref, held_q_ref, query_ref, bias_ref, score_ref, max_ref, acc_ref, result_ref = rest[
        slots + 1 : slots + 9
    ]
    slot_sems, query_sems, out_sems = rest[slots + 9 :]
    rows = q_ref.shape[0]
    scale = 1.0 / math.sqrt(HD)
    wide = GROUP * HD
    first_pos = place_ref[slots]
    starts = [place_ref[slots + i] for i in range(1, DOCS)]

    def first_key(pos):
        return functools.reduce(jnp.maximum, [jnp.where(s <= pos, s, 0) for s in starts])

    last = first_pos // rows
    first = first_key(first_pos) // rows
    paired = first + (last - first) % 2
    masked_pairs = (jnp.maximum(first_key(first_pos + rows - 1) - paired * rows, 0) + 2 * rows - 1) // (
        2 * rows
    )
    pairs = (last - paired) // 2
    masked_pairs = jnp.minimum(masked_pairs, pairs)

    cuts = [(0, heads)]

    def slot_copy(i, cut):
        begin, end = cuts[cut]
        lanes = slice(begin * 2 * HD, end * 2 * HD)
        there = pl.ds(pl.multiple_of(place_ref[i], FT), FT)
        return pltpu.make_async_copy(
            slot_refs[i].at[:, lanes], kv_ref.at[there, lanes], slot_sems.at[cut, i]
        )

    def query_copy(cut):
        begin, end = cuts[cut]
        lanes = slice(begin * wide, end * wide)
        return pltpu.make_async_copy(
            q_ref.at[:, lanes], held_q_ref.at[:, lanes], query_sems.at[cut]
        )

    def wanted(i):
        block = place_ref[i] // rows
        return (block >= first) & (block <= last)

    def all_slots(cut, act):
        for i in range(slots):
            pl.when(wanted(i))(functools.partial(act, i, cut))

    for cut in range(len(cuts)):
        query_copy(cut).start()
        all_slots(cut, lambda i, cut: slot_copy(i, cut).start())

    def mask(block):
        query_pos = first_pos + lax.broadcasted_iota(jnp.int32, (rows, FT), 0)
        low = first_key(query_pos)
        for at in range(0, rows, FT):
            key_pos = block * rows + at + lax.broadcasted_iota(jnp.int32, (rows, FT), 1)
            allowed = (key_pos <= query_pos) & (key_pos >= low)
            bias_ref[block, :, at : at + FT] = jnp.where(allowed, 0.0, MASKED)

    pl.loop(first, paired + 2 * masked_pairs)(mask)
    mask(last)

    def result_copy(h):
        return pltpu.make_async_copy(
            result_ref.at[h], out_ref.at[:, h * wide : (h + 1) * wide], out_sems.at[h]
        )

    for cut in range(len(cuts)):
        query_copy(cut).wait()
        all_slots(cut, lambda i, cut: slot_copy(i, cut).wait())
    for h in range(heads):
        for g in range(GROUP):
            at = h * wide + g * HD
            query_ref[h, g * rows : (g + 1) * rows] = held_q_ref[:, at : at + HD]

    def score(block, count, masked, initial):
        here = pl.ds(pl.multiple_of(block * rows, rows), count * rows)
        for h in range(heads):
            keys = kv_ref[here, 2 * h * HD : (2 * h + 1) * HD]
            scores = contract_last(query_ref[h], keys) * scale
            parts = []
            for i in range(count):
                part = scores[:, i * rows : (i + 1) * rows]
                if masked:
                    part = part.reshape(GROUP, rows, rows) + bias_ref[block + i][None]
                    part = part.reshape(GROUP * rows, rows)
                score_ref[h, block + i] = part
                parts += [part[:, at : at + FT] for at in range(0, rows, FT)]
            if not initial:
                parts.append(max_ref[h])
            max_ref[h] = functools.reduce(jnp.maximum, parts)

    def mix(block, count, initial):
        here = pl.ds(pl.multiple_of(block * rows, rows), count * rows)
        for h in range(heads):
            values = kv_ref[here, (2 * h + 1) * HD : (2 * h + 2) * HD]
            values = jnp.concatenate([values, jnp.ones_like(values)], axis=1)
            weights = [
                jnp.exp(score_ref[h, block + i, :, at : at + FT] - max_ref[h]).astype(jnp.bfloat16)
                for i in range(count)
                for at in range(0, rows, FT)
            ]
            weights = jnp.concatenate(weights, axis=1)
            mixed = jnp.dot(weights, values, preferred_element_type=jnp.float32)
            acc_ref[h] = mixed if initial else acc_ref[h] + mixed

    score(last, 1, masked=True, initial=True)

    @pl.when(paired > first)
    def _():
        score(first, 1, masked=True, initial=False)

    @pl.loop(0, masked_pairs)
    def _(pair):
        score(paired + 2 * pair, 2, masked=True, initial=False)

    @pl.loop(masked_pairs, pairs)
    def _(pair):
        score(paired + 2 * pair, 2, masked=False, initial=False)

    for h in range(heads):
        row_max = jnp.max(max_ref[h], axis=1, keepdims=True)
        max_ref[h] = jnp.broadcast_to(row_max, (GROUP * rows, FT))

    mix(last, 1, initial=True)

    @pl.when(paired > first)
    def _():
        mix(first, 1, initial=False)

    @pl.loop(0, pairs)
    def _(pair):
        mix(paired + 2 * pair, 2, initial=False)

    for h in range(heads):
        mixed = acc_ref[h, :, :HD] / acc_ref[h, :, HD:]
        for g in range(GROUP):
            result_ref[h, :, g * HD : (g + 1) * HD] = mixed[g * rows : (g + 1) * rows].astype(
                result_ref.dtype
            )
        result_copy(h).start()
    for h in range(heads):
        result_copy(h).wait()


def attend(queries, slots, place):
    rows = queries.shape[0]
    columns = slots[0].shape[1]
    heads = columns // (2 * HD)
    blocks = len(slots) * FT // rows
    wide = GROUP * HD
    tall = GROUP * rows
    anywhere = pl.BlockSpec(memory_space=pl.ANY)
    scalars = pl.BlockSpec(memory_space=pltpu.SMEM)
    cells = heads * tall * blocks * rows
    return pl.pallas_call(
        functools.partial(attend_kernel, slots=len(slots), heads=heads),
        in_specs=[scalars] + [anywhere] * (1 + len(slots)),
        out_specs=anywhere,
        out_shape=jax.ShapeDtypeStruct(queries.shape, jnp.bfloat16),
        scratch_shapes=[
            pltpu.VMEM((len(slots) * FT, columns), jnp.bfloat16),
            pltpu.VMEM(queries.shape, jnp.bfloat16),
            pltpu.VMEM((heads, tall, HD), jnp.bfloat16),
            pltpu.VMEM((blocks, rows, rows), jnp.float32),
            pltpu.VMEM((heads, blocks, tall, rows), jnp.float32),
            pltpu.VMEM((heads, tall, FT), jnp.float32),
            pltpu.VMEM((heads, tall, 2 * HD), jnp.float32),
            pltpu.VMEM((heads, rows, wide), jnp.bfloat16),
            pltpu.SemaphoreType.DMA((2, len(slots))),
            pltpu.SemaphoreType.DMA((2,)),
            pltpu.SemaphoreType.DMA((heads,)),
        ],
        compiler_params=pltpu.CompilerParams(vmem_limit_bytes=LANGUAGE_VMEM),
        cost_estimate=pl.CostEstimate(
            flops=6 * cells * HD,
            bytes_accessed=2 * len(slots) * FT * columns + 4 * rows * heads * wide,
            transcendentals=cells,
        ),
    )(place, queries, *slots)


def shards(
    vis_qkv,
    vis_resid,
    vis_out_w,
    merge_gain,
    merge_bias,
    vis_kv_w,
    frame_host,
    vis_pos,
    doc_ids,
    text_kv,
    queries,
):
    device = lax.axis_index("ctx")
    tp_index = lax.axis_index("tp")
    tp_size = lax.axis_size("tp")
    per_device = queries.shape[0]
    patches = vis_qkv.shape[0]
    width = vis_qkv.shape[2]
    local_kv = vis_kv_w.shape[2] // tp_size
    positions = doc_ids.shape[0]
    frames = vis_pos.shape[0]

    peers = lax.axis_size("ctx")
    rows = peers // 2
    first_pos = device * per_device

    fields = jnp.transpose(vis_qkv, (1, 0, 2))
    part_count = 2
    part_rows = patches // part_count
    text_high = text_kv[FT:]
    handed = shifted(text_high, "ctx", peers // 2)
    (first_context,) = vit_attention(fields, text_high, 0, tp_index)
    second_context, low_rows, high_rows = vit_attention(
        fields, first_context, 1, tp_index, (first_context, vis_out_w, vis_resid)
    )
    contexts = [first_context, second_context]
    arrived = [
        [shifted(context, "tp", distance) for distance in range(1, tp_size)]
        for context in contexts
    ]

    def out_rows(distance):
        source = lax.rem(tp_after + tp_size - distance, tp_size)
        return lax.dynamic_slice_in_dim(vis_out_w, source * width, width, axis=0)

    vis_pos, text_kv, _ = lax.optimization_barrier((vis_pos, text_kv, second_context))
    first_frame = jnp.any(vis_pos == first_pos)
    second_frame = jnp.any(vis_pos == first_pos + FT)
    text_block = jnp.where(first_frame, text_kv[FT:], text_kv[:FT]).reshape(FT, local_kv)
    handed, text_block, _ = lax.optimization_barrier((handed, text_block, low_rows))
    text_block = jnp.where(
        first_frame & second_frame, handed.reshape(FT, local_kv), text_block
    )
    hidden_parts = [low_rows, high_rows]
    text = Ring(text_block, rows)
    tp_after = tp_index
    for part in range(part_count):
        for distance in range(1, tp_size):
            hidden_parts[part] = hidden_parts[part] + jnp.dot(
                arrived[part][distance - 1], out_rows(distance), preferred_element_type=jnp.float32
            )
        if part == 0:
            tp_after, _ = lax.optimization_barrier((tp_index, hidden_parts[0]))
    hidden = jnp.concatenate(hidden_parts, axis=0)
    sums = jnp.stack([jnp.sum(hidden, axis=1), jnp.sum(hidden * hidden, axis=1)])
    others = [shifted(sums, "tp", distance) for distance in range(1, tp_size)]
    sums = text.advance(sums)
    row_sum, row_squares = functools.reduce(jnp.add, others, sums)
    mean_value = row_sum / VD
    variance = row_squares / VD - mean_value * mean_value
    normed = (hidden - mean_value[:, None]) * lax.rsqrt(variance + 1e-06)[
        :, None
    ] * merge_gain + merge_bias
    normed = normed.astype(jnp.bfloat16)

    received = []
    for distance in range(1, tp_size):
        block = lax.rem(tp_index + distance, tp_size)
        part = merged_columns(normed, vis_kv_w, block, local_kv, jnp.bfloat16)
        received.append(shifted(part, "tp", distance))
    normed, _ = text.advance((normed, part))
    own = merged_columns(normed, vis_kv_w, tp_index, local_kv, jnp.float32)
    for part in received:
        own = own + part.astype(jnp.float32)
    own = text.advance(own.astype(jnp.bfloat16))
    vision = Ring(own, rows)
    vis_pos, own = lax.optimization_barrier((vis_pos, own))
    place = tables(device, vis_pos, frame_host, doc_ids, peers, per_device)
    for hop in range(1, rows):
        if hop == 1:
            place = vision.advance(place, lag=1)
        elif hop == 2:
            text.blocks[-1] = vision.advance(text.blocks[-1], lag=1)
        else:
            vision.advance((), lag=1)
    return attend(queries, text.all() + vision.all(), place)


def solution(mesh):
    return jax.shard_map(
        shards,
        mesh=mesh,
        in_specs=(
            P(("dp", "ctx"), None, "tp"),
            P(("dp", "ctx"), "tp"),
            P(None, "tp"),
            P("tp"),
            P("tp"),
            P(None, "tp", None),
            P("dp"),
            P("dp"),
            P("dp"),
            P(("dp", "ctx"), "tp", None, None),
            P(("dp", "ctx"), "tp"),
        ),
        out_specs=P(("dp", "ctx"), "tp"),
        check_vma=False,
    )
```

```python
import functools
import math

import jax
import jax.numpy as jnp
from jax import lax
from jax.experimental import pallas as pl
from jax.experimental.pallas import tpu as pltpu
from jax.sharding import PartitionSpec as P

VD = 1280
VH = 16
HD = 128
H = 32
KVH = 8
FT = 128
GROUP = H // KVH
DOCS = 4
LANES = 128

MASKED = -1e30
VMEM_LIMIT = 16 * 1024 * 1024
MERGE_VMEM = 52 * 1024 * 1024
LANGUAGE_VMEM = 58 * 1024 * 1024


def contract_last(a, b):
    return lax.dot_general(a, b, (((1,), (1,)), ((), ())), preferred_element_type=jnp.float32)


def shifted(block, axis, distance):
    count = lax.axis_size(axis)
    return lax.ppermute(block, axis, [(i, (i + distance) % count) for i in range(count)])


def ring_place(row, rows):
    return jnp.where(row % 2 == 1, (row + 1) // 2, (rows - row // 2) % rows)


def to_next_row(block, rows):
    order = [0] + list(range(1, rows, 2)) + list(range(rows - 2, 0, -2))
    after = dict(zip(order, order[1:] + order[:1]))
    return lax.ppermute(
        block,
        "ctx",
        [(2 * row + side, 2 * after[row] + side) for row in range(rows) for side in range(2)],
    )


def to_other_side(block, rows):
    return lax.ppermute(
        block, "ctx", [(2 * row + side, 2 * row + 1 - side) for row in range(rows) for side in range(2)]
    )


class Ring:
    def __init__(self, block, rows):
        self.rows = rows
        self.blocks = [block]
        self.start(block)

    def start(self, block):
        self.moving = to_next_row(block, self.rows) if len(self.blocks) < 2 * self.rows - 1 else None
        self.blocks.append(to_other_side(block, self.rows))

    def advance(self, beside, lag=0):
        if self.moving is None:
            return beside
        if len(self.blocks) > 2 * lag:
            at = len(self.blocks) - 1 - 2 * lag
            held, self.blocks[at], beside = lax.optimization_barrier(
                (self.moving, self.blocks[at], beside)
            )
        else:
            held, beside = lax.optimization_barrier((self.moving, beside))
        self.blocks.append(held)
        self.start(held)
        return beside

    def all(self):
        while self.moving is not None:
            self.advance(())
        return self.blocks


def vit_kernel(index_ref, q_ref, k_ref, v_ref, after_ref, *rest, heads, dim):
    o_ref = rest[0]
    if len(rest) > 1:
        earlier_ref, weight_ref, resid_ref, o_ref, low_ref, high_ref = rest
    width = q_ref.shape[2]
    to_exp = 1.0 / math.sqrt(dim)
    tiles = {}
    for g in range(heads):
        first, last = g * dim, (g + 1) * dim
        low = first // LANES * LANES
        high = min(width, -(-last // LANES) * LANES)
        lane = lax.broadcasted_iota(jnp.int32, (1, high - low), 1) + low
        inside = (lane >= first) & (lane < last)
        keep = jnp.where(inside, 1.0, 0.0).astype(jnp.bfloat16)
        other = jnp.where(inside, 0.0, 1.0).astype(jnp.bfloat16)
        scores = contract_last(q_ref[0, :, low:high] * keep, k_ref[0, :, low:high])
        row_max = jnp.max(scores, axis=1, keepdims=True)
        weights = jnp.exp((scores - row_max) * to_exp).astype(jnp.bfloat16)
        mixed = jnp.dot(
            weights, v_ref[0, :, low:high] * keep + other, preferred_element_type=jnp.float32
        )
        spare = 0 if low < first else last - low
        mixed = mixed / mixed[:, spare : spare + 1]
        for at in range(low, high, LANES):
            end = min(at + LANES, high)
            piece = mixed[:, at - low : end - low]
            if at in tiles:
                piece = jnp.where(inside[:, at - low : end - low], piece, tiles[at])
            tiles[at] = piece
    for at, piece in tiles.items():
        o_ref[:, at : at + piece.shape[1]] = piece.astype(o_ref.dtype)
    if len(rest) > 1:
        rows = o_ref.shape[0]
        for part, (context, hidden_ref) in enumerate([(earlier_ref, low_ref), (o_ref, high_ref)]):
            here = slice(part * rows, (part + 1) * rows)
            hidden_ref[...] = resid_ref[here].astype(jnp.float32) + jnp.dot(
                context[...], weight_ref[...], preferred_element_type=jnp.float32
            )


def vit_attention(fields, after, part, tp_index, projection=None):
    _, patches, width = fields.shape
    rows = patches // 2
    dim = VD // VH
    one = pl.BlockSpec((rows, width), lambda f, _: (0, 0))
    in_specs = [
        pl.BlockSpec((1, rows, width), lambda f, _: (0, part, 0)),
        pl.BlockSpec((1, patches, width), lambda f, _: (1, 0, 0)),
        pl.BlockSpec((1, patches, width), lambda f, _: (2, 0, 0)),
        pl.BlockSpec(memory_space=pl.ANY),
    ]
    out_specs = [one]
    out_shape = [jax.ShapeDtypeStruct((rows, width), jnp.bfloat16)]
    if projection:
        in_specs += [
            one,
            pl.BlockSpec((width, width), lambda f, index: (index[0], 0)),
            pl.BlockSpec((patches, width), lambda f, _: (0, 0)),
        ]
        out_specs += [one, one]
        out_shape += [jax.ShapeDtypeStruct((rows, width), jnp.float32)] * 2
    return pl.pallas_call(
        functools.partial(vit_kernel, heads=width // dim, dim=dim),
        grid_spec=pltpu.PrefetchScalarGridSpec(
            num_scalar_prefetch=1, grid=(1,), in_specs=in_specs, out_specs=out_specs
        ),
        out_shape=out_shape,
        compiler_params=pltpu.CompilerParams(
            vmem_limit_bytes=VMEM_LIMIT
        ),
        cost_estimate=pl.CostEstimate(flops=1024, bytes_accessed=1024, transcendentals=0),
    )(jnp.reshape(tp_index, (1,)), fields, fields, fields, after, *(projection or ()))


def merge_kernel(block_ref, x_ref, w_ref, o_ref, held_ref, rows_ref, sems):
    tokens, columns = o_ref.shape
    patches = x_ref.shape[0]

    def weights_in(j):
        lanes = pl.ds(pl.multiple_of(block_ref[0] * columns, columns), columns)
        return pltpu.make_async_copy(w_ref.at[j, :, lanes], held_ref.at[j], sems.at[j])

    for j in range(4):
        weights_in(j).start()
    token = lax.broadcasted_iota(jnp.int32, (tokens, patches), 0)
    patch = lax.broadcasted_iota(jnp.int32, (tokens, patches), 1)
    for j in range(4):
        pick = jnp.where(patch == 4 * token + j, 1.0, 0.0).astype(jnp.bfloat16)
        rows_ref[j] = jnp.dot(pick, x_ref[...], preferred_element_type=jnp.float32).astype(
            jnp.bfloat16
        )
    total = None
    for j in range(4):
        weights_in(j).wait()
        product = jnp.dot(rows_ref[j], held_ref[j], preferred_element_type=jnp.float32)
        total = product if total is None else total + product
    o_ref[...] = total.astype(o_ref.dtype)


def merged_columns(normed, weights, block, columns, dtype):
    patches, width = normed.shape
    tokens = patches // 4
    return pl.pallas_call(
        merge_kernel,
        in_specs=[
            pl.BlockSpec(memory_space=pltpu.SMEM),
            pl.BlockSpec(memory_space=pltpu.VMEM),
            pl.BlockSpec(memory_space=pl.ANY),
        ],
        out_specs=pl.BlockSpec(memory_space=pltpu.VMEM),
        out_shape=jax.ShapeDtypeStruct((tokens, columns), dtype),
        scratch_shapes=[
            pltpu.VMEM((4, width, columns), jnp.bfloat16),
            pltpu.VMEM((4, tokens, width), jnp.bfloat16),
            pltpu.SemaphoreType.DMA((4,)),
        ],
        compiler_params=pltpu.CompilerParams(vmem_limit_bytes=MERGE_VMEM),
        cost_estimate=pl.CostEstimate(
            flops=2 * tokens * 4 * width * columns,
            bytes_accessed=4 * width * columns * 2 + patches * width * 2,
            transcendentals=0,
        ),
    )(jnp.reshape(block, (1,)), normed, weights)


def tables_kernel(
    device_ref, vis_pos_ref, frame_host_ref, doc_ref, place_ref, *, peers, per_device,
):
    device = device_ref[0]
    rows = peers // 2
    frames = vis_pos_ref.shape[0]
    slots_each = per_device // FT
    first_pos = device * per_device
    starts = [
        jnp.sum(jnp.where(doc_ref[...] < d, 1.0, 0.0)).astype(jnp.int32) for d in range(1, DOCS)
    ]
    for i, value in enumerate([first_pos] + starts):
        place_ref[2 * peers + i] = value

    def block_from(source):
        hop = lax.rem(ring_place(device // 2, rows) + rows - ring_place(source // 2, rows), rows)
        return 2 * hop + jnp.where(lax.rem(source, 2) == lax.rem(device, 2), 0, 1)

    def one_slot(slot, carry):
        frame, before_is_text = carry
        pos = slot * FT
        here = jnp.minimum(frame, frames - 1)
        is_frame = (frame < frames) & (vis_pos_ref[here] == pos)
        owner = slot // slots_each
        second = lax.rem(slot, slots_each) != 0
        partner = lax.rem(owner + peers // 2, peers)
        holder = jnp.where(second & (before_is_text == 1), partner, owner)
        source = jnp.where(is_frame, frame_host_ref[here], holder)
        flag = jnp.where(is_frame, 1, 0)
        place_ref[block_from(source) + peers * flag] = pos
        return frame + flag, 1 - flag

    lax.fori_loop(0, peers * slots_each, one_slot, (jnp.int32(0), jnp.int32(0)))


def tables(device, vis_pos, frame_host, doc_ids, peers, per_device):
    scalars = pl.BlockSpec(memory_space=pltpu.SMEM)
    return pl.pallas_call(
        functools.partial(tables_kernel, peers=peers, per_device=per_device),
        in_specs=[scalars] * 3 + [pl.BlockSpec(memory_space=pltpu.VMEM)],
        out_specs=scalars,
        out_shape=jax.ShapeDtypeStruct((2 * peers + DOCS,), jnp.int32),
    )(jnp.reshape(device, (1,)), vis_pos, frame_host, doc_ids.reshape(-1, LANES))


def attend_kernel(place_ref, q_ref, *rest, slots, heads):
    slot_refs, out_ref = rest[:slots], rest[slots]
    kv_ref, held_q_ref, query_ref, bias_ref, score_ref, max_ref, acc_ref, result_ref = rest[
        slots + 1 : slots + 9
    ]
    slot_sems, query_sems, out_sems = rest[slots + 9 :]
    rows = q_ref.shape[0]
    scale = 1.0 / math.sqrt(HD)
    wide = GROUP * HD
    first_pos = place_ref[slots]
    starts = [place_ref[slots + i] for i in range(1, DOCS)]

    def first_key(pos):
        return functools.reduce(jnp.maximum, [jnp.where(s <= pos, s, 0) for s in starts])

    last = first_pos // rows
    first = first_key(first_pos) // rows
    paired = first + (last - first) % 2
    masked_pairs = (jnp.maximum(first_key(first_pos + rows - 1) - paired * rows, 0) + 2 * rows - 1) // (
        2 * rows
    )
    pairs = (last - paired) // 2
    masked_pairs = jnp.minimum(masked_pairs, pairs)

    cuts = [(0, heads)]

    def slot_copy(i, cut):
        begin, end = cuts[cut]
        lanes = slice(begin * 2 * HD, end * 2 * HD)
        there = pl.ds(pl.multiple_of(place_ref[i], FT), FT)
        return pltpu.make_async_copy(
            slot_refs[i].at[:, lanes], kv_ref.at[there, lanes], slot_sems.at[cut, i]
        )

    def query_copy(cut):
        begin, end = cuts[cut]
        lanes = slice(begin * wide, end * wide)
        return pltpu.make_async_copy(
            q_ref.at[:, lanes], held_q_ref.at[:, lanes], query_sems.at[cut]
        )

    def wanted(i):
        block = place_ref[i] // rows
        return (block >= first) & (block <= last)

    def all_slots(cut, act):
        for i in range(slots):
            pl.when(wanted(i))(functools.partial(act, i, cut))

    for cut in range(len(cuts)):
        query_copy(cut).start()
        all_slots(cut, lambda i, cut: slot_copy(i, cut).start())

    def mask(block):
        query_pos = first_pos + lax.broadcasted_iota(jnp.int32, (rows, FT), 0)
        low = first_key(query_pos)
        for at in range(0, rows, FT):
            key_pos = block * rows + at + lax.broadcasted_iota(jnp.int32, (rows, FT), 1)
            allowed = (key_pos <= query_pos) & (key_pos >= low)
            bias_ref[block, :, at : at + FT] = jnp.where(allowed, 0.0, MASKED)

    pl.loop(first, paired + 2 * masked_pairs)(mask)
    mask(last)

    def result_copy(h):
        return pltpu.make_async_copy(
            result_ref.at[h], out_ref.at[:, h * wide : (h + 1) * wide], out_sems.at[h]
        )

    for cut in range(len(cuts)):
        query_copy(cut).wait()
        all_slots(cut, lambda i, cut: slot_copy(i, cut).wait())
    for h in range(heads):
        for g in range(GROUP):
            at = h * wide + g * HD
            query_ref[h, g * rows : (g + 1) * rows] = held_q_ref[:, at : at + HD]

    def score(block, count, masked, initial):
        here = pl.ds(pl.multiple_of(block * rows, rows), count * rows)
        for h in range(heads):
            keys = kv_ref[here, 2 * h * HD : (2 * h + 1) * HD]
            scores = contract_last(query_ref[h], keys) * scale
            parts = []
            for i in range(count):
                part = scores[:, i * rows : (i + 1) * rows]
                if masked:
                    part = part.reshape(GROUP, rows, rows) + bias_ref[block + i][None]
                    part = part.reshape(GROUP * rows, rows)
                score_ref[h, block + i] = part
                parts += [part[:, at : at + FT] for at in range(0, rows, FT)]
            if not initial:
                parts.append(max_ref[h])
            max_ref[h] = functools.reduce(jnp.maximum, parts)

    def mix(block, count, initial):
        here = pl.ds(pl.multiple_of(block * rows, rows), count * rows)
        for h in range(heads):
            values = kv_ref[here, (2 * h + 1) * HD : (2 * h + 2) * HD]
            values = jnp.concatenate([values, jnp.ones_like(values)], axis=1)
            weights = [
                jnp.exp(score_ref[h, block + i, :, at : at + FT] - max_ref[h]).astype(jnp.bfloat16)
                for i in range(count)
                for at in range(0, rows, FT)
            ]
            weights = jnp.concatenate(weights, axis=1)
            mixed = jnp.dot(weights, values, preferred_element_type=jnp.float32)
            acc_ref[h] = mixed if initial else acc_ref[h] + mixed

    score(last, 1, masked=True, initial=True)

    @pl.when(paired > first)
    def _():
        score(first, 1, masked=True, initial=False)

    @pl.loop(0, masked_pairs)
    def _(pair):
        score(paired + 2 * pair, 2, masked=True, initial=False)

    @pl.loop(masked_pairs, pairs)
    def _(pair):
        score(paired + 2 * pair, 2, masked=False, initial=False)

    for h in range(heads):
        row_max = jnp.max(max_ref[h], axis=1, keepdims=True)
        max_ref[h] = jnp.broadcast_to(row_max, (GROUP * rows, FT))

    mix(last, 1, initial=True)

    @pl.when(paired > first)
    def _():
        mix(first, 1, initial=False)

    @pl.loop(0, pairs)
    def _(pair):
        mix(paired + 2 * pair, 2, initial=False)

    for h in range(heads):
        mixed = acc_ref[h, :, :HD] / acc_ref[h, :, HD:]
        for g in range(GROUP):
            result_ref[h, :, g * HD : (g + 1) * HD] = mixed[g * rows : (g + 1) * rows].astype(
                result_ref.dtype
            )
        result_copy(h).start()
    for h in range(heads):
        result_copy(h).wait()


def attend(queries, slots, place):
    rows = queries.shape[0]
    columns = slots[0].shape[1]
    heads = columns // (2 * HD)
    blocks = len(slots) * FT // rows
    wide = GROUP * HD
    tall = GROUP * rows
    anywhere = pl.BlockSpec(memory_space=pl.ANY)
    scalars = pl.BlockSpec(memory_space=pltpu.SMEM)
    cells = heads * tall * blocks * rows
    return pl.pallas_call(
        functools.partial(attend_kernel, slots=len(slots), heads=heads),
        in_specs=[scalars] + [anywhere] * (1 + len(slots)),
        out_specs=anywhere,
        out_shape=jax.ShapeDtypeStruct(queries.shape, jnp.bfloat16),
        scratch_shapes=[
            pltpu.VMEM((len(slots) * FT, columns), jnp.bfloat16),
            pltpu.VMEM(queries.shape, jnp.bfloat16),
            pltpu.VMEM((heads, tall, HD), jnp.bfloat16),
            pltpu.VMEM((blocks, rows, rows), jnp.float32),
            pltpu.VMEM((heads, blocks, tall, rows), jnp.float32),
            pltpu.VMEM((heads, tall, FT), jnp.float32),
            pltpu.VMEM((heads, tall, 2 * HD), jnp.float32),
            pltpu.VMEM((heads, rows, wide), jnp.bfloat16),
            pltpu.SemaphoreType.DMA((2, len(slots))),
            pltpu.SemaphoreType.DMA((2,)),
            pltpu.SemaphoreType.DMA((heads,)),
        ],
        compiler_params=pltpu.CompilerParams(vmem_limit_bytes=LANGUAGE_VMEM),
        cost_estimate=pl.CostEstimate(
            flops=6 * cells * HD,
            bytes_accessed=2 * len(slots) * FT * columns + 4 * rows * heads * wide,
            transcendentals=cells,
        ),
    )(place, queries, *slots)


def shards(
    vis_qkv,
    vis_resid,
    vis_out_w,
    merge_gain,
    merge_bias,
    vis_kv_w,
    frame_host,
    vis_pos,
    doc_ids,
    text_kv,
    queries,
):
    device = lax.axis_index("ctx")
    tp_index = lax.axis_index("tp")
    tp_size = lax.axis_size("tp")
    per_device = queries.shape[0]
    patches = vis_qkv.shape[0]
    width = vis_qkv.shape[2]
    local_kv = vis_kv_w.shape[2] // tp_size
    positions = doc_ids.shape[0]
    frames = vis_pos.shape[0]

    peers = lax.axis_size("ctx")
    rows = peers // 2
    first_pos = device * per_device

    fields = jnp.transpose(vis_qkv, (1, 0, 2))
    part_count = 2
    part_rows = patches // part_count
    text_high = text_kv[FT:]
    handed = shifted(text_high, "ctx", peers // 2)
    (first_context,) = vit_attention(fields, text_high, 0, tp_index)
    second_context, low_rows, high_rows = vit_attention(
        fields, first_context, 1, tp_index, (first_context, vis_out_w, vis_resid)
    )
    contexts = [first_context, second_context]
    arrived = [
        [shifted(context, "tp", distance) for distance in range(1, tp_size)]
        for context in contexts
    ]

    def out_rows(distance):
        source = lax.rem(tp_after + tp_size - distance, tp_size)
        return lax.dynamic_slice_in_dim(vis_out_w, source * width, width, axis=0)

    vis_pos, text_kv, _ = lax.optimization_barrier((vis_pos, text_kv, second_context))
    first_frame = jnp.any(vis_pos == first_pos)
    second_frame = jnp.any(vis_pos == first_pos + FT)
    text_block = lax.dynamic_slice_in_dim(text_kv, jnp.where(first_frame, FT, 0), FT)
    text_block = text_block.reshape(FT, local_kv)
    handed, text_block, _ = lax.optimization_barrier((handed, text_block, low_rows))
    text_block = jnp.where(
        first_frame & second_frame, handed.reshape(FT, local_kv), text_block
    )
    hidden_parts = [low_rows, high_rows]
    text = Ring(text_block, rows)
    tp_after = tp_index
    for part in range(part_count):
        for distance in range(1, tp_size):
            hidden_parts[part] = hidden_parts[part] + jnp.dot(
                arrived[part][distance - 1], out_rows(distance), preferred_element_type=jnp.float32
            )
        if part == 0:
            tp_after, _ = lax.optimization_barrier((tp_index, hidden_parts[0]))
    hidden = jnp.concatenate(hidden_parts, axis=0)
    sums = jnp.stack([jnp.sum(hidden, axis=1), jnp.sum(hidden * hidden, axis=1)])
    others = [shifted(sums, "tp", distance) for distance in range(1, tp_size)]
    sums = text.advance(sums)
    row_sum, row_squares = functools.reduce(jnp.add, others, sums)
    mean_value = row_sum / VD
    variance = row_squares / VD - mean_value * mean_value
    normed = (hidden - mean_value[:, None]) * lax.rsqrt(variance + 1e-06)[
        :, None
    ] * merge_gain + merge_bias
    normed = normed.astype(jnp.bfloat16)

    received = []
    for distance in range(1, tp_size):
        block = lax.rem(tp_index + distance, tp_size)
        part = merged_columns(normed, vis_kv_w, block, local_kv, jnp.bfloat16)
        received.append(shifted(part, "tp", distance))
    own = merged_columns(normed, vis_kv_w, tp_index, local_kv, jnp.float32)
    own = text.advance(own)
    for part in received:
        own = own + part.astype(jnp.float32)
    own = own.astype(jnp.bfloat16)
    vision = Ring(own, rows)
    vis_pos, own = lax.optimization_barrier((vis_pos, own))
    place = tables(device, vis_pos, frame_host, doc_ids, peers, per_device)
    for hop in range(1, rows):
        if hop == 1:
            vision.moving, place = text.advance((vision.moving, place))
        vision.advance((), lag=1)
    return attend(queries, text.all() + vision.all(), place)


def solution(mesh):
    return jax.shard_map(
        shards,
        mesh=mesh,
        in_specs=(
            P(("dp", "ctx"), None, "tp"),
            P(("dp", "ctx"), "tp"),
            P(None, "tp"),
            P("tp"),
            P("tp"),
            P(None, "tp", None),
            P("dp"),
            P("dp"),
            P("dp"),
            P(("dp", "ctx"), "tp", None, None),
            P(("dp", "ctx"), "tp"),
        ),
        out_specs=P(("dp", "ctx"), "tp"),
        check_vma=False,
    )
```

```python
import functools
import math

import jax
import jax.numpy as jnp
from jax import lax
from jax.experimental import pallas as pl
from jax.experimental.pallas import tpu as pltpu
from jax.sharding import PartitionSpec as P

VD = 1280
VH = 16
HD = 128
H = 32
KVH = 8
FT = 128
GROUP = H // KVH
DOCS = 4
LANES = 128

MASKED = -1e30
VMEM_LIMIT = 16 * 1024 * 1024
MERGE_VMEM = 52 * 1024 * 1024
LANGUAGE_VMEM = 58 * 1024 * 1024


def contract_last(a, b):
    return lax.dot_general(a, b, (((1,), (1,)), ((), ())), preferred_element_type=jnp.float32)


def shifted(block, axis, distance):
    count = lax.axis_size(axis)
    return lax.ppermute(block, axis, [(i, (i + distance) % count) for i in range(count)])


def ring_place(row, rows):
    return jnp.where(row % 2 == 1, (row + 1) // 2, (rows - row // 2) % rows)


def to_next_row(block, rows):
    order = [0] + list(range(1, rows, 2)) + list(range(rows - 2, 0, -2))
    after = dict(zip(order, order[1:] + order[:1]))
    return lax.ppermute(
        block,
        "ctx",
        [(2 * row + side, 2 * after[row] + side) for row in range(rows) for side in range(2)],
    )


def to_other_side(block, rows):
    return lax.ppermute(
        block, "ctx", [(2 * row + side, 2 * row + 1 - side) for row in range(rows) for side in range(2)]
    )


class Ring:
    def __init__(self, block, rows):
        self.rows = rows
        self.blocks = [block]
        self.start(block)

    def start(self, block):
        self.moving = to_next_row(block, self.rows) if len(self.blocks) < 2 * self.rows - 1 else None
        self.blocks.append(to_other_side(block, self.rows))

    def advance(self, beside, lag=0):
        if self.moving is None:
            return beside
        if len(self.blocks) > 2 * lag:
            at = len(self.blocks) - 1 - 2 * lag
            held, self.blocks[at], beside = lax.optimization_barrier(
                (self.moving, self.blocks[at], beside)
            )
        else:
            held, beside = lax.optimization_barrier((self.moving, beside))
        self.blocks.append(held)
        self.start(held)
        return beside

    def all(self):
        while self.moving is not None:
            self.advance(())
        return self.blocks


def vit_kernel(index_ref, q_ref, k_ref, v_ref, after_ref, *rest, heads, dim):
    o_ref = rest[0]
    if len(rest) > 1:
        earlier_ref, weight_ref, resid_ref, o_ref, low_ref, high_ref = rest
    width = q_ref.shape[2]
    to_exp = 1.0 / math.sqrt(dim)
    tiles = {}
    for g in range(heads):
        first, last = g * dim, (g + 1) * dim
        low = first // LANES * LANES
        high = min(width, -(-last // LANES) * LANES)
        lane = lax.broadcasted_iota(jnp.int32, (1, high - low), 1) + low
        inside = (lane >= first) & (lane < last)
        keep = jnp.where(inside, 1.0, 0.0).astype(jnp.bfloat16)
        other = jnp.where(inside, 0.0, 1.0).astype(jnp.bfloat16)
        scores = contract_last(q_ref[0, :, low:high] * keep, k_ref[0, :, low:high])
        row_max = jnp.max(scores, axis=1, keepdims=True)
        weights = jnp.exp((scores - row_max) * to_exp).astype(jnp.bfloat16)
        mixed = jnp.dot(
            weights, v_ref[0, :, low:high] * keep + other, preferred_element_type=jnp.float32
        )
        spare = 0 if low < first else last - low
        mixed = mixed / mixed[:, spare : spare + 1]
        for at in range(low, high, LANES):
            end = min(at + LANES, high)
            piece = mixed[:, at - low : end - low]
            if at in tiles:
                piece = jnp.where(inside[:, at - low : end - low], piece, tiles[at])
            tiles[at] = piece
    for at, piece in tiles.items():
        o_ref[:, at : at + piece.shape[1]] = piece.astype(o_ref.dtype)
    if len(rest) > 1:
        rows = o_ref.shape[0]
        for part, (context, hidden_ref) in enumerate([(earlier_ref, low_ref), (o_ref, high_ref)]):
            here = slice(part * rows, (part + 1) * rows)
            hidden_ref[...] = resid_ref[here].astype(jnp.float32) + jnp.dot(
                context[...], weight_ref[...], preferred_element_type=jnp.float32
            )


def vit_attention(fields, after, part, tp_index, projection=None):
    _, patches, width = fields.shape
    rows = patches // 2
    dim = VD // VH
    one = pl.BlockSpec((rows, width), lambda f, _: (0, 0))
    in_specs = [
        pl.BlockSpec((1, rows, width), lambda f, _: (0, part, 0)),
        pl.BlockSpec((1, patches, width), lambda f, _: (1, 0, 0)),
        pl.BlockSpec((1, patches, width), lambda f, _: (2, 0, 0)),
        pl.BlockSpec(memory_space=pl.ANY),
    ]
    out_specs = [one]
    out_shape = [jax.ShapeDtypeStruct((rows, width), jnp.bfloat16)]
    if projection:
        in_specs += [
            one,
            pl.BlockSpec((width, width), lambda f, index: (index[0], 0)),
            pl.BlockSpec((patches, width), lambda f, _: (0, 0)),
        ]
        out_specs += [one, one]
        out_shape += [jax.ShapeDtypeStruct((rows, width), jnp.float32)] * 2
    return pl.pallas_call(
        functools.partial(vit_kernel, heads=width // dim, dim=dim),
        grid_spec=pltpu.PrefetchScalarGridSpec(
            num_scalar_prefetch=1, grid=(1,), in_specs=in_specs, out_specs=out_specs
        ),
        out_shape=out_shape,
        compiler_params=pltpu.CompilerParams(
            vmem_limit_bytes=VMEM_LIMIT
        ),
        cost_estimate=pl.CostEstimate(flops=1024, bytes_accessed=1024, transcendentals=0),
    )(jnp.reshape(tp_index, (1,)), fields, fields, fields, after, *(projection or ()))


def merge_kernel(block_ref, x_ref, w_ref, o_ref, held_ref, rows_ref, sems):
    tokens, columns = o_ref.shape
    patches = x_ref.shape[0]

    def weights_in(j):
        lanes = pl.ds(pl.multiple_of(block_ref[0] * columns, columns), columns)
        return pltpu.make_async_copy(w_ref.at[j, :, lanes], held_ref.at[j], sems.at[j])

    for j in range(4):
        weights_in(j).start()
    token = lax.broadcasted_iota(jnp.int32, (tokens, patches), 0)
    patch = lax.broadcasted_iota(jnp.int32, (tokens, patches), 1)
    for j in range(4):
        pick = jnp.where(patch == 4 * token + j, 1.0, 0.0).astype(jnp.bfloat16)
        rows_ref[j] = jnp.dot(pick, x_ref[...], preferred_element_type=jnp.float32).astype(
            jnp.bfloat16
        )
    total = None
    for j in range(4):
        weights_in(j).wait()
        product = jnp.dot(rows_ref[j], held_ref[j], preferred_element_type=jnp.float32)
        total = product if total is None else total + product
    o_ref[...] = total.astype(o_ref.dtype)


def merged_columns(normed, weights, block, columns, dtype):
    patches, width = normed.shape
    tokens = patches // 4
    return pl.pallas_call(
        merge_kernel,
        in_specs=[
            pl.BlockSpec(memory_space=pltpu.SMEM),
            pl.BlockSpec(memory_space=pltpu.VMEM),
            pl.BlockSpec(memory_space=pl.ANY),
        ],
        out_specs=pl.BlockSpec(memory_space=pltpu.VMEM),
        out_shape=jax.ShapeDtypeStruct((tokens, columns), dtype),
        scratch_shapes=[
            pltpu.VMEM((4, width, columns), jnp.bfloat16),
            pltpu.VMEM((4, tokens, width), jnp.bfloat16),
            pltpu.SemaphoreType.DMA((4,)),
        ],
        compiler_params=pltpu.CompilerParams(vmem_limit_bytes=MERGE_VMEM),
        cost_estimate=pl.CostEstimate(
            flops=2 * tokens * 4 * width * columns,
            bytes_accessed=4 * width * columns * 2 + patches * width * 2,
            transcendentals=0,
        ),
    )(jnp.reshape(block, (1,)), normed, weights)


def tables_kernel(
    device_ref, vis_pos_ref, frame_host_ref, doc_ref, place_ref, *, peers, per_device,
):
    device = device_ref[0]
    rows = peers // 2
    frames = vis_pos_ref.shape[0]
    slots_each = per_device // FT
    first_pos = device * per_device
    starts = [
        jnp.sum(jnp.where(doc_ref[...] < d, 1.0, 0.0)).astype(jnp.int32) for d in range(1, DOCS)
    ]
    for i, value in enumerate([first_pos] + starts):
        place_ref[2 * peers + i] = value

    def block_from(source):
        hop = lax.rem(ring_place(device // 2, rows) + rows - ring_place(source // 2, rows), rows)
        return 2 * hop + jnp.where(lax.rem(source, 2) == lax.rem(device, 2), 0, 1)

    def one_slot(slot, carry):
        frame, before_is_text = carry
        pos = slot * FT
        here = jnp.minimum(frame, frames - 1)
        is_frame = (frame < frames) & (vis_pos_ref[here] == pos)
        owner = slot // slots_each
        second = lax.rem(slot, slots_each) != 0
        partner = lax.rem(owner + peers // 2, peers)
        holder = jnp.where(second & (before_is_text == 1), partner, owner)
        source = jnp.where(is_frame, frame_host_ref[here], holder)
        flag = jnp.where(is_frame, 1, 0)
        place_ref[block_from(source) + peers * flag] = pos
        return frame + flag, 1 - flag

    lax.fori_loop(0, peers * slots_each, one_slot, (jnp.int32(0), jnp.int32(0)))


def tables(device, vis_pos, frame_host, doc_ids, peers, per_device):
    scalars = pl.BlockSpec(memory_space=pltpu.SMEM)
    return pl.pallas_call(
        functools.partial(tables_kernel, peers=peers, per_device=per_device),
        in_specs=[scalars] * 3 + [pl.BlockSpec(memory_space=pltpu.VMEM)],
        out_specs=scalars,
        out_shape=jax.ShapeDtypeStruct((2 * peers + DOCS,), jnp.int32),
    )(jnp.reshape(device, (1,)), vis_pos, frame_host, doc_ids.reshape(-1, LANES))


def attend_kernel(place_ref, q_ref, *rest, slots, heads):
    slot_refs, out_ref = rest[:slots], rest[slots]
    kv_ref, held_q_ref, query_ref, bias_ref, score_ref, max_ref, acc_ref, result_ref = rest[
        slots + 1 : slots + 9
    ]
    slot_sems, query_sems, out_sems = rest[slots + 9 :]
    rows = q_ref.shape[0]
    scale = 1.0 / math.sqrt(HD)
    wide = GROUP * HD
    first_pos = place_ref[slots]
    starts = [place_ref[slots + i] for i in range(1, DOCS)]

    def first_key(pos):
        return functools.reduce(jnp.maximum, [jnp.where(s <= pos, s, 0) for s in starts])

    last = first_pos // rows
    first = first_key(first_pos) // rows
    paired = first + (last - first) % 2
    masked_pairs = (jnp.maximum(first_key(first_pos + rows - 1) - paired * rows, 0) + 2 * rows - 1) // (
        2 * rows
    )
    pairs = (last - paired) // 2
    masked_pairs = jnp.minimum(masked_pairs, pairs)

    cuts = [(0, heads)]

    def slot_copy(i, cut):
        begin, end = cuts[cut]
        lanes = slice(begin * 2 * HD, end * 2 * HD)
        there = pl.ds(pl.multiple_of(place_ref[i], FT), FT)
        return pltpu.make_async_copy(
            slot_refs[i].at[:, lanes], kv_ref.at[there, lanes], slot_sems.at[cut, i]
        )

    def query_copy(cut):
        begin, end = cuts[cut]
        lanes = slice(begin * wide, end * wide)
        return pltpu.make_async_copy(
            q_ref.at[:, lanes], held_q_ref.at[:, lanes], query_sems.at[cut]
        )

    def wanted(i):
        block = place_ref[i] // rows
        return (block >= first) & (block <= last)

    def all_slots(cut, act):
        for i in range(slots):
            pl.when(wanted(i))(functools.partial(act, i, cut))

    for cut in range(len(cuts)):
        query_copy(cut).start()
        all_slots(cut, lambda i, cut: slot_copy(i, cut).start())

    def mask(block):
        query_pos = first_pos + lax.broadcasted_iota(jnp.int32, (rows, FT), 0)
        low = first_key(query_pos)
        for at in range(0, rows, FT):
            key_pos = block * rows + at + lax.broadcasted_iota(jnp.int32, (rows, FT), 1)
            allowed = (key_pos <= query_pos) & (key_pos >= low)
            bias_ref[block, :, at : at + FT] = jnp.where(allowed, 0.0, MASKED)

    pl.loop(first, paired + 2 * masked_pairs)(mask)
    mask(last)

    def result_copy(h):
        return pltpu.make_async_copy(
            result_ref.at[h], out_ref.at[:, h * wide : (h + 1) * wide], out_sems.at[h]
        )

    for cut in range(len(cuts)):
        query_copy(cut).wait()
        all_slots(cut, lambda i, cut: slot_copy(i, cut).wait())
    for h in range(heads):
        for g in range(GROUP):
            at = h * wide + g * HD
            query_ref[h, g * rows : (g + 1) * rows] = held_q_ref[:, at : at + HD]

    def score(block, count, masked, initial):
        here = pl.ds(pl.multiple_of(block * rows, rows), count * rows)
        for h in range(heads):
            keys = kv_ref[here, 2 * h * HD : (2 * h + 1) * HD]
            scores = contract_last(query_ref[h], keys) * scale
            parts = []
            for i in range(count):
                part = scores[:, i * rows : (i + 1) * rows]
                if masked:
                    part = part.reshape(GROUP, rows, rows) + bias_ref[block + i][None]
                    part = part.reshape(GROUP * rows, rows)
                score_ref[h, block + i] = part
                parts += [part[:, at : at + FT] for at in range(0, rows, FT)]
            if not initial:
                parts.append(max_ref[h])
            max_ref[h] = functools.reduce(jnp.maximum, parts)

    def mix(block, count, initial):
        here = pl.ds(pl.multiple_of(block * rows, rows), count * rows)
        for h in range(heads):
            values = kv_ref[here, (2 * h + 1) * HD : (2 * h + 2) * HD]
            values = jnp.concatenate([values, jnp.ones_like(values)], axis=1)
            weights = [
                jnp.exp(score_ref[h, block + i, :, at : at + FT] - max_ref[h]).astype(jnp.bfloat16)
                for i in range(count)
                for at in range(0, rows, FT)
            ]
            weights = jnp.concatenate(weights, axis=1)
            mixed = jnp.dot(weights, values, preferred_element_type=jnp.float32)
            acc_ref[h] = mixed if initial else acc_ref[h] + mixed

    score(last, 1, masked=True, initial=True)

    @pl.when(paired > first)
    def _():
        score(first, 1, masked=True, initial=False)

    @pl.loop(0, masked_pairs)
    def _(pair):
        score(paired + 2 * pair, 2, masked=True, initial=False)

    @pl.loop(masked_pairs, pairs)
    def _(pair):
        score(paired + 2 * pair, 2, masked=False, initial=False)

    for h in range(heads):
        row_max = jnp.max(max_ref[h], axis=1, keepdims=True)
        max_ref[h] = jnp.broadcast_to(row_max, (GROUP * rows, FT))

    mix(last, 1, initial=True)

    @pl.when(paired > first)
    def _():
        mix(first, 1, initial=False)

    @pl.loop(0, pairs)
    def _(pair):
        mix(paired + 2 * pair, 2, initial=False)

    for h in range(heads):
        mixed = acc_ref[h, :, :HD] / acc_ref[h, :, HD:]
        for g in range(GROUP):
            result_ref[h, :, g * HD : (g + 1) * HD] = mixed[g * rows : (g + 1) * rows].astype(
                result_ref.dtype
            )
        result_copy(h).start()
    for h in range(heads):
        result_copy(h).wait()


def attend(queries, slots, place):
    rows = queries.shape[0]
    columns = slots[0].shape[1]
    heads = columns // (2 * HD)
    blocks = len(slots) * FT // rows
    wide = GROUP * HD
    tall = GROUP * rows
    anywhere = pl.BlockSpec(memory_space=pl.ANY)
    scalars = pl.BlockSpec(memory_space=pltpu.SMEM)
    cells = heads * tall * blocks * rows
    return pl.pallas_call(
        functools.partial(attend_kernel, slots=len(slots), heads=heads),
        in_specs=[scalars] + [anywhere] * (1 + len(slots)),
        out_specs=anywhere,
        out_shape=jax.ShapeDtypeStruct(queries.shape, jnp.bfloat16),
        scratch_shapes=[
            pltpu.VMEM((len(slots) * FT, columns), jnp.bfloat16),
            pltpu.VMEM(queries.shape, jnp.bfloat16),
            pltpu.VMEM((heads, tall, HD), jnp.bfloat16),
            pltpu.VMEM((blocks, rows, rows), jnp.float32),
            pltpu.VMEM((heads, blocks, tall, rows), jnp.float32),
            pltpu.VMEM((heads, tall, FT), jnp.float32),
            pltpu.VMEM((heads, tall, 2 * HD), jnp.float32),
            pltpu.VMEM((heads, rows, wide), jnp.bfloat16),
            pltpu.SemaphoreType.DMA((2, len(slots))),
            pltpu.SemaphoreType.DMA((2,)),
            pltpu.SemaphoreType.DMA((heads,)),
        ],
        compiler_params=pltpu.CompilerParams(vmem_limit_bytes=LANGUAGE_VMEM),
        cost_estimate=pl.CostEstimate(
            flops=6 * cells * HD,
            bytes_accessed=2 * len(slots) * FT * columns + 4 * rows * heads * wide,
            transcendentals=cells,
        ),
    )(place, queries, *slots)


def shards(
    vis_qkv,
    vis_resid,
    vis_out_w,
    merge_gain,
    merge_bias,
    vis_kv_w,
    frame_host,
    vis_pos,
    doc_ids,
    text_kv,
    queries,
):
    device = lax.axis_index("ctx")
    tp_index = lax.axis_index("tp")
    tp_size = lax.axis_size("tp")
    per_device = queries.shape[0]
    patches = vis_qkv.shape[0]
    width = vis_qkv.shape[2]
    local_kv = vis_kv_w.shape[2] // tp_size
    positions = doc_ids.shape[0]
    frames = vis_pos.shape[0]

    peers = lax.axis_size("ctx")
    rows = peers // 2
    first_pos = device * per_device

    fields = jnp.transpose(vis_qkv, (1, 0, 2))
    part_count = 2
    part_rows = patches // part_count
    text_high = text_kv[FT:]
    handed = shifted(text_high, "ctx", peers // 2)
    (first_context,) = vit_attention(fields, text_high, 0, tp_index)
    second_context, low_rows, high_rows = vit_attention(
        fields, first_context, 1, tp_index, (first_context, vis_out_w, vis_resid)
    )
    contexts = [first_context, second_context]
    arrived = [
        [shifted(context, "tp", distance) for distance in range(1, tp_size)]
        for context in contexts
    ]

    def out_rows(distance):
        source = lax.rem(tp_after + tp_size - distance, tp_size)
        return lax.dynamic_slice_in_dim(vis_out_w, source * width, width, axis=0)

    vis_pos, text_kv, _ = lax.optimization_barrier((vis_pos, text_kv, second_context))
    first_frame = jnp.any(vis_pos == first_pos)
    second_frame = jnp.any(vis_pos == first_pos + FT)
    text_block = lax.dynamic_slice_in_dim(text_kv, jnp.where(first_frame, FT, 0), FT)
    handed, text_block, _ = lax.optimization_barrier((handed, text_block, low_rows))
    text_block = jnp.where(first_frame & second_frame, handed, text_block)
    hidden_parts = [low_rows, high_rows]
    text = Ring(text_block, rows)
    tp_after = tp_index
    for part in range(part_count):
        for distance in range(1, tp_size):
            hidden_parts[part] = hidden_parts[part] + jnp.dot(
                arrived[part][distance - 1], out_rows(distance), preferred_element_type=jnp.float32
            )
        if part == 0:
            tp_after, _ = lax.optimization_barrier((tp_index, hidden_parts[0]))
    hidden = jnp.concatenate(hidden_parts, axis=0)
    sums = jnp.stack([jnp.sum(hidden, axis=1), jnp.sum(hidden * hidden, axis=1)])
    others = [shifted(sums, "tp", distance) for distance in range(1, tp_size)]
    sums = text.advance(sums)
    row_sum, row_squares = functools.reduce(jnp.add, others, sums)
    mean_value = row_sum / VD
    variance = row_squares / VD - mean_value * mean_value
    normed = (hidden - mean_value[:, None]) * lax.rsqrt(variance + 1e-06)[
        :, None
    ] * merge_gain + merge_bias
    normed = normed.astype(jnp.bfloat16)

    received = []
    for distance in range(1, tp_size):
        block = lax.rem(tp_index + distance, tp_size)
        part = merged_columns(normed, vis_kv_w, block, local_kv, jnp.bfloat16)
        received.append(shifted(part, "tp", distance))
    own = merged_columns(normed, vis_kv_w, tp_index, local_kv, jnp.float32)
    own = text.advance(own)
    for part in received:
        own = own + part.astype(jnp.float32)
    own = own.astype(jnp.bfloat16)
    vision = Ring(own, rows)
    vis_pos, own = lax.optimization_barrier((vis_pos, own))
    place = tables(device, vis_pos, frame_host, doc_ids, peers, per_device)
    def laid(blocks, beside):
        come, _ = lax.optimization_barrier((blocks, beside))
        return [block.reshape(FT, local_kv) for block in come]

    texts, fresh = [], []
    for hop in range(1, rows):
        if hop == 1:
            vision.moving, place = text.advance((vision.moving, place))
        fresh = vision.advance(fresh, lag=1)
        texts += fresh
        ready = 2 * rows - 1 if hop > 1 else min(4, 2 * rows - 1)
        fresh = laid(text.blocks[len(texts) : ready], vision.blocks[-2])
    texts += fresh
    texts += laid(text.all()[len(texts) :], vision.blocks[-2])
    return attend(queries, texts + vision.all(), place)


def solution(mesh):
    return jax.shard_map(
        shards,
        mesh=mesh,
        in_specs=(
            P(("dp", "ctx"), None, "tp"),
            P(("dp", "ctx"), "tp"),
            P(None, "tp"),
            P("tp"),
            P("tp"),
            P(None, "tp", None),
            P("dp"),
            P("dp"),
            P("dp"),
            P(("dp", "ctx"), "tp", None, None),
            P(("dp", "ctx"), "tp"),
        ),
        out_specs=P(("dp", "ctx"), "tp"),
        check_vma=False,
    )
```

```python
import functools
import math

import jax
import jax.numpy as jnp
from jax import lax
from jax.experimental import pallas as pl
from jax.experimental.pallas import tpu as pltpu
from jax.sharding import PartitionSpec as P

VD = 1280
VH = 16
HD = 128
H = 32
KVH = 8
FT = 128
GROUP = H // KVH
DOCS = 4
LANES = 128

MASKED = -1e30
VMEM_LIMIT = 16 * 1024 * 1024
MERGE_VMEM = 52 * 1024 * 1024
LANGUAGE_VMEM = 54 * 1024 * 1024


def contract_last(a, b):
    return lax.dot_general(a, b, (((1,), (1,)), ((), ())), preferred_element_type=jnp.float32)


def shifted(block, axis, distance):
    count = lax.axis_size(axis)
    return lax.ppermute(block, axis, [(i, (i + distance) % count) for i in range(count)])


def ring_place(row, rows):
    return jnp.where(row % 2 == 1, (row + 1) // 2, (rows - row // 2) % rows)


def to_next_row(block, rows):
    order = [0] + list(range(1, rows, 2)) + list(range(rows - 2, 0, -2))
    after = dict(zip(order, order[1:] + order[:1]))
    return lax.ppermute(
        block,
        "ctx",
        [(2 * row + side, 2 * after[row] + side) for row in range(rows) for side in range(2)],
    )


def to_other_side(block, rows):
    return lax.ppermute(
        block, "ctx", [(2 * row + side, 2 * row + 1 - side) for row in range(rows) for side in range(2)]
    )


class Ring:
    def __init__(self, block, rows):
        self.rows = rows
        self.blocks = [block]
        self.start(block)

    def start(self, block):
        self.moving = to_next_row(block, self.rows) if len(self.blocks) < 2 * self.rows - 1 else None
        self.blocks.append(to_other_side(block, self.rows))

    def advance(self, beside, lag=0):
        if self.moving is None:
            return beside
        if len(self.blocks) > 2 * lag:
            at = len(self.blocks) - 1 - 2 * lag
            held, self.blocks[at], beside = lax.optimization_barrier(
                (self.moving, self.blocks[at], beside)
            )
        else:
            held, beside = lax.optimization_barrier((self.moving, beside))
        self.blocks.append(held)
        self.start(held)
        return beside

    def all(self):
        while self.moving is not None:
            self.advance(())
        return self.blocks


def vit_kernel(index_ref, q_ref, k_ref, v_ref, after_ref, *rest, first_row, heads, dim):
    o_ref = rest[0]
    if len(rest) > 1:
        earlier_ref, weight_ref, resid_ref, o_ref, low_ref, high_ref = rest
    rows, width = o_ref.shape
    to_exp = 1.0 / math.sqrt(dim)
    tiles = {}
    for g in range(heads):
        first, last = g * dim, (g + 1) * dim
        low = first // LANES * LANES
        high = min(width, -(-last // LANES) * LANES)
        lane = lax.broadcasted_iota(jnp.int32, (1, high - low), 1) + low
        inside = (lane >= first) & (lane < last)
        keep = jnp.where(inside, 1.0, 0.0).astype(jnp.bfloat16)
        other = jnp.where(inside, 0.0, 1.0).astype(jnp.bfloat16)
        scores = contract_last(
            q_ref[0, first_row : first_row + rows, low:high] * keep, k_ref[0, :, low:high]
        )
        row_max = jnp.max(scores, axis=1, keepdims=True)
        weights = jnp.exp((scores - row_max) * to_exp).astype(jnp.bfloat16)
        mixed = jnp.dot(
            weights, v_ref[0, :, low:high] * keep + other, preferred_element_type=jnp.float32
        )
        spare = 0 if low < first else last - low
        mixed = mixed / mixed[:, spare : spare + 1]
        for at in range(low, high, LANES):
            end = min(at + LANES, high)
            piece = mixed[:, at - low : end - low]
            if at in tiles:
                piece = jnp.where(inside[:, at - low : end - low], piece, tiles[at])
            tiles[at] = piece
    for at, piece in tiles.items():
        o_ref[:, at : at + piece.shape[1]] = piece.astype(o_ref.dtype)
    if len(rest) > 1:
        for start, context, hidden_ref in ((0, earlier_ref, low_ref), (first_row, o_ref, high_ref)):
            here = slice(start, start + hidden_ref.shape[0])
            hidden_ref[...] = resid_ref[here].astype(jnp.float32) + jnp.dot(
                context[...], weight_ref[...], preferred_element_type=jnp.float32
            )


def vit_attention(fields, after, part, tp_index, projection=None):
    _, patches, width = fields.shape
    quarter = patches // 4
    first_row, rows = (0, quarter) if part == 0 else (quarter, patches - quarter)
    dim = VD // VH
    one = pl.BlockSpec((rows, width), lambda f, _: (0, 0))
    in_specs = [
        pl.BlockSpec((1, patches, width), lambda f, _: (0, 0, 0)),
        pl.BlockSpec((1, patches, width), lambda f, _: (1, 0, 0)),
        pl.BlockSpec((1, patches, width), lambda f, _: (2, 0, 0)),
        pl.BlockSpec(memory_space=pl.ANY),
    ]
    out_specs = [one]
    out_shape = [jax.ShapeDtypeStruct((rows, width), jnp.bfloat16)]
    if projection:
        in_specs += [
            pl.BlockSpec((first_row, width), lambda f, _: (0, 0)),
            pl.BlockSpec((width, width), lambda f, index: (index[0], 0)),
            pl.BlockSpec((patches, width), lambda f, _: (0, 0)),
        ]
        out_specs += [pl.BlockSpec((first_row, width), lambda f, _: (0, 0)), one]
        out_shape += [jax.ShapeDtypeStruct((n, width), jnp.float32) for n in (first_row, rows)]
    return pl.pallas_call(
        functools.partial(vit_kernel, first_row=first_row, heads=width // dim, dim=dim),
        grid_spec=pltpu.PrefetchScalarGridSpec(
            num_scalar_prefetch=1, grid=(1,), in_specs=in_specs, out_specs=out_specs
        ),
        out_shape=out_shape,
        compiler_params=pltpu.CompilerParams(
            vmem_limit_bytes=VMEM_LIMIT
        ),
        cost_estimate=pl.CostEstimate(flops=1024, bytes_accessed=1024, transcendentals=0),
    )(jnp.reshape(tp_index, (1,)), fields, fields, fields, after, *(projection or ()))


def merge_kernel(block_ref, x_ref, w_ref, o_ref, held_ref, rows_ref, sems):
    tokens, columns = o_ref.shape
    patches = x_ref.shape[0]

    def weights_in(j):
        lanes = pl.ds(pl.multiple_of(block_ref[0] * columns, columns), columns)
        return pltpu.make_async_copy(w_ref.at[j, :, lanes], held_ref.at[j], sems.at[j])

    for j in range(4):
        weights_in(j).start()
    token = lax.broadcasted_iota(jnp.int32, (tokens, patches), 0)
    patch = lax.broadcasted_iota(jnp.int32, (tokens, patches), 1)
    for j in range(4):
        pick = jnp.where(patch == 4 * token + j, 1.0, 0.0).astype(jnp.bfloat16)
        rows_ref[j] = jnp.dot(pick, x_ref[...], preferred_element_type=jnp.float32).astype(
            jnp.bfloat16
        )
    total = None
    for j in range(4):
        weights_in(j).wait()
        product = jnp.dot(rows_ref[j], held_ref[j], preferred_element_type=jnp.float32)
        total = product if total is None else total + product
    o_ref[...] = total.astype(o_ref.dtype)


def merged_columns(normed, weights, block, columns, dtype):
    patches, width = normed.shape
    tokens = patches // 4
    return pl.pallas_call(
        merge_kernel,
        in_specs=[
            pl.BlockSpec(memory_space=pltpu.SMEM),
            pl.BlockSpec(memory_space=pltpu.VMEM),
            pl.BlockSpec(memory_space=pl.ANY),
        ],
        out_specs=pl.BlockSpec(memory_space=pltpu.VMEM),
        out_shape=jax.ShapeDtypeStruct((tokens, columns), dtype),
        scratch_shapes=[
            pltpu.VMEM((4, width, columns), jnp.bfloat16),
            pltpu.VMEM((4, tokens, width), jnp.bfloat16),
            pltpu.SemaphoreType.DMA((4,)),
        ],
        compiler_params=pltpu.CompilerParams(vmem_limit_bytes=MERGE_VMEM),
        cost_estimate=pl.CostEstimate(
            flops=2 * tokens * 4 * width * columns,
            bytes_accessed=4 * width * columns * 2 + patches * width * 2,
            transcendentals=0,
        ),
    )(jnp.reshape(block, (1,)), normed, weights)


def tables_kernel(
    device_ref, vis_pos_ref, frame_host_ref, doc_ref, place_ref, *, peers, per_device,
):
    device = device_ref[0]
    rows = peers // 2
    frames = vis_pos_ref.shape[0]
    slots_each = per_device // FT
    first_pos = device * per_device
    starts = [
        jnp.sum(jnp.where(doc_ref[...] < d, 1.0, 0.0)).astype(jnp.int32) for d in range(1, DOCS)
    ]
    for i, value in enumerate([first_pos] + starts):
        place_ref[2 * peers + i] = value

    def block_from(source):
        hop = lax.rem(ring_place(device // 2, rows) + rows - ring_place(source // 2, rows), rows)
        return 2 * hop + jnp.where(lax.rem(source, 2) == lax.rem(device, 2), 0, 1)

    def one_slot(slot, carry):
        frame, before_is_text = carry
        pos = slot * FT
        here = jnp.minimum(frame, frames - 1)
        is_frame = (frame < frames) & (vis_pos_ref[here] == pos)
        owner = slot // slots_each
        second = lax.rem(slot, slots_each) != 0
        partner = lax.rem(owner + peers // 2, peers)
        holder = jnp.where(second & (before_is_text == 1), partner, owner)
        source = jnp.where(is_frame, frame_host_ref[here], holder)
        flag = jnp.where(is_frame, 1, 0)
        place_ref[block_from(source) + peers * flag] = pos
        return frame + flag, 1 - flag

    lax.fori_loop(0, peers * slots_each, one_slot, (jnp.int32(0), jnp.int32(0)))


def tables(device, vis_pos, frame_host, doc_ids, peers, per_device):
    scalars = pl.BlockSpec(memory_space=pltpu.SMEM)
    return pl.pallas_call(
        functools.partial(tables_kernel, peers=peers, per_device=per_device),
        in_specs=[scalars] * 3 + [pl.BlockSpec(memory_space=pltpu.VMEM)],
        out_specs=scalars,
        out_shape=jax.ShapeDtypeStruct((2 * peers + DOCS,), jnp.int32),
    )(jnp.reshape(device, (1,)), vis_pos, frame_host, doc_ids.reshape(-1, LANES))


def attend_kernel(place_ref, q_ref, *rest, slots, heads):
    slot_refs, out_ref = rest[:slots], rest[slots]
    kv_ref, held_q_ref, query_ref, bias_ref, score_ref, max_ref, acc_ref, result_ref = rest[
        slots + 1 : slots + 9
    ]
    slot_sems, query_sems, out_sems = rest[slots + 9 :]
    rows = q_ref.shape[0]
    scale = 1.0 / math.sqrt(HD)
    wide = GROUP * HD
    first_pos = place_ref[slots]
    starts = [place_ref[slots + i] for i in range(1, DOCS)]

    def first_key(pos):
        return functools.reduce(jnp.maximum, [jnp.where(s <= pos, s, 0) for s in starts])

    last = first_pos // rows
    first = first_key(first_pos) // rows
    paired = first + (last - first) % 2
    masked_pairs = (jnp.maximum(first_key(first_pos + rows - 1) - paired * rows, 0) + 2 * rows - 1) // (
        2 * rows
    )
    pairs = (last - paired) // 2
    masked_pairs = jnp.minimum(masked_pairs, pairs)

    cuts = [(0, heads)]

    def slot_copy(i, cut):
        begin, end = cuts[cut]
        lanes = slice(begin * 2 * HD, end * 2 * HD)
        there = pl.ds(pl.multiple_of(place_ref[i], FT), FT)
        return pltpu.make_async_copy(
            slot_refs[i].at[:, lanes], kv_ref.at[there, lanes], slot_sems.at[cut, i]
        )

    def query_copy(cut):
        begin, end = cuts[cut]
        lanes = slice(begin * wide, end * wide)
        return pltpu.make_async_copy(
            q_ref.at[:, lanes], held_q_ref.at[:, lanes], query_sems.at[cut]
        )

    def wanted(i):
        block = place_ref[i] // rows
        return (block >= first) & (block <= last)

    def all_slots(cut, act):
        for i in range(slots):
            pl.when(wanted(i))(functools.partial(act, i, cut))

    for cut in range(len(cuts)):
        query_copy(cut).start()
        all_slots(cut, lambda i, cut: slot_copy(i, cut).start())

    def mask(block):
        query_pos = first_pos + lax.broadcasted_iota(jnp.int32, (rows, FT), 0)
        low = first_key(query_pos)
        for at in range(0, rows, FT):
            key_pos = block * rows + at + lax.broadcasted_iota(jnp.int32, (rows, FT), 1)
            allowed = (key_pos <= query_pos) & (key_pos >= low)
            bias_ref[block, :, at : at + FT] = jnp.where(allowed, 0.0, MASKED)

    pl.loop(first, paired + 2 * masked_pairs)(mask)
    mask(last)

    def result_copy(h):
        return pltpu.make_async_copy(
            result_ref.at[h], out_ref.at[:, h * wide : (h + 1) * wide], out_sems.at[h]
        )

    for cut in range(len(cuts)):
        query_copy(cut).wait()
        all_slots(cut, lambda i, cut: slot_copy(i, cut).wait())
    for h in range(heads):
        for g in range(GROUP):
            at = h * wide + g * HD
            query_ref[h, g * rows : (g + 1) * rows] = held_q_ref[:, at : at + HD]

    def score(block, count, masked, initial):
        here = pl.ds(pl.multiple_of(block * rows, rows), count * rows)
        for h in range(heads):
            keys = kv_ref[here, 2 * h * HD : (2 * h + 1) * HD]
            scores = contract_last(query_ref[h], keys) * scale
            parts = []
            for i in range(count):
                part = scores[:, i * rows : (i + 1) * rows]
                if masked:
                    part = part.reshape(GROUP, rows, rows) + bias_ref[block + i][None]
                    part = part.reshape(GROUP * rows, rows)
                score_ref[h, block + i] = part
                parts += [part[:, at : at + FT] for at in range(0, rows, FT)]
            if not initial:
                parts.append(max_ref[h])
            max_ref[h] = functools.reduce(jnp.maximum, parts)

    def mix(block, count, initial):
        here = pl.ds(pl.multiple_of(block * rows, rows), count * rows)
        for h in range(heads):
            values = kv_ref[here, (2 * h + 1) * HD : (2 * h + 2) * HD]
            values = jnp.concatenate([values, jnp.ones_like(values)], axis=1)
            weights = [
                jnp.exp(score_ref[h, block + i, :, at : at + FT] - max_ref[h]).astype(jnp.bfloat16)
                for i in range(count)
                for at in range(0, rows, FT)
            ]
            weights = jnp.concatenate(weights, axis=1)
            mixed = jnp.dot(weights, values, preferred_element_type=jnp.float32)
            acc_ref[h] = mixed if initial else acc_ref[h] + mixed

    score(last, 1, masked=True, initial=True)

    @pl.when(paired > first)
    def _():
        score(first, 1, masked=True, initial=False)

    @pl.loop(0, masked_pairs)
    def _(pair):
        score(paired + 2 * pair, 2, masked=True, initial=False)

    @pl.loop(masked_pairs, pairs)
    def _(pair):
        score(paired + 2 * pair, 2, masked=False, initial=False)

    for h in range(heads):
        row_max = jnp.max(max_ref[h], axis=1, keepdims=True)
        max_ref[h] = jnp.broadcast_to(row_max, (GROUP * rows, FT))

    mix(last, 1, initial=True)

    @pl.when(paired > first)
    def _():
        mix(first, 1, initial=False)

    @pl.loop(0, pairs)
    def _(pair):
        mix(paired + 2 * pair, 2, initial=False)

    for h in range(heads):
        mixed = acc_ref[h, :, :HD] / acc_ref[h, :, HD:]
        for g in range(GROUP):
            result_ref[h, :, g * HD : (g + 1) * HD] = mixed[g * rows : (g + 1) * rows].astype(
                result_ref.dtype
            )
        result_copy(h).start()
    for h in range(heads):
        result_copy(h).wait()


def attend(queries, slots, place):
    rows = queries.shape[0]
    columns = slots[0].shape[1]
    heads = columns // (2 * HD)
    blocks = len(slots) * FT // rows
    wide = GROUP * HD
    tall = GROUP * rows
    anywhere = pl.BlockSpec(memory_space=pl.ANY)
    scalars = pl.BlockSpec(memory_space=pltpu.SMEM)
    cells = heads * tall * blocks * rows
    return pl.pallas_call(
        functools.partial(attend_kernel, slots=len(slots), heads=heads),
        in_specs=[scalars] + [anywhere] * (1 + len(slots)),
        out_specs=anywhere,
        out_shape=jax.ShapeDtypeStruct(queries.shape, jnp.bfloat16),
        scratch_shapes=[
            pltpu.VMEM((len(slots) * FT, columns), jnp.bfloat16),
            pltpu.VMEM(queries.shape, jnp.bfloat16),
            pltpu.VMEM((heads, tall, HD), jnp.bfloat16),
            pltpu.VMEM((blocks, rows, rows), jnp.float32),
            pltpu.VMEM((heads, blocks, tall, rows), jnp.float32),
            pltpu.VMEM((heads, tall, FT), jnp.float32),
            pltpu.VMEM((heads, tall, 2 * HD), jnp.float32),
            pltpu.VMEM((heads, rows, wide), jnp.bfloat16),
            pltpu.SemaphoreType.DMA((2, len(slots))),
            pltpu.SemaphoreType.DMA((2,)),
            pltpu.SemaphoreType.DMA((heads,)),
        ],
        compiler_params=pltpu.CompilerParams(vmem_limit_bytes=LANGUAGE_VMEM),
        cost_estimate=pl.CostEstimate(
            flops=6 * cells * HD,
            bytes_accessed=2 * len(slots) * FT * columns + 4 * rows * heads * wide,
            transcendentals=cells,
        ),
    )(place, queries, *slots)


def shards(
    vis_qkv,
    vis_resid,
    vis_out_w,
    merge_gain,
    merge_bias,
    vis_kv_w,
    frame_host,
    vis_pos,
    doc_ids,
    text_kv,
    queries,
):
    device = lax.axis_index("ctx")
    tp_index = lax.axis_index("tp")
    tp_size = lax.axis_size("tp")
    per_device = queries.shape[0]
    patches = vis_qkv.shape[0]
    width = vis_qkv.shape[2]
    local_kv = vis_kv_w.shape[2] // tp_size
    positions = doc_ids.shape[0]
    frames = vis_pos.shape[0]

    peers = lax.axis_size("ctx")
    rows = peers // 2
    first_pos = device * per_device

    fields = jnp.transpose(vis_qkv, (1, 0, 2))
    part_count = 2
    part_rows = patches // part_count
    text_high = text_kv[FT:]
    handed = shifted(text_high, "ctx", peers // 2)
    (first_context,) = vit_attention(fields, text_high, 0, tp_index)
    second_context, low_rows, high_rows = vit_attention(
        fields, first_context, 1, tp_index, (first_context, vis_out_w, vis_resid)
    )
    contexts = [first_context, second_context]
    arrived = [
        [shifted(context, "tp", distance) for distance in range(1, tp_size)]
        for context in contexts
    ]

    def out_rows(distance):
        source = lax.rem(tp_after + tp_size - distance, tp_size)
        return lax.dynamic_slice_in_dim(vis_out_w, source * width, width, axis=0)

    vis_pos, text_kv, _ = lax.optimization_barrier((vis_pos, text_kv, second_context))
    first_frame = jnp.any(vis_pos == first_pos)
    second_frame = jnp.any(vis_pos == first_pos + FT)
    text_block = lax.dynamic_slice_in_dim(text_kv, jnp.where(first_frame, FT, 0), FT)
    handed, text_block, _ = lax.optimization_barrier((handed, text_block, low_rows))
    text_block = jnp.where(first_frame & second_frame, handed, text_block)
    hidden_parts = [low_rows, high_rows]
    text = Ring(text_block, rows)
    tp_after = tp_index
    for part in range(part_count):
        for distance in range(1, tp_size):
            hidden_parts[part] = hidden_parts[part] + jnp.dot(
                arrived[part][distance - 1], out_rows(distance), preferred_element_type=jnp.float32
            )
        if part == 0:
            tp_after, _ = lax.optimization_barrier((tp_index, hidden_parts[0]))
    hidden = jnp.concatenate(hidden_parts, axis=0)
    sums = jnp.stack([jnp.sum(hidden, axis=1), jnp.sum(hidden * hidden, axis=1)])
    others = [shifted(sums, "tp", distance) for distance in range(1, tp_size)]
    sums = text.advance(sums)
    row_sum, row_squares = functools.reduce(jnp.add, others, sums)
    mean_value = row_sum / VD
    variance = row_squares / VD - mean_value * mean_value
    normed = (hidden - mean_value[:, None]) * lax.rsqrt(variance + 1e-06)[
        :, None
    ] * merge_gain + merge_bias
    normed = normed.astype(jnp.bfloat16)

    received = []
    for distance in range(1, tp_size):
        block = lax.rem(tp_index + distance, tp_size)
        part = merged_columns(normed, vis_kv_w, block, local_kv, jnp.bfloat16)
        received.append(shifted(part, "tp", distance))
    own = merged_columns(normed, vis_kv_w, tp_index, local_kv, jnp.float32)
    own = text.advance(own)
    for part in received:
        own = own + part.astype(jnp.float32)
    own = own.astype(jnp.bfloat16)
    vision = Ring(own, rows)
    vis_pos, own = lax.optimization_barrier((vis_pos, own))
    place = tables(device, vis_pos, frame_host, doc_ids, peers, per_device)
    def laid(blocks, beside):
        come, _ = lax.optimization_barrier((blocks, beside))
        return [block.reshape(FT, local_kv) for block in come]

    texts, fresh = [], []
    for hop in range(1, rows):
        if hop == 1:
            vision.moving, place = text.advance((vision.moving, place))
        fresh = vision.advance(fresh, lag=1)
        texts += fresh
        ready = 2 * rows - 1 if hop > 1 else min(4, 2 * rows - 1)
        fresh = laid(text.blocks[len(texts) : ready], vision.blocks[-2])
    texts += fresh
    texts += laid(text.all()[len(texts) :], vision.blocks[-2])
    return attend(queries, texts + vision.all(), place)


def solution(mesh):
    return jax.shard_map(
        shards,
        mesh=mesh,
        in_specs=(
            P(("dp", "ctx"), None, "tp"),
            P(("dp", "ctx"), "tp"),
            P(None, "tp"),
            P("tp"),
            P("tp"),
            P(None, "tp", None),
            P("dp"),
            P("dp"),
            P("dp"),
            P(("dp", "ctx"), "tp", None, None),
            P(("dp", "ctx"), "tp"),
        ),
        out_specs=P(("dp", "ctx"), "tp"),
        check_vma=False,
    )
```
